32 devices in a mesh: seq: 8 (over z, y), ch: 4 (over x, core).
Axes of the slice: x: 2, y: 2, z: 4, core: 2. Of those that a mesh axis runs over, the one named last changes fastest.
Arguments:
- streams: bfloat16 [2048, 3, 4096], P(('seq', 'ch')), may hold values from -6 to 6
- filter_taps: float32 [4096, 2048], P('ch', 'seq')
- skip_gain: float32 [4096], P('ch'), may hold values from -1 to 1
Outputs:
- mixed_out: bfloat16 [4096, 2048], P('ch', 'seq')
The draws below stay inside these ranges and needn't reach their ends.
All inputs are finite; a program needn't handle non-finite values.
Results may differ from the reference program's by a relative error of at most 0.001.
Values may be sent and summed in bfloat16 or wider, within the bound.
No kernel may reach another device: no remote copies, remote signals or barrier semaphores. Data moves between devices by JAX's collectives and lax.ppermute only.
A program may use at most 128 MiB of HBM per device.

```python
import math
import jax
import jax.numpy as jnp
from jax import lax

C = 4096
SEQUENCE_EXTENT = 2048
SPAN = 4096


def geometric_total(rate):
    return jnp.expm1(-rate * SEQUENCE_EXTENT) / jnp.expm1(-rate)


def draw_filter_taps(key, part):
    key = jax.random.fold_in(key, 7)
    gradual_decay_starter, decay_speed_starter, quick_decay_starter, jitter_random_starter, spike_random_starter, omission_random_starter, floor_random_starter = jax.random.split(key, 7)
    slow_share = 0.5
    slow_pick = jax.random.uniform(gradual_decay_starter, (C, 1)) < slow_share
    slow_rate = jnp.exp(jax.random.uniform(decay_speed_starter, (C, 1), minval=math.log(0.05), maxval=0.0)) * (math.log(10.0) / SEQUENCE_EXTENT)
    fast_rate = jax.random.uniform(quick_decay_starter, (C, 1), minval=1.0 / 50.0, maxval=1.0 / 30.0)
    decay_rate = jnp.where(slow_pick, slow_rate, fast_rate)
    floor_drawn = jax.random.uniform(floor_random_starter, (C, 1), minval=0.04, maxval=0.08)
    floor_weight = jnp.where(slow_pick, 0.0, floor_drawn)
    lags = jnp.arange(SEQUENCE_EXTENT, dtype=jnp.float32)[None, :]
    kernel_decay_profile = jnp.exp(-decay_rate * lags) + floor_weight * jnp.exp(-slow_rate * lags)
    spike_placement_index = jax.random.randint(spike_random_starter, (3,), 1, SEQUENCE_EXTENT)
    spike_retained_mask = jax.random.uniform(omission_random_starter, (3,), minval=0.5, maxval=0.8)
    for chosen_branch_mask in range(3):
        kernel_decay_profile = kernel_decay_profile * jnp.where(jnp.arange(SEQUENCE_EXTENT)[None, :] >= spike_placement_index[chosen_branch_mask], spike_retained_mask[chosen_branch_mask], 1.0)
    scale_sum = geometric_total(2.0 * decay_rate) + 2.0 * floor_weight * geometric_total(decay_rate + slow_rate) + floor_weight * floor_weight * geometric_total(2.0 * slow_rate)
    noise = jax.random.truncated_normal(jitter_random_starter, -6.0, 6.0, (C, SEQUENCE_EXTENT))
    return (noise * kernel_decay_profile / jnp.sqrt(scale_sum)).astype(jnp.float32)


def block_levels(stream_key, extent, pieces, least, high):
    factor_of = 1.0
    for axis_at, blocks in pieces:
        steps = jax.random.uniform(jax.random.fold_in(jax.random.fold_in(stream_key, 6), axis_at), (blocks,), jnp.float32, least / len(pieces), high / len(pieces))
        factor_of = factor_of * jnp.repeat(jnp.exp(steps), extent[axis_at] // blocks).reshape((-1,) + (1,) * (len(extent) - 1 - axis_at))
    return factor_of


def scatter_about(stream_key, extent, deviation, reach, cuts=(), kind=jnp.bfloat16):
    array = deviation * jax.random.normal(stream_key, extent, jnp.float32)
    if cuts:
        array = array * block_levels(stream_key, extent, cuts, -0.22, 0.18)
    return jnp.clip(array, -reach, reach).astype(kind)


def setup_inputs(seed: int = 0) -> dict:
    splits = jax.random.split(jax.random.key(seed), 4)
    return {
        "streams": scatter_about(splits[0], (SEQUENCE_EXTENT, 3, C), 1.0, 6.0, ((0, 32),)),
        "filter_taps": draw_filter_taps(jax.random.fold_in(splits[3], 71), 0),
        "skip_gain": jnp.clip(jax.random.uniform(splits[2], (C,), jnp.float32, -1.0, 1.0) * block_levels(splits[2], (C,), ((0, 4),), -0.4, 0.0), -1.0, 1.0),
    }


def reference(streams, filter_taps, skip_gain):
    group = 256
    count = C // group

    def one_group(index):
        start = (index * group).astype(jnp.int32)
        part = lax.dynamic_slice_in_dim(streams, start, group, 2)
        taps = lax.dynamic_slice_in_dim(filter_taps, start, group, 0)
        gains = lax.dynamic_slice_in_dim(skip_gain, start, group, 0)
        queries = jnp.transpose(part[:, 0, :]).astype(jnp.float32)
        gated_values = jnp.transpose(part[:, 1, :]).astype(jnp.float32) * jnp.transpose(part[:, 2, :]).astype(jnp.float32)
        spectrum = jnp.fft.rfft(gated_values, n=SPAN, axis=1) * jnp.fft.rfft(taps, n=SPAN, axis=1)
        convolved = jnp.fft.irfft(spectrum, n=SPAN, axis=1)[:, :SEQUENCE_EXTENT]
        mixed_sum = convolved + gains[:, None] * gated_values
        return (queries * mixed_sum).astype(jnp.bfloat16)

    result = lax.map(one_group, jnp.arange(count, dtype=jnp.int32))
    return result.reshape(C, SEQUENCE_EXTENT)
```

```python
import functools
import math

import jax
import jax.numpy as jnp
import numpy as np
from jax import lax
from jax.experimental import pallas as pl
from jax.experimental.pallas import tpu as pltpu
from jax.sharding import PartitionSpec as P

TOP = 32000.0
TOP_LEVEL = 32255.0
LOW_POWER = 125.0
EXPONENT_BITS = 8
EXPONENT_BIAS = 127.0
LANES = 128
ROW = 256
CHUNK = 16
HALF = 64
VMEM_BYTES = 24 * 1024 * 1024
SMALL_BYTES = 12 * 1024 * 1024


def split_first(values, axis):
    count = min(values.shape[axis], LANES if axis == values.ndim - 1 else EXPONENT_BITS)
    first = lax.slice_in_dim(values, 0, count, axis=axis)
    if count == values.shape[axis]:
        return first, None
    return first, lax.slice_in_dim(values, count, values.shape[axis], axis=axis)


def encode(values, axis):
    size = jnp.abs(values)
    peak = jnp.max(size, axis=axis, keepdims=True)
    power = jnp.floor(jnp.log(jnp.maximum(peak, 1e-30)) * (1.0 / math.log(2.0))) + 1.0
    power = jnp.clip(power, -100.0, 126.0)
    share = size * jnp.exp2(-power)
    level = jnp.minimum(
        share * (2.0 * TOP), jnp.minimum(share * TOP + TOP / 4, share * (TOP / 2) + TOP / 2)
    )
    first, rest = split_first(level, axis)
    place = lax.broadcasted_iota(jnp.int32, first.shape, axis).astype(jnp.float32)
    halves = jnp.floor((power + (EXPONENT_BIAS + 0.25)) * jnp.exp2(-place))
    bit = halves - 2.0 * jnp.floor(halves * 0.5)
    marked = 2.0 * jnp.floor((first - bit) * 0.5 + 0.5) + bit
    level = jnp.where(place < EXPONENT_BITS, marked, jnp.floor(first + 0.5))
    if rest is not None:
        level = jnp.concatenate([level, jnp.floor(rest + 0.5)], axis=axis)
    level = jnp.minimum(level, TOP_LEVEL) * (1.0 / 128.0)
    octave = jnp.floor(level)
    code = jnp.exp2(octave - LOW_POWER) * (level - octave + 1.0)
    return jnp.where(values < 0.0, -code, code).astype(jnp.bfloat16)


def decode(code, axis):
    code = code.astype(jnp.float32)
    size = jnp.abs(code)
    octave = jnp.floor(jnp.log(size) * (1.0 / math.log(2.0)) + 0.002)
    level = (octave + size * jnp.exp2(-octave) + (LOW_POWER - 1.0)) * 128.0
    first, _ = split_first(level, axis)
    first = jnp.floor(first + 0.5)
    place = lax.broadcasted_iota(jnp.int32, first.shape, axis).astype(jnp.float32)
    bit = first - 2.0 * jnp.floor(first * 0.5)
    held = jnp.where(place < EXPONENT_BITS, bit * jnp.exp2(place), 0.0)
    scale = jnp.exp2(jnp.sum(held, axis=axis, keepdims=True) - EXPONENT_BIAS)
    share = jnp.maximum(
        level * (0.5 / TOP),
        jnp.maximum(level * (1.0 / TOP) - 0.25, level * (2.0 / TOP) - 1.0),
    )
    return jnp.where(code < 0.0, -share, share) * scale


def tables(blocks):
    n2 = np.arange(ROW)
    k1 = np.arange(blocks)
    main = 2.0 * np.pi * np.outer(n2, n2) / ROW
    wave = np.concatenate([np.cos(main), np.sin(main)], axis=1).astype(np.float32)
    high = wave.astype(jnp.bfloat16)
    low = (wave - high.astype(np.float32)).astype(jnp.bfloat16)
    twist = 2.0 * np.pi * np.outer(k1 + 0.25, n2) / (blocks * ROW)
    mix = 2.0 * np.pi * np.outer(k1 + 0.25, np.arange(blocks)) / blocks
    twist = np.stack([np.cos(twist), np.sin(twist)], axis=1).astype(np.float32)
    mix = np.stack([np.cos(mix), np.sin(mix)], axis=0).astype(np.float32)
    return high, low, twist, mix


def put_split(ref, at, values):
    high = values.astype(jnp.bfloat16)
    ref[pl.ds(at, values.shape[0]), 0:ROW] = high
    ref[pl.ds(at, values.shape[0]), ROW : 2 * ROW] = high
    ref[pl.ds(at, values.shape[0]), 2 * ROW : 3 * ROW] = (
        values - high.astype(jnp.float32)
    ).astype(jnp.bfloat16)


def weighted(pairs):
    total = None
    for value, weight in pairs:
        term = value * float(weight)
        total = term if total is None else total + term
    return total


def mix_forward(blocks_in, twist_ref, mix, at, ref):
    half = len(blocks_in) // 2
    for k1 in range(half):
        sums = []
        for start in (0, 1):
            taken = [(blocks_in[n1], mix[:, k1, n1]) for n1 in range(start, 2 * half, 2)]
            sums.append(weighted([(value, weight[0]) for value, weight in taken]))
            sums.append(weighted([(value, -weight[1]) for value, weight in taken]))
        even_re, even_im, odd_re, odd_im = sums
        for k, re, im in (
            (k1, even_re + odd_re, even_im + odd_im),
            (k1 + half, even_re - odd_re, even_im - odd_im),
        ):
            cos_twist, sin_twist = twist_ref[k, 0:1, :], twist_ref[k, 1:2, :]
            put_split(ref, 2 * k * HALF + at, re * cos_twist + im * sin_twist)
            put_split(ref, (2 * k + 1) * HALF + at, im * cos_twist - re * sin_twist)


def mix_back(spectra, twist_ref, mix):
    half = len(spectra) // 2
    turned = []
    for k, (re, im) in enumerate(spectra):
        cos_twist, sin_twist = twist_ref[k, 0:1, :], twist_ref[k, 1:2, :]
        turned.append((re * cos_twist - im * sin_twist, im * cos_twist + re * sin_twist))
    totals = [None] * (2 * half)
    for k1 in range(half):
        (re, im), (other_re, other_im) = turned[k1], turned[k1 + half]
        both = ((re + other_re, im + other_im), (re - other_re, im - other_im))
        for n1 in range(2 * half):
            re, im = both[n1 % 2]
            term = weighted([(re, mix[0, k1, n1]), (im, -mix[1, k1, n1])])
            totals[n1] = term if totals[n1] is None else totals[n1] + term
    return totals


def spectrum_rows(waves_ref, k, at):
    re = waves_ref[pl.ds(2 * k * HALF + at, CHUNK), :]
    im = waves_ref[pl.ds((2 * k + 1) * HALF + at, CHUNK), :]
    return re, im


def send_kernel(streams_ref, gated_ref, *query_refs):
    me, step = lax.axis_index("ch"), pl.program_id(0)
    for turn, query_ref in enumerate(query_refs):

        @pl.when(step == me ^ turn)
        def _():
            query_ref[...] = streams_ref[0]

    for block in range(gated_ref.shape[0]):
        lanes = slice(block * LANES, (block + 1) * LANES)
        keys = streams_ref[1, :, lanes].astype(jnp.float32)
        values = streams_ref[2, :, lanes].astype(jnp.float32)
        gated_ref[block, 0] = encode(keys * values, 0)


def taps_kernel(taps_ref, skip_ref, *code_refs):
    me = lax.axis_index("seq")
    first = (me == 0).astype(jnp.float32)
    row = lax.broadcasted_iota(jnp.int32, (LANES, LANES), 0)
    lane = lax.broadcasted_iota(jnp.int32, (LANES, LANES), 1)
    for turn, code_ref in enumerate(code_refs):
        block = me ^ turn
        gains = jnp.broadcast_to(skip_ref[pl.ds(block, 1), :], (LANES, LANES))
        gain = jnp.sum(jnp.where(row == lane, gains, 0.0), axis=1, keepdims=True) * first
        start = taps_ref[block, :, :LANES] + jnp.where(lane == 0, gain, 0.0)
        taps = jnp.concatenate([start, taps_ref[block, :, LANES:]], axis=1)
        code_ref[...] = encode(taps, 1)


def conv_kernel(mix, gated_ref, *refs):
    blocks = len(mix[0])
    wave_ref, twist_ref, out_ref, u, codes, *scratch = refs[blocks:]
    rows, u_waves, h_waves = scratch[0:2], scratch[2:4], scratch[4:6]
    me = lax.axis_index("seq")
    parts = ROW // gated_ref.shape[1]
    for turn, code_ref in enumerate(refs[:blocks]):
        codes[me ^ turn] = code_ref[...]

    def unpack(block):
        pieces = [decode(gated_ref[block * parts + part], 0) for part in range(parts)]
        u[block] = jnp.transpose(jnp.concatenate(pieces, axis=0))

    def forward_taps(half, at):
        start = pl.ds(half * HALF + at, CHUNK)
        taken = [decode(codes[n1, start, :], 1) for n1 in range(blocks)]
        mix_forward(taken, twist_ref, mix, at, rows[half])

    def forward_gated(half, at):
        start = pl.ds(half * HALF + at, CHUNK)
        mix_forward([u[n1, start, :] for n1 in range(blocks)], twist_ref, mix, at, rows[half])

    def product(half, at):
        for k in range(blocks):
            re, im = spectrum_rows(u_waves[half], k, at)
            re, im = re[:, :ROW] + im[:, ROW:], im[:, :ROW] - re[:, ROW:]
            taps_re, taps_im = spectrum_rows(h_waves[half], k, at)
            taps_re, taps_im = (
                taps_re[:, :ROW] + taps_im[:, ROW:],
                taps_im[:, :ROW] - taps_re[:, ROW:],
            )
            put_split(rows[half], 2 * k * HALF + at, re * taps_re - im * taps_im)
            put_split(rows[half], (2 * k + 1) * HALF + at, re * taps_im + im * taps_re)

    def back(half, at):
        spectra = []
        for k in range(blocks):
            re, im = spectrum_rows(u_waves[half], k, at)
            spectra.append((re[:, :ROW] - im[:, ROW:], im[:, :ROW] + re[:, ROW:]))
        start = pl.ds(half * HALF + at, CHUNK)
        for n1, total in enumerate(mix_back(spectra, twist_ref, mix)):
            out_ref[n1, start, :] = encode(total * (1.0 / (blocks * ROW)), 1)

    def stage(source, target, work, half, more=None):
        steps = 2
        count = rows[0].shape[0] // steps
        chunks = HALF // CHUNK // steps

        def step(index, _):
            if source is not None:
                at = pl.ds(pl.multiple_of(index * count, count), count)
                target[at, :] = jnp.dot(
                    source[at, :], wave_ref[...], preferred_element_type=jnp.float32
                )
            for chunk in range(chunks):
                work(half, pl.multiple_of((index * chunks + chunk) * CHUNK, CHUNK))
            for block in range(blocks // steps if more else 0):
                more(index * (blocks // steps) + block)
            return 0

        lax.fori_loop(0, steps, step, 0)

    stage(None, None, forward_taps, 0)
    stage(rows[0], h_waves[0], forward_taps, 1, unpack)
    stage(rows[1], h_waves[1], forward_gated, 0)
    stage(rows[0], u_waves[0], forward_gated, 1)
    stage(rows[1], u_waves[1], product, 0)
    stage(rows[0], u_waves[0], product, 1)
    stage(rows[1], u_waves[1], back, 0)
    stage(None, None, back, 1)


def turn_kernel(*refs):
    query_refs, out_ref, whole = refs[:-2], refs[-2], refs[-1]
    me = lax.axis_index("ch")
    held = query_refs[0].shape[0]
    for turn, query_ref in enumerate(query_refs):
        at = pl.multiple_of((me ^ turn) * held, held)
        whole[pl.ds(at, held), :] = query_ref[...].astype(jnp.float32)
    out_ref[...] = jnp.transpose(whole[...]).astype(jnp.bfloat16)


def mix_kernel(query_ref, conv_ref, out_ref):
    for block in range(conv_ref.shape[0]):
        at = slice(block * LANES, (block + 1) * LANES)
        queries = query_ref[at, :].astype(jnp.float32)
        out_ref[at, :] = (queries * decode(conv_ref[block], 1)).astype(jnp.bfloat16)


def plain_conv(gated, taps):
    blocks = gated.shape[0]
    high, low, twist, mix = tables(blocks)
    wave = jnp.asarray(high, jnp.float32) + jnp.asarray(low, jnp.float32)
    cos_twist, sin_twist = twist[:, 0][:, None, :], twist[:, 1][:, None, :]
    dot = functools.partial(jnp.einsum, precision=lax.Precision.HIGHEST)

    def forward(values):
        re = dot("ncm,kn->kcm", values, mix[0])
        im = -dot("ncm,kn->kcm", values, mix[1])
        re, im = re * cos_twist + im * sin_twist, im * cos_twist - re * sin_twist
        re, im = dot("kcm,mq->kcq", re, wave), dot("kcm,mq->kcq", im, wave)
        return re[..., :ROW] + im[..., ROW:], im[..., :ROW] - re[..., ROW:]

    u_re, u_im = forward(gated)
    h_re, h_im = forward(taps)
    re = dot("kcm,mq->kcq", u_re * h_re - u_im * h_im, wave)
    im = dot("kcm,mq->kcq", u_re * h_im + u_im * h_re, wave)
    re, im = re[..., :ROW] - im[..., ROW:], im[..., :ROW] + re[..., ROW:]
    re, im = re * cos_twist - im * sin_twist, im * cos_twist + re * sin_twist
    total = dot("kcm,kn->ncm", re, mix[0]) - dot("kcm,kn->ncm", im, mix[1])
    return total * (1.0 / (blocks * ROW))


def scatter(blocks, axis):
    count = len(blocks)
    return [
        lax.ppermute(block, axis, [(i, i ^ turn) for i in range(count)]) if turn else block
        for turn, block in enumerate(blocks)
    ]


def body(streams, filter_taps, skip_gain):
    groups, parts = lax.axis_size("seq"), lax.axis_size("ch")
    held, _, channels = streams.shape
    wide = channels // parts
    own = wide // groups
    blocks = filter_taps.shape[1] * groups // ROW
    streams = jnp.transpose(streams, (1, 0, 2))
    fits = own == LANES and filter_taps.shape[1] == ROW and ROW % held == 0 and groups % 4 == 0
    fits = fits and groups & (groups - 1) == 0 and parts & (parts - 1) == 0
    small = pltpu.CompilerParams(vmem_limit_bytes=SMALL_BYTES)
    if fits:
        gated, *queries = pl.pallas_call(
            send_kernel,
            grid=(parts,),
            in_specs=[pl.BlockSpec((3, held, wide), lambda g: (0, 0, g))],
            out_specs=[
                pl.BlockSpec((groups, 1, held, own), lambda g: (0, g, 0, 0)),
            ]
            + [pl.BlockSpec((held, wide), lambda g: (0, 0))] * parts,
            out_shape=[
                jax.ShapeDtypeStruct((groups, parts, held, own), jnp.bfloat16),
            ]
            + [jax.ShapeDtypeStruct((held, wide), jnp.bfloat16)] * parts,
            cost_estimate=cost(2**25, 2**23),
            compiler_params=small,
            name="encode_gated",
        )(streams)
        taps = pl.pallas_call(
            taps_kernel,
            out_shape=[jax.ShapeDtypeStruct((own, ROW), jnp.bfloat16)] * groups,
            compiler_params=small,
            cost_estimate=cost(2**25, 2**23),
            name="encode_taps",
        )(filter_taps.reshape(groups, own, ROW), skip_gain.reshape(groups, own))
    else:
        gated = encode(streams[1].astype(jnp.float32) * streams[2].astype(jnp.float32), 0)
        gated = jnp.transpose(gated.reshape(held, parts, groups, own), (2, 1, 0, 3))
        queries = jnp.transpose(streams[0].reshape(held, parts, wide), (1, 0, 2))
        first = lax.axis_index("seq") == 0
        taps = filter_taps.at[:, 0].add(jnp.where(first, skip_gain, 0.0))
        taps = encode(taps, 1).reshape(groups, own, -1)
    exchange = functools.partial(lax.all_to_all, split_axis=0, concat_axis=0, tiled=True)
    gated = gated.reshape(groups * parts, held, own)
    if fits:
        taps = scatter(taps, "seq")
        gated = exchange(gated, ("seq", "ch"))
        queries = scatter(queries, "ch")
    else:
        taps = exchange(taps, "seq")
        gated = exchange(gated, ("seq", "ch"))
        queries = exchange(queries, "ch").reshape(parts * held, wide)
    if fits:
        high, low, twist, mix = tables(blocks)
        wave = np.concatenate([high, low, high], axis=0)
        convolved = pl.pallas_call(
            functools.partial(conv_kernel, mix),
            out_shape=jax.ShapeDtypeStruct((blocks, own, ROW), jnp.bfloat16),
            scratch_shapes=[
                pltpu.VMEM((blocks, own, ROW), jnp.float32),
                pltpu.VMEM((blocks, own, ROW), jnp.bfloat16),
            ]
            + [pltpu.VMEM((blocks * 2 * HALF, 3 * ROW), jnp.bfloat16)] * 2
            + [pltpu.VMEM((blocks * 2 * HALF, 2 * ROW), jnp.float32)] * 4,
            compiler_params=pltpu.CompilerParams(vmem_limit_bytes=VMEM_BYTES),
            cost_estimate=cost(2**32, 2**24),
            name="convolve",
        )(gated, *taps, wave, twist)
    else:
        gated = decode(gated, 1).reshape(blocks, ROW, own)
        taps = jnp.transpose(decode(taps, 2), (1, 0, 2)).reshape(own, blocks, ROW)
        convolved = plain_conv(jnp.transpose(gated, (0, 2, 1)), jnp.transpose(taps, (1, 0, 2)))
        convolved = jnp.transpose(convolved, (1, 0, 2)).reshape(own, groups, -1)
        convolved = encode(jnp.transpose(convolved, (1, 0, 2)), 2)
    convolved = exchange(convolved, "seq")
    if fits:
        queries = pl.pallas_call(
            turn_kernel,
            out_shape=jax.ShapeDtypeStruct((wide, ROW), jnp.bfloat16),
            scratch_shapes=[pltpu.VMEM((ROW, wide), jnp.float32)],
            compiler_params=small,
            cost_estimate=cost(2**20, 2**21),
            name="turn_queries",
        )(*queries)
        return pl.pallas_call(
            mix_kernel,
            grid=(4,),
            in_specs=[
                pl.BlockSpec((wide // 4, ROW), lambda i: (i, 0)),
                pl.BlockSpec((groups // 4, own, ROW), lambda i: (i, 0, 0)),
            ],
            out_specs=pl.BlockSpec((wide // 4, ROW), lambda i: (i, 0)),
            out_shape=jax.ShapeDtypeStruct((wide, ROW), jnp.bfloat16),
            compiler_params=small,
            name="mix_out",
        )(queries, convolved)
    queries = jnp.transpose(queries.astype(jnp.float32))
    return (queries * decode(convolved, 2).reshape(wide, -1)).astype(jnp.bfloat16)


def cost(flops, moved):
    return pl.CostEstimate(flops=int(flops), bytes_accessed=int(moved), transcendentals=0)


def solution(mesh):
    placed = (P(("seq", "ch"), None, None), P("ch", "seq"), P("ch"))
    return jax.shard_map(
        body, mesh=mesh, in_specs=placed, out_specs=P("ch", "seq"), check_vma=False
    )
```

```python
import functools
import math

import jax
import jax.numpy as jnp
import numpy as np
from jax import lax
from jax.experimental import pallas as pl
from jax.experimental.pallas import tpu as pltpu
from jax.sharding import PartitionSpec as P

TOP = 32000.0
TOP_LEVEL = 32255.0
LOW_POWER = 125.0
EXPONENT_BITS = 8
EXPONENT_BIAS = 127.0
LANES = 128
ROW = 256
CHUNK = 16
HALF = 64
VMEM_BYTES = 24 * 1024 * 1024
SMALL_BYTES = 12 * 1024 * 1024
ALL_BYTES = 60 * 1024 * 1024


def split_first(values, axis):
    count = min(values.shape[axis], LANES if axis == values.ndim - 1 else EXPONENT_BITS)
    first = lax.slice_in_dim(values, 0, count, axis=axis)
    if count == values.shape[axis]:
        return first, None
    return first, lax.slice_in_dim(values, count, values.shape[axis], axis=axis)


def encode(values, axis):
    size = jnp.abs(values)
    peak = jnp.max(size, axis=axis, keepdims=True)
    power = jnp.floor(jnp.log(jnp.maximum(peak, 1e-30)) * (1.0 / math.log(2.0))) + 1.0
    power = jnp.clip(power, -100.0, 126.0)
    share = size * jnp.exp2(-power)
    level = jnp.minimum(
        share * (2.0 * TOP), jnp.minimum(share * TOP + TOP / 4, share * (TOP / 2) + TOP / 2)
    )
    first, rest = split_first(level, axis)
    place = lax.broadcasted_iota(jnp.int32, first.shape, axis).astype(jnp.float32)
    halves = jnp.floor((power + (EXPONENT_BIAS + 0.25)) * jnp.exp2(-place))
    bit = halves - 2.0 * jnp.floor(halves * 0.5)
    marked = 2.0 * jnp.floor((first - bit) * 0.5 + 0.5) + bit
    level = jnp.where(place < EXPONENT_BITS, marked, jnp.floor(first + 0.5))
    if rest is not None:
        level = jnp.concatenate([level, jnp.floor(rest + 0.5)], axis=axis)
    level = jnp.minimum(level, TOP_LEVEL) * (1.0 / 128.0)
    octave = jnp.floor(level)
    code = jnp.exp2(octave - LOW_POWER) * (level - octave + 1.0)
    return jnp.where(values < 0.0, -code, code).astype(jnp.bfloat16)


def decode(code, axis):
    code = code.astype(jnp.float32)
    size = jnp.abs(code)
    octave = jnp.floor(jnp.log(size) * (1.0 / math.log(2.0)) + 0.002)
    level = (octave + size * jnp.exp2(-octave) + (LOW_POWER - 1.0)) * 128.0
    first, _ = split_first(level, axis)
    first = jnp.floor(first + 0.5)
    place = lax.broadcasted_iota(jnp.int32, first.shape, axis).astype(jnp.float32)
    bit = first - 2.0 * jnp.floor(first * 0.5)
    held = jnp.where(place < EXPONENT_BITS, bit * jnp.exp2(place), 0.0)
    scale = jnp.exp2(jnp.sum(held, axis=axis, keepdims=True) - EXPONENT_BIAS)
    share = jnp.maximum(
        level * (0.5 / TOP),
        jnp.maximum(level * (1.0 / TOP) - 0.25, level * (2.0 / TOP) - 1.0),
    )
    return jnp.where(code < 0.0, -share, share) * scale


def tables(blocks):
    n2 = np.arange(ROW)
    k1 = np.arange(blocks)
    main = 2.0 * np.pi * np.outer(n2, n2) / ROW
    wave = np.concatenate([np.cos(main), np.sin(main)], axis=1).astype(np.float32)
    high = wave.astype(jnp.bfloat16)
    low = (wave - high.astype(np.float32)).astype(jnp.bfloat16)
    twist = 2.0 * np.pi * np.outer(k1 + 0.25, n2) / (blocks * ROW)
    mix = 2.0 * np.pi * np.outer(k1 + 0.25, np.arange(blocks)) / blocks
    twist = np.stack([np.cos(twist), np.sin(twist)], axis=1).astype(np.float32)
    mix = np.stack([np.cos(mix), np.sin(mix)], axis=0).astype(np.float32)
    return high, low, twist, mix


def put_split(ref, at, values):
    high = values.astype(jnp.bfloat16)
    ref[pl.ds(at, values.shape[0]), 0:ROW] = high
    ref[pl.ds(at, values.shape[0]), ROW : 2 * ROW] = high
    ref[pl.ds(at, values.shape[0]), 2 * ROW : 3 * ROW] = (
        values - high.astype(jnp.float32)
    ).astype(jnp.bfloat16)


def weighted(pairs):
    total = None
    for value, weight in pairs:
        term = value * float(weight)
        total = term if total is None else total + term
    return total


def mix_forward(blocks_in, twist_ref, mix, at, ref):
    half = len(blocks_in) // 2
    for k1 in range(half):
        sums = []
        for start in (0, 1):
            taken = [(blocks_in[n1], mix[:, k1, n1]) for n1 in range(start, 2 * half, 2)]
            sums.append(weighted([(value, weight[0]) for value, weight in taken]))
            sums.append(weighted([(value, -weight[1]) for value, weight in taken]))
        even_re, even_im, odd_re, odd_im = sums
        for k, re, im in (
            (k1, even_re + odd_re, even_im + odd_im),
            (k1 + half, even_re - odd_re, even_im - odd_im),
        ):
            cos_twist, sin_twist = twist_ref[k, 0:1, :], twist_ref[k, 1:2, :]
            put_split(ref, 2 * k * HALF + at, re * cos_twist + im * sin_twist)
            put_split(ref, (2 * k + 1) * HALF + at, im * cos_twist - re * sin_twist)


def mix_back(spectra, twist_ref, mix):
    half = len(spectra) // 2
    turned = []
    for k, (re, im) in enumerate(spectra):
        cos_twist, sin_twist = twist_ref[k, 0:1, :], twist_ref[k, 1:2, :]
        turned.append((re * cos_twist - im * sin_twist, im * cos_twist + re * sin_twist))
    totals = [None] * (2 * half)
    for k1 in range(half):
        (re, im), (other_re, other_im) = turned[k1], turned[k1 + half]
        both = ((re + other_re, im + other_im), (re - other_re, im - other_im))
        for n1 in range(2 * half):
            re, im = both[n1 % 2]
            term = weighted([(re, mix[0, k1, n1]), (im, -mix[1, k1, n1])])
            totals[n1] = term if totals[n1] is None else totals[n1] + term
    return totals


def spectrum_rows(waves_ref, k, at):
    re = waves_ref[pl.ds(2 * k * HALF + at, CHUNK), :]
    im = waves_ref[pl.ds((2 * k + 1) * HALF + at, CHUNK), :]
    return re, im


def send_kernel(streams_ref, gated_ref, keys, values, codes, in_sems, out_sems):
    groups, parts = gated_ref.shape[:2]
    per = groups // 2
    width = per * LANES
    arrivals = []
    for chunk in range(2 * parts):
        lanes = pl.ds(chunk * width, width)
        for stream, buffer in ((1, keys), (2, values)):
            copy = pltpu.make_async_copy(
                streams_ref.at[stream, :, lanes], buffer.at[chunk], in_sems.at[stream - 1, chunk]
            )
            copy.start()
            arrivals.append(copy)
    copies = []
    for chunk in range(2 * parts):
        for copy in arrivals[2 * chunk : 2 * chunk + 2]:
            copy.wait()
        part, first = chunk // 2, chunk % 2 * per
        for block in range(per):
            lanes = slice(block * LANES, (block + 1) * LANES)
            left = keys[chunk, :, lanes].astype(jnp.float32)
            right = values[chunk, :, lanes].astype(jnp.float32)
            codes[first + block, part] = encode(left * right, 0)
        place = (pl.ds(first, per), part)
        copy = pltpu.make_async_copy(codes.at[place], gated_ref.at[place], out_sems.at[chunk])
        copy.start()
        copies.append(copy)
    for copy in copies:
        copy.wait()


def query_kernel(streams_ref, *refs):
    query_refs, sems = refs[:-1], refs[-1]
    me = lax.axis_index("ch")
    wide = query_refs[0].shape[1]
    copies = []
    for turn, query_ref in enumerate(query_refs):
        lanes = pl.ds(pl.multiple_of((me ^ turn) * wide, wide), wide)
        copy = pltpu.make_async_copy(streams_ref.at[0, :, lanes], query_ref, sems.at[turn])
        copy.start()
        copies.append(copy)
    for copy in copies:
        copy.wait()


def taps_kernel(taps_ref, skip_ref, *code_refs):
    me = lax.axis_index("seq")
    first = (me == 0).astype(jnp.float32)
    row = lax.broadcasted_iota(jnp.int32, (LANES, LANES), 0)
    lane = lax.broadcasted_iota(jnp.int32, (LANES, LANES), 1)
    for turn, code_ref in enumerate(code_refs):
        block = me ^ turn
        gains = jnp.broadcast_to(skip_ref[pl.ds(block, 1), :], (LANES, LANES))
        gain = jnp.sum(jnp.where(row == lane, gains, 0.0), axis=1, keepdims=True) * first
        start = taps_ref[block, :, :LANES] + jnp.where(lane == 0, gain, 0.0)
        taps = jnp.concatenate([start, taps_ref[block, :, LANES:]], axis=1)
        code_ref[...] = encode(taps, 1)


def combined(waves_ref, k, at):
    re, im = spectrum_rows(waves_ref, k, at)
    return re[:, :ROW] + im[:, ROW:], im[:, :ROW] - re[:, ROW:]


def stage(wave_ref, source, target, work, half):
    steps = 2
    chunks = HALF // CHUNK // steps

    def step(index, _):
        if source is not None:
            count = source.shape[0] // steps
            at = pl.ds(pl.multiple_of(index * count, count), count)
            target[at, :] = jnp.dot(
                source[at, :], wave_ref[...], preferred_element_type=jnp.float32
            )
        for chunk in range(chunks):
            work(half, pl.multiple_of((index * chunks + chunk) * CHUNK, CHUNK))
        return 0

    lax.fori_loop(0, steps, step, 0)


def gated_spectrum_kernel(mix, gated_ref, wave_ref, twist_ref, out_ref, u, *scratch):
    blocks = u.shape[0]
    rows, waves = scratch[0:2], scratch[2:4]
    parts = ROW // gated_ref.shape[1]

    def unpack(block, _):
        pieces = [decode(gated_ref[block * parts + part], 0) for part in range(parts)]
        u[block] = jnp.transpose(jnp.concatenate(pieces, axis=0))
        return 0

    def forward(half, at):
        start = pl.ds(half * HALF + at, CHUNK)
        mix_forward([u[n1, start, :] for n1 in range(blocks)], twist_ref, mix, at, rows[half])

    def finish(half, at):
        for k in range(blocks):
            re, im = combined(waves[half], k, at)
            out_ref[half, k, 0, pl.ds(at, CHUNK), :] = re
            out_ref[half, k, 1, pl.ds(at, CHUNK), :] = im

    lax.fori_loop(0, blocks, unpack, 0)
    stage(wave_ref, None, None, forward, 0)
    stage(wave_ref, rows[0], waves[0], forward, 1)
    stage(wave_ref, rows[1], waves[1], finish, 0)
    stage(wave_ref, None, None, finish, 1)


def conv_kernel(mix, gated_ref, *refs):
    blocks = len(mix[0])
    wave_ref, twist_ref = refs[blocks : blocks + 2]
    out_refs = refs[blocks + 2 : 2 * blocks + 2]
    codes, out, *scratch = refs[2 * blocks + 2 :]
    rows, waves = scratch[0:2], scratch[2:4]
    me = lax.axis_index("seq")
    for turn, code_ref in enumerate(refs[:blocks]):
        codes[me ^ turn] = code_ref[...]

    def forward(half, at):
        start = pl.ds(half * HALF + at, CHUNK)
        taken = [decode(codes[n1, start, :], 1) for n1 in range(blocks)]
        mix_forward(taken, twist_ref, mix, at, rows[half])

    def product(half, at):
        for k in range(blocks):
            re, im = combined(waves[half], k, at)
            gated_re = gated_ref[half, k, 0, pl.ds(at, CHUNK), :]
            gated_im = gated_ref[half, k, 1, pl.ds(at, CHUNK), :]
            put_split(rows[half], 2 * k * HALF + at, re * gated_re - im * gated_im)
            put_split(rows[half], (2 * k + 1) * HALF + at, re * gated_im + im * gated_re)

    def back(half, at):
        spectra = []
        for k in range(blocks):
            re, im = spectrum_rows(waves[half], k, at)
            spectra.append((re[:, :ROW] - im[:, ROW:], im[:, :ROW] + re[:, ROW:]))
        start = pl.ds(half * HALF + at, CHUNK)
        for n1, total in enumerate(mix_back(spectra, twist_ref, mix)):
            out[n1, start, :] = encode(total * (1.0 / (blocks * ROW)), 1)

    stage(wave_ref, None, None, forward, 0)
    stage(wave_ref, rows[0], waves[0], forward, 1)
    stage(wave_ref, rows[1], waves[1], product, 0)
    stage(wave_ref, rows[0], waves[0], product, 1)
    stage(wave_ref, rows[1], waves[1], back, 0)
    stage(wave_ref, None, None, back, 1)
    for turn, out_ref in enumerate(out_refs):
        out_ref[...] = out[me ^ turn]


def turn_kernel(*refs):
    query_refs, out_ref, whole = refs[:-2], refs[-2], refs[-1]
    me = lax.axis_index("ch")
    held = query_refs[0].shape[0]
    for turn, query_ref in enumerate(query_refs):
        at = pl.multiple_of((me ^ turn) * held, held)
        whole[pl.ds(at, held), :] = query_ref[...].astype(jnp.float32)
    out_ref[...] = jnp.transpose(whole[...]).astype(jnp.bfloat16)


def mix_kernel(query_ref, *refs):
    conv_refs, (out_ref, mixed, sems) = refs[:-3], refs[-3:]
    me = lax.axis_index("seq")
    copies = []
    for turn, conv_ref in enumerate(conv_refs):
        at = pl.ds(pl.multiple_of((me ^ turn) * LANES, LANES), LANES)
        queries = query_ref[at, :].astype(jnp.float32)
        mixed[at, :] = (queries * decode(conv_ref[...], 1)).astype(jnp.bfloat16)
        copy = pltpu.make_async_copy(mixed.at[at], out_ref.at[at], sems.at[turn])
        copy.start()
        copies.append(copy)
    for copy in copies:
        copy.wait()


def plain_conv(gated, taps):
    blocks = gated.shape[0]
    high, low, twist, mix = tables(blocks)
    wave = jnp.asarray(high, jnp.float32) + jnp.asarray(low, jnp.float32)
    cos_twist, sin_twist = twist[:, 0][:, None, :], twist[:, 1][:, None, :]
    dot = functools.partial(jnp.einsum, precision=lax.Precision.HIGHEST)

    def forward(values):
        re = dot("ncm,kn->kcm", values, mix[0])
        im = -dot("ncm,kn->kcm", values, mix[1])
        re, im = re * cos_twist + im * sin_twist, im * cos_twist - re * sin_twist
        re, im = dot("kcm,mq->kcq", re, wave), dot("kcm,mq->kcq", im, wave)
        return re[..., :ROW] + im[..., ROW:], im[..., :ROW] - re[..., ROW:]

    u_re, u_im = forward(gated)
    h_re, h_im = forward(taps)
    re = dot("kcm,mq->kcq", u_re * h_re - u_im * h_im, wave)
    im = dot("kcm,mq->kcq", u_re * h_im + u_im * h_re, wave)
    re, im = re[..., :ROW] - im[..., ROW:], im[..., :ROW] + re[..., ROW:]
    re, im = re * cos_twist - im * sin_twist, im * cos_twist + re * sin_twist
    total = dot("kcm,kn->ncm", re, mix[0]) - dot("kcm,kn->ncm", im, mix[1])
    return total * (1.0 / (blocks * ROW))


def scatter(blocks, axis):
    count = len(blocks)
    return [
        lax.ppermute(block, axis, [(i, i ^ turn) for i in range(count)]) if turn else block
        for turn, block in enumerate(blocks)
    ]


def body(streams, filter_taps, skip_gain):
    groups, parts = lax.axis_size("seq"), lax.axis_size("ch")
    held, _, channels = streams.shape
    wide = channels // parts
    own = wide // groups
    blocks = filter_taps.shape[1] * groups // ROW
    streams = jnp.transpose(streams, (1, 0, 2))
    fits = own == LANES and filter_taps.shape[1] == ROW and ROW % held == 0 and groups % 4 == 0
    fits = fits and groups & (groups - 1) == 0 and parts & (parts - 1) == 0
    small = pltpu.CompilerParams(vmem_limit_bytes=SMALL_BYTES)
    if fits:
        far = pl.BlockSpec(memory_space=pl.ANY)
        coded = (groups, parts, held, own)
        stream = pltpu.VMEM((2 * parts, held, wide // 2), jnp.bfloat16)
        gated = pl.pallas_call(
            send_kernel,
            in_specs=[far],
            out_specs=far,
            out_shape=jax.ShapeDtypeStruct(coded, jnp.bfloat16),
            scratch_shapes=[
                stream,
                stream,
                pltpu.VMEM(coded, jnp.bfloat16),
                pltpu.SemaphoreType.DMA((2, 2 * parts)),
                pltpu.SemaphoreType.DMA((2 * parts,)),
            ],
            compiler_params=pltpu.CompilerParams(vmem_limit_bytes=ALL_BYTES),
            cost_estimate=cost(2**25, 2**23),
            name="encode_gated",
        )(streams)
        queries = pl.pallas_call(
            query_kernel,
            in_specs=[far],
            out_specs=[far] * parts,
            out_shape=[jax.ShapeDtypeStruct((held, wide), jnp.bfloat16)] * parts,
            scratch_shapes=[pltpu.SemaphoreType.DMA((parts,))],
            compiler_params=small,
            cost_estimate=cost(2**10, 2**20),
            name="send_queries",
        )(streams)
        taps = pl.pallas_call(
            taps_kernel,
            out_shape=[jax.ShapeDtypeStruct((own, ROW), jnp.bfloat16)] * groups,
            compiler_params=small,
            cost_estimate=cost(2**25, 2**23),
            name="encode_taps",
        )(filter_taps.reshape(groups, own, ROW), skip_gain.reshape(groups, own))
    else:
        gated = encode(streams[1].astype(jnp.float32) * streams[2].astype(jnp.float32), 0)
        gated = jnp.transpose(gated.reshape(held, parts, groups, own), (2, 1, 0, 3))
        queries = jnp.transpose(streams[0].reshape(held, parts, wide), (1, 0, 2))
        first = lax.axis_index("seq") == 0
        taps = filter_taps.at[:, 0].add(jnp.where(first, skip_gain, 0.0))
        taps = encode(taps, 1).reshape(groups, own, -1)
    exchange = functools.partial(lax.all_to_all, split_axis=0, concat_axis=0, tiled=True)
    gated = gated.reshape(groups * parts, held, own)
    if fits:
        taps = scatter(taps, "seq")
        gated = exchange(gated, ("seq", "ch"))
        queries = scatter(queries, "ch")
    else:
        taps = exchange(taps, "seq")
        gated = exchange(gated, ("seq", "ch"))
        queries = exchange(queries, "ch").reshape(parts * held, wide)
    if fits:
        high, low, twist, mix = tables(blocks)
        wave = np.concatenate([high, low, high], axis=0)
        scratch = [pltpu.VMEM((blocks * 2 * HALF, 3 * ROW), jnp.bfloat16)] * 2
        scratch += [pltpu.VMEM((blocks * 2 * HALF, 2 * ROW), jnp.float32)] * 2
        large = pltpu.CompilerParams(vmem_limit_bytes=VMEM_BYTES)
        gated = pl.pallas_call(
            functools.partial(gated_spectrum_kernel, mix),
            out_shape=jax.ShapeDtypeStruct((2, blocks, 2, HALF, ROW), jnp.float32),
            scratch_shapes=[pltpu.VMEM((blocks, own, ROW), jnp.float32)] + scratch,
            compiler_params=large,
            cost_estimate=cost(2**32, 2**24),
            name="gated_spectrum",
        )(gated, wave, twist)
        convolved = pl.pallas_call(
            functools.partial(conv_kernel, mix),
            out_shape=[jax.ShapeDtypeStruct((own, ROW), jnp.bfloat16)] * groups,
            scratch_shapes=[pltpu.VMEM((blocks, own, ROW), jnp.bfloat16)] * 2 + scratch,
            compiler_params=large,
            cost_estimate=cost(2**32, 2**24),
            name="convolve",
        )(gated, *taps, wave, twist)
    else:
        gated = decode(gated, 1).reshape(blocks, ROW, own)
        taps = jnp.transpose(decode(taps, 2), (1, 0, 2)).reshape(own, blocks, ROW)
        convolved = plain_conv(jnp.transpose(gated, (0, 2, 1)), jnp.transpose(taps, (1, 0, 2)))
        convolved = jnp.transpose(convolved, (1, 0, 2)).reshape(own, groups, -1)
        convolved = encode(jnp.transpose(convolved, (1, 0, 2)), 2)
    if fits:
        convolved = scatter(convolved, "seq")
        queries = pl.pallas_call(
            turn_kernel,
            out_shape=jax.ShapeDtypeStruct((wide, ROW), jnp.bfloat16),
            scratch_shapes=[pltpu.VMEM((ROW, wide), jnp.float32)],
            compiler_params=small,
            cost_estimate=cost(2**20, 2**21),
            name="turn_queries",
        )(*queries)
        return pl.pallas_call(
            mix_kernel,
            out_specs=far,
            out_shape=jax.ShapeDtypeStruct((wide, ROW), jnp.bfloat16),
            scratch_shapes=[
                pltpu.VMEM((wide, ROW), jnp.bfloat16),
                pltpu.SemaphoreType.DMA((groups,)),
            ],
            compiler_params=small,
            name="mix_out",
        )(queries, *convolved)
    convolved = exchange(convolved, "seq")
    queries = jnp.transpose(queries.astype(jnp.float32))
    return (queries * decode(convolved, 2).reshape(wide, -1)).astype(jnp.bfloat16)


def cost(flops, moved):
    return pl.CostEstimate(flops=int(flops), bytes_accessed=int(moved), transcendentals=0)


def solution(mesh):
    placed = (P(("seq", "ch"), None, None), P("ch", "seq"), P("ch"))
    return jax.shard_map(
        body, mesh=mesh, in_specs=placed, out_specs=P("ch", "seq"), check_vma=False
    )
```

```python
import functools
import math

import jax
import jax.numpy as jnp
import numpy as np
from jax import lax
from jax.experimental import pallas as pl
from jax.experimental.pallas import tpu as pltpu
from jax.sharding import PartitionSpec as P

TOP = 32000.0
TOP_LEVEL = 32255.0
LOW_POWER = 125.0
EXPONENT_BITS = 8
EXPONENT_BIAS = 127.0
LANES = 128
ROW = 256
CHUNK = 16
HALF = 64
VMEM_BYTES = 20 * 1024 * 1024
SMALL_BYTES = 12 * 1024 * 1024
ALL_BYTES = 60 * 1024 * 1024


def split_first(values, axis):
    count = min(values.shape[axis], LANES if axis == values.ndim - 1 else EXPONENT_BITS)
    first = lax.slice_in_dim(values, 0, count, axis=axis)
    if count == values.shape[axis]:
        return first, None
    return first, lax.slice_in_dim(values, count, values.shape[axis], axis=axis)


def encode(values, axis):
    size = jnp.abs(values)
    peak = jnp.max(size, axis=axis, keepdims=True)
    power = jnp.floor(jnp.log(jnp.maximum(peak, 1e-30)) * (1.0 / math.log(2.0))) + 1.0
    power = jnp.clip(power, -100.0, 126.0)
    share = size * jnp.exp2(-power)
    level = jnp.minimum(
        share * (2.0 * TOP), jnp.minimum(share * TOP + TOP / 4, share * (TOP / 2) + TOP / 2)
    )
    first, rest = split_first(level, axis)
    place = lax.broadcasted_iota(jnp.int32, first.shape, axis).astype(jnp.float32)
    halves = jnp.floor((power + (EXPONENT_BIAS + 0.25)) * jnp.exp2(-place))
    bit = halves - 2.0 * jnp.floor(halves * 0.5)
    marked = 2.0 * jnp.floor((first - bit) * 0.5 + 0.5) + bit
    level = jnp.where(place < EXPONENT_BITS, marked, jnp.floor(first + 0.5))
    if rest is not None:
        level = jnp.concatenate([level, jnp.floor(rest + 0.5)], axis=axis)
    level = jnp.minimum(level, TOP_LEVEL) * (1.0 / 128.0)
    octave = jnp.floor(level)
    code = jnp.exp2(octave - LOW_POWER) * (level - octave + 1.0)
    return jnp.where(values < 0.0, -code, code).astype(jnp.bfloat16)


def decode(code, axis, halvings=0):
    code = code.astype(jnp.float32)
    size = jnp.abs(code)
    octave = jnp.floor(jnp.log(size) * (1.0 / math.log(2.0)) + 0.002)
    level = (octave + size * jnp.exp2(-octave) + (LOW_POWER - 1.0)) * 128.0
    first, _ = split_first(level, axis)
    first = jnp.floor(first + 0.5)
    place = lax.broadcasted_iota(jnp.int32, first.shape, axis).astype(jnp.float32)
    bit = first - 2.0 * jnp.floor(first * 0.5)
    held = jnp.where(place < EXPONENT_BITS, bit * jnp.exp2(place), 0.0)
    scale = jnp.exp2(jnp.sum(held, axis=axis, keepdims=True) - (EXPONENT_BIAS + halvings))
    share = jnp.maximum(
        level * (0.5 / TOP),
        jnp.maximum(level * (1.0 / TOP) - 0.25, level * (2.0 / TOP) - 1.0),
    )
    return jnp.where(code < 0.0, -share, share) * scale


def tables(blocks):
    n2 = np.arange(ROW)
    k1 = np.arange(blocks)
    main = 2.0 * np.pi * np.outer(n2, n2) / ROW
    twist = 2.0 * np.pi * np.outer(k1 + 0.25, n2) / (blocks * ROW)
    mix = 2.0 * np.pi * np.outer(k1 + 0.25, np.arange(blocks)) / blocks
    wave = np.concatenate([np.cos(main), np.sin(main)], axis=1).astype(np.float32)
    twist = np.stack([np.cos(twist), np.sin(twist)], axis=1).astype(np.float32)
    mix = np.stack([np.cos(mix), np.sin(mix)], axis=0).astype(np.float32)
    return wave, twist, mix


def folded(wave):
    half = np.concatenate([wave[:, :LANES], wave[:, ROW : ROW + LANES]], axis=1)
    half[:, LANES] = wave[:, LANES]
    parts = []
    for values in (half, half.T):
        high = values.astype(jnp.bfloat16)
        low = (values - high.astype(np.float32)).astype(jnp.bfloat16)
        parts.append(np.concatenate([high, low, high], axis=0))
    return parts


def put_split(ref, at, values):
    high = values.astype(jnp.bfloat16)
    ref[pl.ds(at, values.shape[0]), 0:ROW] = high
    ref[pl.ds(at, values.shape[0]), ROW : 2 * ROW] = high
    ref[pl.ds(at, values.shape[0]), 2 * ROW : 3 * ROW] = (
        values - high.astype(jnp.float32)
    ).astype(jnp.bfloat16)


def turned(value, steps):
    if steps == 0:
        return value
    re, im = value
    cos, sin = math.cos(math.pi * steps / 16), math.sin(math.pi * steps / 16)
    return re * cos - im * sin, im * cos + re * sin


def four_points(values, sign):
    (a_re, a_im), (b_re, b_im), (c_re, c_im), (d_re, d_im) = values
    sum_re, sum_im, gap_re, gap_im = a_re + c_re, a_im + c_im, a_re - c_re, a_im - c_im
    more_re, more_im = b_re + d_re, b_im + d_im
    side_re, side_im = sign * (d_im - b_im), sign * (b_re - d_re)
    return (
        (sum_re + more_re, sum_im + more_im),
        (gap_re + side_re, gap_im + side_im),
        (sum_re - more_re, sum_im - more_im),
        (gap_re - side_re, gap_im - side_im),
    )


def mix_forward(taken, twist_ref, at, ref):
    far = [value * math.sqrt(0.5) for value in taken[4:]]
    even = [turned((taken[n] + far[n], -far[n]), -n) for n in range(4)]
    odd = [turned((taken[n] - far[n], far[n]), -5 * n) for n in range(4)]
    for start, values in ((0, four_points(even, -1.0)), (1, four_points(odd, -1.0))):
        for index, (re, im) in enumerate(values):
            k = start + 2 * index
            cos_twist, sin_twist = twist_ref[k, 0:1, :], twist_ref[k, 1:2, :]
            put_split(ref, 2 * k * HALF + at, re * cos_twist + im * sin_twist)
            put_split(ref, (2 * k + 1) * HALF + at, im * cos_twist - re * sin_twist)


def mix_back(spectra, twist_ref):
    twisted = []
    for k, (re, im) in enumerate(spectra):
        cos_twist, sin_twist = twist_ref[k, 0:1, :], twist_ref[k, 1:2, :]
        twisted.append((re * cos_twist - im * sin_twist, im * cos_twist + re * sin_twist))
    even, odd = four_points(twisted[0::2], 1.0), four_points(twisted[1::2], 1.0)
    near, far = [], []
    for n in range(4):
        (even_re, even_im), (odd_re, odd_im) = turned(even[n], n), turned(odd[n], 5 * n)
        near.append(even_re + odd_re)
        far.append(((even_re - odd_re) - (even_im - odd_im)) * math.sqrt(0.5))
    return near + far


def spectrum_rows(waves_ref, k, at):
    re = waves_ref[pl.ds(2 * k * HALF + at, CHUNK), :]
    im = waves_ref[pl.ds((2 * k + 1) * HALF + at, CHUNK), :]
    return re, im


def send_kernel(streams_ref, gated_ref, keys, values, codes, in_sems, out_sems):
    groups, parts = gated_ref.shape[:2]
    per = groups // 2
    width = per * LANES
    arrivals = []
    for chunk in range(2 * parts):
        lanes = pl.ds(chunk * width, width)
        for stream, buffer in ((1, keys), (2, values)):
            copy = pltpu.make_async_copy(
                streams_ref.at[stream, :, lanes], buffer.at[chunk], in_sems.at[stream - 1, chunk]
            )
            copy.start()
            arrivals.append(copy)
    copies = []
    for chunk in range(2 * parts):
        for copy in arrivals[2 * chunk : 2 * chunk + 2]:
            copy.wait()
        part, first = chunk // 2, chunk % 2 * per
        for block in range(per):
            lanes = slice(block * LANES, (block + 1) * LANES)
            left = keys[chunk, :, lanes].astype(jnp.float32)
            right = values[chunk, :, lanes].astype(jnp.float32)
            codes[first + block, part] = encode(left * right, 0)
        place = (pl.ds(first, per), part)
        copy = pltpu.make_async_copy(codes.at[place], gated_ref.at[place], out_sems.at[chunk])
        copy.start()
        copies.append(copy)
    for copy in copies:
        copy.wait()


def query_kernel(streams_ref, *refs):
    query_refs, sems = refs[:-1], refs[-1]
    me = lax.axis_index("ch")
    wide = query_refs[0].shape[1]
    copies = []
    for turn, query_ref in enumerate(query_refs):
        lanes = pl.ds(pl.multiple_of((me ^ turn) * wide, wide), wide)
        copy = pltpu.make_async_copy(streams_ref.at[0, :, lanes], query_ref, sems.at[turn])
        copy.start()
        copies.append(copy)
    for copy in copies:
        copy.wait()


def taps_kernel(taps_ref, skip_ref, *code_refs):
    me = lax.axis_index("seq")
    first = (me == 0).astype(jnp.float32)
    row = lax.broadcasted_iota(jnp.int32, (LANES, LANES), 0)
    lane = lax.broadcasted_iota(jnp.int32, (LANES, LANES), 1)
    for turn, code_ref in enumerate(code_refs):
        block = me ^ turn
        gains = jnp.broadcast_to(skip_ref[pl.ds(block, 1), :], (LANES, LANES))
        gain = jnp.sum(jnp.where(row == lane, gains, 0.0), axis=1, keepdims=True) * first
        start = taps_ref[block, :, :LANES] + jnp.where(lane == 0, gain, 0.0)
        taps = jnp.concatenate([start, taps_ref[block, :, LANES:]], axis=1)
        code_ref[...] = encode(taps, 1)


def first_lane():
    return lax.broadcasted_iota(jnp.int32, (CHUNK, LANES), 1) == 0


def combined(waves_ref, k, at):
    re, im = spectrum_rows(waves_ref, k, at)
    first = first_lane()
    re_cos, re_sin, im_cos, im_sin = re[:, :LANES], re[:, LANES:], im[:, :LANES], im[:, LANES:]
    near = (
        re_cos + jnp.where(first, 0.0, im_sin),
        im_cos - jnp.where(first, 0.0, re_sin),
    )
    far = (
        jnp.where(first, re_sin, re_cos - im_sin),
        jnp.where(first, im_sin, im_cos + re_sin),
    )
    return [jnp.concatenate([left, right], axis=1) for left, right in zip(near, far)]


def put_folded(ref, k, at, re, im):
    first = first_lane()
    near_re, far_re, near_im, far_im = re[:, :LANES], re[:, LANES:], im[:, :LANES], im[:, LANES:]
    back_re = [
        jnp.where(first, near_re, near_re + far_re),
        jnp.where(first, far_re, far_im - near_im),
    ]
    back_im = [
        jnp.where(first, near_im, near_im + far_im),
        jnp.where(first, far_im, near_re - far_re),
    ]
    put_split(ref, 2 * k * HALF + at, jnp.concatenate(back_re, axis=1))
    put_split(ref, (2 * k + 1) * HALF + at, jnp.concatenate(back_im, axis=1))


def stage(wave_ref, source, target, work, half):
    steps = 2
    chunks = HALF // CHUNK // steps

    def step(index, _):
        if source is not None:
            count = source.shape[0] // steps
            at = pl.ds(pl.multiple_of(index * count, count), count)
            target[at, :] = jnp.dot(
                source[at, :], wave_ref[...], preferred_element_type=jnp.float32
            )
        for chunk in range(chunks):
            work(half, pl.multiple_of((index * chunks + chunk) * CHUNK, CHUNK))
        return 0

    lax.fori_loop(0, steps, step, 0)


def gated_spectrum_kernel(gated_ref, wave_ref, twist_ref, out_ref, u, *scratch):
    blocks = u.shape[0]
    rows, waves = scratch[0:2], scratch[2:4]
    parts = ROW // gated_ref.shape[1]

    def unpack(block, _):
        pieces = [decode(gated_ref[block * parts + part], 0) for part in range(parts)]
        u[block] = jnp.transpose(jnp.concatenate(pieces, axis=0))
        return 0

    def forward(half, at):
        start = pl.ds(half * HALF + at, CHUNK)
        mix_forward([u[n1, start, :] for n1 in range(blocks)], twist_ref, at, rows[half])

    def finish(half, at):
        for k in range(blocks):
            re, im = combined(waves[half], k, at)
            out_ref[half, k, 0, pl.ds(at, CHUNK), :] = re
            out_ref[half, k, 1, pl.ds(at, CHUNK), :] = im

    lax.fori_loop(0, blocks, unpack, 0)
    stage(None, None, None, forward, 0)
    stage(wave_ref, rows[0], waves[0], forward, 1)
    stage(wave_ref, rows[1], waves[1], finish, 0)
    stage(None, None, None, finish, 1)


def conv_kernel(gated_ref, *refs):
    blocks = gated_ref.shape[1]
    wave_ref, back_wave_ref, twist_ref, out, codes, *scratch = refs[blocks:]
    rows, waves = scratch[0:2], scratch[2:4]
    scale = math.log2(blocks * ROW)
    me = lax.axis_index("seq")
    for turn, code_ref in enumerate(refs[:blocks]):
        codes[me ^ turn] = code_ref[...]

    def forward(half, at):
        start = pl.ds(half * HALF + at, CHUNK)
        taken = [decode(codes[n1, start, :], 1, scale) for n1 in range(blocks)]
        mix_forward(taken, twist_ref, at, rows[half])

    def product(half, at):
        for k in range(blocks):
            re, im = combined(waves[half], k, at)
            gated_re = gated_ref[half, k, 0, pl.ds(at, CHUNK), :]
            gated_im = gated_ref[half, k, 1, pl.ds(at, CHUNK), :]
            product_re, product_im = re * gated_re - im * gated_im, re * gated_im + im * gated_re
            put_folded(rows[half], k, at, product_re, product_im)

    def back(half, at):
        spectra = [spectrum_rows(waves[half], k, at) for k in range(blocks)]
        start = pl.ds(half * HALF + at, CHUNK)
        for n1, total in enumerate(mix_back(spectra, twist_ref)):
            out[n1, start, :] = encode(total, 1)

    stage(None, None, None, forward, 0)
    stage(wave_ref, rows[0], waves[0], forward, 1)
    stage(wave_ref, rows[1], waves[1], product, 0)
    stage(back_wave_ref, rows[0], waves[0], product, 1)
    stage(back_wave_ref, rows[1], waves[1], back, 0)
    stage(None, None, None, back, 1)


def turn_kernel(*refs):
    query_refs, out_ref, whole = refs[:-2], refs[-2], refs[-1]
    me = lax.axis_index("ch")
    held = query_refs[0].shape[0]
    for turn, query_ref in enumerate(query_refs):
        at = pl.multiple_of((me ^ turn) * held, held)
        whole[pl.ds(at, held), :] = query_ref[...].astype(jnp.float32)
    out_ref[...] = jnp.transpose(whole[...]).astype(jnp.bfloat16)


def mix_kernel(query_ref, conv_ref, out_ref, mixed, sems):
    copies = []
    for block in range(conv_ref.shape[0]):
        at = pl.ds(block * LANES, LANES)
        queries = query_ref[at, :].astype(jnp.float32)
        mixed[at, :] = (queries * decode(conv_ref[block], 1)).astype(jnp.bfloat16)
        copy = pltpu.make_async_copy(mixed.at[at], out_ref.at[at], sems.at[block])
        copy.start()
        copies.append(copy)
    for copy in copies:
        copy.wait()


def plain_conv(gated, taps):
    blocks = gated.shape[0]
    wave, twist, mix = tables(blocks)
    cos_twist, sin_twist = twist[:, 0][:, None, :], twist[:, 1][:, None, :]
    dot = functools.partial(jnp.einsum, precision=lax.Precision.HIGHEST)

    def forward(values):
        re = dot("ncm,kn->kcm", values, mix[0])
        im = -dot("ncm,kn->kcm", values, mix[1])
        re, im = re * cos_twist + im * sin_twist, im * cos_twist - re * sin_twist
        re, im = dot("kcm,mq->kcq", re, wave), dot("kcm,mq->kcq", im, wave)
        return re[..., :ROW] + im[..., ROW:], im[..., :ROW] - re[..., ROW:]

    u_re, u_im = forward(gated)
    h_re, h_im = forward(taps)
    re = dot("kcm,mq->kcq", u_re * h_re - u_im * h_im, wave)
    im = dot("kcm,mq->kcq", u_re * h_im + u_im * h_re, wave)
    re, im = re[..., :ROW] - im[..., ROW:], im[..., :ROW] + re[..., ROW:]
    re, im = re * cos_twist - im * sin_twist, im * cos_twist + re * sin_twist
    total = dot("kcm,kn->ncm", re, mix[0]) - dot("kcm,kn->ncm", im, mix[1])
    return total * (1.0 / (blocks * ROW))


def scatter(blocks, axis):
    count = len(blocks)
    return [
        lax.ppermute(block, axis, [(i, i ^ turn) for i in range(count)]) if turn else block
        for turn, block in enumerate(blocks)
    ]


def body(streams, filter_taps, skip_gain):
    groups, parts = lax.axis_size("seq"), lax.axis_size("ch")
    held, _, channels = streams.shape
    wide = channels // parts
    own = wide // groups
    blocks = filter_taps.shape[1] * groups // ROW
    streams = jnp.transpose(streams, (1, 0, 2))
    fits = blocks == 8 and own == LANES and filter_taps.shape[1] == ROW and ROW % held == 0 and groups % 4 == 0
    fits = fits and groups & (groups - 1) == 0 and parts & (parts - 1) == 0
    small = pltpu.CompilerParams(vmem_limit_bytes=SMALL_BYTES)
    if fits:
        far = pl.BlockSpec(memory_space=pl.ANY)
        coded = (groups, parts, held, own)
        stream = pltpu.VMEM((2 * parts, held, wide // 2), jnp.bfloat16)
        gated = pl.pallas_call(
            send_kernel,
            in_specs=[far],
            out_specs=far,
            out_shape=jax.ShapeDtypeStruct(coded, jnp.bfloat16),
            scratch_shapes=[
                stream,
                stream,
                pltpu.VMEM(coded, jnp.bfloat16),
                pltpu.SemaphoreType.DMA((2, 2 * parts)),
                pltpu.SemaphoreType.DMA((2 * parts,)),
            ],
            compiler_params=pltpu.CompilerParams(vmem_limit_bytes=ALL_BYTES),
            cost_estimate=cost(2**25, 2**23),
            name="encode_gated",
        )(streams)
        queries = pl.pallas_call(
            query_kernel,
            in_specs=[far],
            out_specs=[far] * parts,
            out_shape=[jax.ShapeDtypeStruct((held, wide), jnp.bfloat16)] * parts,
            scratch_shapes=[pltpu.SemaphoreType.DMA((parts,))],
            compiler_params=small,
            cost_estimate=cost(2**10, 2**20),
            name="send_queries",
        )(streams)
        taps = pl.pallas_call(
            taps_kernel,
            out_shape=[jax.ShapeDtypeStruct((own, ROW), jnp.bfloat16)] * groups,
            compiler_params=small,
            cost_estimate=cost(2**25, 2**23),
            name="encode_taps",
        )(filter_taps.reshape(groups, own, ROW), skip_gain.reshape(groups, own))
    else:
        gated = encode(streams[1].astype(jnp.float32) * streams[2].astype(jnp.float32), 0)
        gated = jnp.transpose(gated.reshape(held, parts, groups, own), (2, 1, 0, 3))
        queries = jnp.transpose(streams[0].reshape(held, parts, wide), (1, 0, 2))
        first = lax.axis_index("seq") == 0
        taps = filter_taps.at[:, 0].add(jnp.where(first, skip_gain, 0.0))
        taps = encode(taps, 1).reshape(groups, own, -1)
    exchange = functools.partial(lax.all_to_all, split_axis=0, concat_axis=0, tiled=True)
    gated = gated.reshape(groups * parts, held, own)
    if fits:
        taps = scatter(taps, "seq")
        gated = exchange(gated, ("seq", "ch"))
        queries = scatter(queries, "ch")
    else:
        taps = exchange(taps, "seq")
        gated = exchange(gated, ("seq", "ch"))
        queries = exchange(queries, "ch").reshape(parts * held, wide)
    if fits:
        wave, twist, _ = tables(blocks)
        wave, back_wave = folded(wave)
        scratch = [pltpu.VMEM((blocks * 2 * HALF, 3 * ROW), jnp.bfloat16)] * 2
        scratch += [pltpu.VMEM((blocks * 2 * HALF, ROW), jnp.float32)] * 2
        large = pltpu.CompilerParams(vmem_limit_bytes=VMEM_BYTES)
        gated = pl.pallas_call(
            gated_spectrum_kernel,
            out_shape=jax.ShapeDtypeStruct((2, blocks, 2, HALF, ROW), jnp.float32),
            scratch_shapes=[pltpu.VMEM((blocks, own, ROW), jnp.float32)] + scratch,
            compiler_params=large,
            cost_estimate=cost(2**32, 2**24),
            name="gated_spectrum",
        )(gated, wave, twist)
        convolved = pl.pallas_call(
            conv_kernel,
            out_shape=jax.ShapeDtypeStruct((blocks, own, ROW), jnp.bfloat16),
            scratch_shapes=[pltpu.VMEM((blocks, own, ROW), jnp.bfloat16)] + scratch,
            compiler_params=large,
            cost_estimate=cost(2**32, 2**24),
            name="convolve",
        )(gated, *taps, wave, back_wave, twist)
    else:
        gated = decode(gated, 1).reshape(blocks, ROW, own)
        taps = jnp.transpose(decode(taps, 2), (1, 0, 2)).reshape(own, blocks, ROW)
        convolved = plain_conv(jnp.transpose(gated, (0, 2, 1)), jnp.transpose(taps, (1, 0, 2)))
        convolved = jnp.transpose(convolved, (1, 0, 2)).reshape(own, groups, -1)
        convolved = encode(jnp.transpose(convolved, (1, 0, 2)), 2)
    convolved = exchange(convolved, "seq")
    if fits:
        queries = pl.pallas_call(
            turn_kernel,
            out_shape=jax.ShapeDtypeStruct((wide, ROW), jnp.bfloat16),
            scratch_shapes=[pltpu.VMEM((ROW, wide), jnp.float32)],
            compiler_params=small,
            cost_estimate=cost(2**20, 2**21),
            name="turn_queries",
        )(*queries)
        return pl.pallas_call(
            mix_kernel,
            out_specs=far,
            out_shape=jax.ShapeDtypeStruct((wide, ROW), jnp.bfloat16),
            scratch_shapes=[
                pltpu.VMEM((wide, ROW), jnp.bfloat16),
                pltpu.SemaphoreType.DMA((groups,)),
            ],
            compiler_params=small,
            name="mix_out",
        )(queries, convolved)
    queries = jnp.transpose(queries.astype(jnp.float32))
    return (queries * decode(convolved, 2).reshape(wide, -1)).astype(jnp.bfloat16)


def cost(flops, moved):
    return pl.CostEstimate(flops=int(flops), bytes_accessed=int(moved), transcendentals=0)


def solution(mesh):
    placed = (P(("seq", "ch"), None, None), P("ch", "seq"), P("ch"))
    return jax.shard_map(
        body, mesh=mesh, in_specs=placed, out_specs=P("ch", "seq"), check_vma=False
    )
```

```python
import functools
import math

import jax
import jax.numpy as jnp
import numpy as np
from jax import lax
from jax.experimental import pallas as pl
from jax.experimental.pallas import tpu as pltpu
from jax.sharding import PartitionSpec as P

OCTAVES = 250.0
LOW_POWER = 125.0
EXPONENT_BITS = 8
EXPONENT_BIAS = 127.0
LANES = 128
ROW = 256
CHUNK = 16
HALF = 64
VMEM_BYTES = 20 * 1024 * 1024
SMALL_BYTES = 12 * 1024 * 1024
ALL_BYTES = 60 * 1024 * 1024


def split_first(values, axis):
    count = min(values.shape[axis], LANES if axis == values.ndim - 1 else EXPONENT_BITS)
    first = lax.slice_in_dim(values, 0, count, axis=axis)
    if count == values.shape[axis]:
        return first, None
    return first, lax.slice_in_dim(values, count, values.shape[axis], axis=axis)


def scale_of(peak):
    power = jnp.floor(jnp.log(jnp.maximum(peak, 1e-30)) * (1.0 / math.log(2.0))) + 1.0
    return jnp.clip(power, -100.0, 126.0)


def exponent_bits(power, shape, axis):
    place = lax.broadcasted_iota(jnp.int32, shape, axis).astype(jnp.float32)
    bits = (power + (EXPONENT_BIAS + 0.25)) * jnp.exp2(-1.0 - place)
    return jnp.where(bits - jnp.floor(bits) >= 0.5, 0.5, 0.0), place < EXPONENT_BITS


def encode(values, axis):
    peak = jnp.max(jnp.abs(values), axis=axis, keepdims=True)
    return encode_all([values], scale_of(peak), axis)[0]


def encode_all(blocks, power, axis):
    unit_share, codes, bits = jnp.exp2(-power), [], None
    for values in blocks:
        share = jnp.abs(values) * unit_share
        level = jnp.minimum(
            share * (2.0 * OCTAVES),
            jnp.minimum(share * OCTAVES + OCTAVES / 4, share * (OCTAVES / 2) + OCTAVES / 2),
        )
        level = jnp.minimum(level, OCTAVES + 1.0)
        first, rest = split_first(level, axis)
        bits = exponent_bits(power, first.shape, axis) if bits is None else bits
        odd, holds = bits
        marked = (jnp.floor(first * 64.0 - odd + 0.5) + odd) * (1.0 / 64.0)
        level = jnp.where(holds, marked, first)
        if rest is not None:
            level = jnp.concatenate([level, rest], axis=axis)
        octave = jnp.floor(level)
        unit = jnp.exp2(octave - LOW_POWER)
        code = jnp.where(values < 0.0, -unit, unit) * (level - octave + 1.0)
        codes.append(code.astype(jnp.bfloat16))
    return codes


def decode(code, axis, halvings=0):
    code = code.astype(jnp.float32)
    size = jnp.abs(code)
    octave = jnp.floor(jnp.log(size) * (1.0 / math.log(2.0)) + 0.002)
    level = octave + size * jnp.exp2(-octave)
    first, _ = split_first(level, axis)
    half = first * 64.0 + ((LOW_POWER - 1.0) * 64.0 + 0.25)
    place = lax.broadcasted_iota(jnp.int32, first.shape, axis).astype(jnp.float32)
    weight = jnp.where(place < EXPONENT_BITS, jnp.exp2(place), 0.0)
    held = jnp.where(half - jnp.floor(half) >= 0.5, weight, 0.0)
    scale = jnp.exp2(jnp.sum(held, axis=axis, keepdims=True) - (EXPONENT_BIAS + halvings))
    step = 0.5 / OCTAVES
    low = (LOW_POWER - 1.0) * step
    share = jnp.maximum(
        level * step + low,
        jnp.maximum(
            level * (2.0 * step) + (2.0 * low - 0.25), level * (4.0 * step) + (4.0 * low - 1.0)
        ),
    )
    return jnp.where(code < 0.0, -scale, scale) * share


def tables(blocks):
    n2 = np.arange(ROW)
    k1 = np.arange(blocks)
    main = 2.0 * np.pi * np.outer(n2, n2) / ROW
    twist = 2.0 * np.pi * np.outer(k1 + 0.25, n2) / (blocks * ROW)
    mix = 2.0 * np.pi * np.outer(k1 + 0.25, np.arange(blocks)) / blocks
    wave = np.concatenate([np.cos(main), np.sin(main)], axis=1).astype(np.float32)
    twist = np.stack([np.cos(twist), np.sin(twist)], axis=1).astype(np.float32)
    mix = np.stack([np.cos(mix), np.sin(mix)], axis=0).astype(np.float32)
    return wave, twist, mix


def folded(wave):
    half = np.concatenate([wave[:, :LANES], wave[:, ROW : ROW + LANES]], axis=1)
    half[:, LANES] = wave[:, LANES]
    parts = []
    for values in (half, half.T):
        high = values.astype(jnp.bfloat16)
        low = (values - high.astype(np.float32)).astype(jnp.bfloat16)
        parts.append(np.concatenate([high, low, high], axis=0))
    return parts


def put_split(ref, at, values):
    high = values.astype(jnp.bfloat16)
    ref[pl.ds(at, values.shape[0]), 0:ROW] = high
    ref[pl.ds(at, values.shape[0]), ROW : 2 * ROW] = high
    ref[pl.ds(at, values.shape[0]), 2 * ROW : 3 * ROW] = (
        values - high.astype(jnp.float32)
    ).astype(jnp.bfloat16)


def turned(value, steps):
    if steps == 0:
        return value
    re, im = value
    cos, sin = math.cos(math.pi * steps / 16), math.sin(math.pi * steps / 16)
    return re * cos - im * sin, im * cos + re * sin


def four_points(values, sign):
    (a_re, a_im), (b_re, b_im), (c_re, c_im), (d_re, d_im) = values
    sum_re, sum_im, gap_re, gap_im = a_re + c_re, a_im + c_im, a_re - c_re, a_im - c_im
    more_re, more_im = b_re + d_re, b_im + d_im
    side_re, side_im = sign * (d_im - b_im), sign * (b_re - d_re)
    return (
        (sum_re + more_re, sum_im + more_im),
        (gap_re + side_re, gap_im + side_im),
        (sum_re - more_re, sum_im - more_im),
        (gap_re - side_re, gap_im - side_im),
    )


def mix_forward(taken, twist_ref, at, ref):
    far = [value * math.sqrt(0.5) for value in taken[4:]]
    even = [turned((taken[n] + far[n], -far[n]), -n) for n in range(4)]
    odd = [turned((taken[n] - far[n], far[n]), -5 * n) for n in range(4)]
    for start, values in ((0, four_points(even, -1.0)), (1, four_points(odd, -1.0))):
        for index, (re, im) in enumerate(values):
            k = start + 2 * index
            cos_twist, sin_twist = twist_ref[k, 0:1, :], twist_ref[k, 1:2, :]
            put_split(ref, 2 * k * HALF + at, re * cos_twist + im * sin_twist)
            put_split(ref, (2 * k + 1) * HALF + at, im * cos_twist - re * sin_twist)


def mix_back(spectra, twist_ref):
    twisted = []
    for k, (re, im) in enumerate(spectra):
        cos_twist, sin_twist = twist_ref[k, 0:1, :], twist_ref[k, 1:2, :]
        twisted.append((re * cos_twist - im * sin_twist, im * cos_twist + re * sin_twist))
    even, odd = four_points(twisted[0::2], 1.0), four_points(twisted[1::2], 1.0)
    near, far = [], []
    for n in range(4):
        (even_re, even_im), (odd_re, odd_im) = turned(even[n], n), turned(odd[n], 5 * n)
        near.append(even_re + odd_re)
        far.append(((even_re - odd_re) - (even_im - odd_im)) * math.sqrt(0.5))
    return near + far


def spectrum_rows(waves_ref, k, at):
    re = waves_ref[pl.ds(2 * k * HALF + at, CHUNK), :]
    im = waves_ref[pl.ds((2 * k + 1) * HALF + at, CHUNK), :]
    return re, im


def send_kernel(streams_ref, gated_ref, keys, values, codes, in_sems, out_sems):
    groups, parts = gated_ref.shape[:2]
    per = groups // 2
    width = per * LANES
    arrivals = []
    for chunk in range(2 * parts):
        lanes = pl.ds(chunk * width, width)
        for stream, buffer in ((1, keys), (2, values)):
            copy = pltpu.make_async_copy(
                streams_ref.at[stream, :, lanes], buffer.at[chunk], in_sems.at[stream - 1, chunk]
            )
            copy.start()
            arrivals.append(copy)
    copies = []
    for chunk in range(2 * parts):
        for copy in arrivals[2 * chunk : 2 * chunk + 2]:
            copy.wait()
        part, first = chunk // 2, chunk % 2 * per
        for block in range(per):
            lanes = slice(block * LANES, (block + 1) * LANES)
            left = keys[chunk, :, lanes].astype(jnp.float32)
            right = values[chunk, :, lanes].astype(jnp.float32)
            codes[first + block, part] = encode(left * right, 0)
        place = (pl.ds(first, per), part)
        copy = pltpu.make_async_copy(codes.at[place], gated_ref.at[place], out_sems.at[chunk])
        copy.start()
        copies.append(copy)
    for copy in copies:
        copy.wait()


def query_kernel(streams_ref, *refs):
    query_refs, sems = refs[:-1], refs[-1]
    me = lax.axis_index("ch")
    wide = query_refs[0].shape[1]
    copies = []
    for turn, query_ref in enumerate(query_refs):
        lanes = pl.ds(pl.multiple_of((me ^ turn) * wide, wide), wide)
        copy = pltpu.make_async_copy(streams_ref.at[0, :, lanes], query_ref, sems.at[turn])
        copy.start()
        copies.append(copy)
    for copy in copies:
        copy.wait()


def taps_kernel(taps_ref, skip_ref, *code_refs):
    me = lax.axis_index("seq")
    first = (me == 0).astype(jnp.float32)
    row = lax.broadcasted_iota(jnp.int32, (LANES, LANES), 0)
    lane = lax.broadcasted_iota(jnp.int32, (LANES, LANES), 1)
    for turn, code_ref in enumerate(code_refs):
        block = me ^ turn
        gains = jnp.broadcast_to(skip_ref[pl.ds(block, 1), :], (LANES, LANES))
        gain = jnp.sum(jnp.where(row == lane, gains, 0.0), axis=1, keepdims=True) * first
        start = taps_ref[block, :, :LANES] + jnp.where(lane == 0, gain, 0.0)
        taps = jnp.concatenate([start, taps_ref[block, :, LANES:]], axis=1)
        code_ref[...] = encode(taps, 1)


def first_lane():
    return lax.broadcasted_iota(jnp.int32, (CHUNK, LANES), 1) == 0


def combined(waves_ref, k, at):
    re, im = spectrum_rows(waves_ref, k, at)
    first = first_lane()
    re_cos, re_sin, im_cos, im_sin = re[:, :LANES], re[:, LANES:], im[:, :LANES], im[:, LANES:]
    near = (
        re_cos + jnp.where(first, 0.0, im_sin),
        im_cos - jnp.where(first, 0.0, re_sin),
    )
    far = (
        jnp.where(first, re_sin, re_cos - im_sin),
        jnp.where(first, im_sin, im_cos + re_sin),
    )
    return [jnp.concatenate([left, right], axis=1) for left, right in zip(near, far)]


def put_folded(ref, k, at, re, im):
    first = first_lane()
    near_re, far_re, near_im, far_im = re[:, :LANES], re[:, LANES:], im[:, :LANES], im[:, LANES:]
    back_re = [
        jnp.where(first, near_re, near_re + far_re),
        jnp.where(first, far_re, far_im - near_im),
    ]
    back_im = [
        jnp.where(first, near_im, near_im + far_im),
        jnp.where(first, far_im, near_re - far_re),
    ]
    put_split(ref, 2 * k * HALF + at, jnp.concatenate(back_re, axis=1))
    put_split(ref, (2 * k + 1) * HALF + at, jnp.concatenate(back_im, axis=1))


def stage(wave_ref, source, target, work, half):
    steps = 2
    chunks = HALF // CHUNK // steps

    def step(index, _):
        if source is not None:
            count = source.shape[0] // steps
            at = pl.ds(pl.multiple_of(index * count, count), count)
            target[at, :] = jnp.dot(
                source[at, :], wave_ref[...], preferred_element_type=jnp.float32
            )
        for chunk in range(chunks):
            work(half, pl.multiple_of((index * chunks + chunk) * CHUNK, CHUNK))
        return 0

    lax.fori_loop(0, steps, step, 0)


def gated_spectrum_kernel(gated_ref, wave_ref, twist_ref, out_ref, u, *scratch):
    blocks = u.shape[0]
    rows, waves = scratch[0:2], scratch[2:4]
    parts = ROW // gated_ref.shape[1]

    def unpack(block, _):
        pieces = [decode(gated_ref[block * parts + part], 0) for part in range(parts)]
        u[block] = jnp.transpose(jnp.concatenate(pieces, axis=0))
        return 0

    def forward(half, at):
        start = pl.ds(half * HALF + at, CHUNK)
        mix_forward([u[n1, start, :] for n1 in range(blocks)], twist_ref, at, rows[half])

    def finish(half, at):
        for k in range(blocks):
            re, im = combined(waves[half], k, at)
            out_ref[half, k, 0, pl.ds(at, CHUNK), :] = re
            out_ref[half, k, 1, pl.ds(at, CHUNK), :] = im

    lax.fori_loop(0, blocks, unpack, 0)
    stage(None, None, None, forward, 0)
    stage(wave_ref, rows[0], waves[0], forward, 1)
    stage(wave_ref, rows[1], waves[1], finish, 0)
    stage(None, None, None, finish, 1)


def conv_kernel(gated_ref, *refs):
    blocks = gated_ref.shape[1]
    wave_ref, back_wave_ref, twist_ref, out_ref, codes, out, sems, *scratch = refs[blocks:]
    rows, waves = scratch[0:2], scratch[2:4]
    scale = math.log2(blocks * ROW)
    me = lax.axis_index("seq")
    for turn, code_ref in enumerate(refs[:blocks]):
        codes[me ^ turn] = code_ref[...]

    def forward(half, at):
        start = pl.ds(half * HALF + at, CHUNK)
        taken = [decode(codes[n1, start, :], 1, scale) for n1 in range(blocks)]
        mix_forward(taken, twist_ref, at, rows[half])

    def product(half, at):
        for k in range(blocks):
            re, im = combined(waves[half], k, at)
            gated_re = gated_ref[half, k, 0, pl.ds(at, CHUNK), :]
            gated_im = gated_ref[half, k, 1, pl.ds(at, CHUNK), :]
            product_re, product_im = re * gated_re - im * gated_im, re * gated_im + im * gated_re
            put_folded(rows[half], k, at, product_re, product_im)

    def back(half, at):
        spectra = [spectrum_rows(waves[half], k, at) for k in range(blocks)]
        start = pl.ds(half * HALF + at, CHUNK)
        totals = mix_back(spectra, twist_ref)
        sizes = [jnp.abs(total) for total in totals]
        peak = jnp.max(functools.reduce(jnp.maximum, sizes), axis=1, keepdims=True)
        for n1, code in enumerate(encode_all(totals, scale_of(peak), 1)):
            out[n1, start, :] = code

    def out_copy(half):
        start = pl.ds(half * HALF, HALF)
        return pltpu.make_async_copy(out.at[:, start, :], out_ref.at[:, start, :], sems.at[half])

    stage(None, None, None, forward, 0)
    stage(wave_ref, rows[0], waves[0], forward, 1)
    stage(wave_ref, rows[1], waves[1], product, 0)
    stage(back_wave_ref, rows[0], waves[0], product, 1)
    stage(back_wave_ref, rows[1], waves[1], back, 0)
    out_copy(0).start()
    stage(None, None, None, back, 1)
    out_copy(1).start()
    out_copy(0).wait()
    out_copy(1).wait()


def turn_kernel(*refs):
    query_refs, out_ref, whole = refs[:-2], refs[-2], refs[-1]
    me = lax.axis_index("ch")
    held = query_refs[0].shape[0]
    for turn, query_ref in enumerate(query_refs):
        at = pl.multiple_of((me ^ turn) * held, held)
        whole[pl.ds(at, held), :] = query_ref[...].astype(jnp.float32)
    out_ref[...] = jnp.transpose(whole[...]).astype(jnp.bfloat16)


def mix_kernel(query_ref, conv_ref, out_ref, mixed, sems):
    copies = []
    for block in range(conv_ref.shape[0]):
        at = pl.ds(block * LANES, LANES)
        queries = query_ref[at, :].astype(jnp.float32)
        mixed[at, :] = (queries * decode(conv_ref[block], 1)).astype(jnp.bfloat16)
        copy = pltpu.make_async_copy(mixed.at[at], out_ref.at[at], sems.at[block])
        copy.start()
        copies.append(copy)
    for copy in copies:
        copy.wait()


def plain_conv(gated, taps):
    blocks = gated.shape[0]
    wave, twist, mix = tables(blocks)
    cos_twist, sin_twist = twist[:, 0][:, None, :], twist[:, 1][:, None, :]
    dot = functools.partial(jnp.einsum, precision=lax.Precision.HIGHEST)

    def forward(values):
        re = dot("ncm,kn->kcm", values, mix[0])
        im = -dot("ncm,kn->kcm", values, mix[1])
        re, im = re * cos_twist + im * sin_twist, im * cos_twist - re * sin_twist
        re, im = dot("kcm,mq->kcq", re, wave), dot("kcm,mq->kcq", im, wave)
        return re[..., :ROW] + im[..., ROW:], im[..., :ROW] - re[..., ROW:]

    u_re, u_im = forward(gated)
    h_re, h_im = forward(taps)
    re = dot("kcm,mq->kcq", u_re * h_re - u_im * h_im, wave)
    im = dot("kcm,mq->kcq", u_re * h_im + u_im * h_re, wave)
    re, im = re[..., :ROW] - im[..., ROW:], im[..., :ROW] + re[..., ROW:]
    re, im = re * cos_twist - im * sin_twist, im * cos_twist + re * sin_twist
    total = dot("kcm,kn->ncm", re, mix[0]) - dot("kcm,kn->ncm", im, mix[1])
    return total * (1.0 / (blocks * ROW))


def scatter(blocks, axis):
    count = len(blocks)
    return [
        lax.ppermute(block, axis, [(i, i ^ turn) for i in range(count)]) if turn else block
        for turn, block in enumerate(blocks)
    ]


def body(streams, filter_taps, skip_gain):
    groups, parts = lax.axis_size("seq"), lax.axis_size("ch")
    held, _, channels = streams.shape
    wide = channels // parts
    own = wide // groups
    blocks = filter_taps.shape[1] * groups // ROW
    streams = jnp.transpose(streams, (1, 0, 2))
    fits = blocks == 8 and own == LANES and filter_taps.shape[1] == ROW and ROW % held == 0 and groups % 4 == 0
    fits = fits and groups & (groups - 1) == 0 and parts & (parts - 1) == 0
    small = pltpu.CompilerParams(vmem_limit_bytes=SMALL_BYTES)
    if fits:
        far = pl.BlockSpec(memory_space=pl.ANY)
        coded = (groups, parts, held, own)
        stream = pltpu.VMEM((2 * parts, held, wide // 2), jnp.bfloat16)
        gated = pl.pallas_call(
            send_kernel,
            in_specs=[far],
            out_specs=far,
            out_shape=jax.ShapeDtypeStruct(coded, jnp.bfloat16),
            scratch_shapes=[
                stream,
                stream,
                pltpu.VMEM(coded, jnp.bfloat16),
                pltpu.SemaphoreType.DMA((2, 2 * parts)),
                pltpu.SemaphoreType.DMA((2 * parts,)),
            ],
            compiler_params=pltpu.CompilerParams(vmem_limit_bytes=ALL_BYTES),
            cost_estimate=cost(2**25, 2**23),
            name="encode_gated",
        )(streams)
        queries = pl.pallas_call(
            query_kernel,
            in_specs=[far],
            out_specs=[far] * parts,
            out_shape=[jax.ShapeDtypeStruct((held, wide), jnp.bfloat16)] * parts,
            scratch_shapes=[pltpu.SemaphoreType.DMA((parts,))],
            compiler_params=small,
            cost_estimate=cost(2**10, 2**20),
            name="send_queries",
        )(streams)
        taps = pl.pallas_call(
            taps_kernel,
            out_shape=[jax.ShapeDtypeStruct((own, ROW), jnp.bfloat16)] * groups,
            compiler_params=small,
            cost_estimate=cost(2**25, 2**23),
            name="encode_taps",
        )(filter_taps.reshape(groups, own, ROW), skip_gain.reshape(groups, own))
    else:
        gated = encode(streams[1].astype(jnp.float32) * streams[2].astype(jnp.float32), 0)
        gated = jnp.transpose(gated.reshape(held, parts, groups, own), (2, 1, 0, 3))
        queries = jnp.transpose(streams[0].reshape(held, parts, wide), (1, 0, 2))
        first = lax.axis_index("seq") == 0
        taps = filter_taps.at[:, 0].add(jnp.where(first, skip_gain, 0.0))
        taps = encode(taps, 1).reshape(groups, own, -1)
    exchange = functools.partial(lax.all_to_all, split_axis=0, concat_axis=0, tiled=True)
    gated = gated.reshape(groups * parts, held, own)
    if fits:
        taps = scatter(taps, "seq")
        gated = exchange(gated, ("seq", "ch"))
        queries = scatter(queries, "ch")
    else:
        taps = exchange(taps, "seq")
        gated = exchange(gated, ("seq", "ch"))
        queries = exchange(queries, "ch").reshape(parts * held, wide)
    if fits:
        wave, twist, _ = tables(blocks)
        wave, back_wave = folded(wave)
        scratch = [pltpu.VMEM((blocks * 2 * HALF, 3 * ROW), jnp.bfloat16)] * 2
        scratch += [pltpu.VMEM((blocks * 2 * HALF, ROW), jnp.float32)] * 2
        large = pltpu.CompilerParams(vmem_limit_bytes=VMEM_BYTES)
        gated = pl.pallas_call(
            gated_spectrum_kernel,
            out_shape=jax.ShapeDtypeStruct((2, blocks, 2, HALF, ROW), jnp.float32),
            scratch_shapes=[pltpu.VMEM((blocks, own, ROW), jnp.float32)] + scratch,
            compiler_params=large,
            cost_estimate=cost(2**32, 2**24),
            name="gated_spectrum",
        )(gated, wave, twist)
        convolved = pl.pallas_call(
            conv_kernel,
            out_shape=jax.ShapeDtypeStruct((blocks, own, ROW), jnp.bfloat16),
            in_specs=[pl.BlockSpec(memory_space=pltpu.VMEM)] * (groups + 4),
            out_specs=far,
            scratch_shapes=[
                pltpu.VMEM((blocks, own, ROW), jnp.bfloat16),
                pltpu.VMEM((blocks, own, ROW), jnp.bfloat16),
                pltpu.SemaphoreType.DMA((2,)),
            ]
            + scratch,
            compiler_params=large,
            cost_estimate=cost(2**32, 2**24),
            name="convolve",
        )(gated, *taps, wave, back_wave, twist)
    else:
        gated = decode(gated, 1).reshape(blocks, ROW, own)
        taps = jnp.transpose(decode(taps, 2), (1, 0, 2)).reshape(own, blocks, ROW)
        convolved = plain_conv(jnp.transpose(gated, (0, 2, 1)), jnp.transpose(taps, (1, 0, 2)))
        convolved = jnp.transpose(convolved, (1, 0, 2)).reshape(own, groups, -1)
        convolved = encode(jnp.transpose(convolved, (1, 0, 2)), 2)
    convolved = exchange(convolved, "seq")
    if fits:
        queries = pl.pallas_call(
            turn_kernel,
            out_shape=jax.ShapeDtypeStruct((wide, ROW), jnp.bfloat16),
            scratch_shapes=[pltpu.VMEM((ROW, wide), jnp.float32)],
            compiler_params=small,
            cost_estimate=cost(2**20, 2**21),
            name="turn_queries",
        )(*queries)
        return pl.pallas_call(
            mix_kernel,
            out_specs=far,
            out_shape=jax.ShapeDtypeStruct((wide, ROW), jnp.bfloat16),
            scratch_shapes=[
                pltpu.VMEM((wide, ROW), jnp.bfloat16),
                pltpu.SemaphoreType.DMA((groups,)),
            ],
            compiler_params=small,
            name="mix_out",
        )(queries, convolved)
    queries = jnp.transpose(queries.astype(jnp.float32))
    return (queries * decode(convolved, 2).reshape(wide, -1)).astype(jnp.bfloat16)


def cost(flops, moved):
    return pl.CostEstimate(flops=int(flops), bytes_accessed=int(moved), transcendentals=0)


def solution(mesh):
    placed = (P(("seq", "ch"), None, None), P("ch", "seq"), P("ch"))
    return jax.shard_map(
        body, mesh=mesh, in_specs=placed, out_specs=P("ch", "seq"), check_vma=False
    )
```

```python
import functools
import math

import jax
import jax.numpy as jnp
import numpy as np
from jax import lax
from jax.experimental import pallas as pl
from jax.experimental.pallas import tpu as pltpu
from jax.sharding import PartitionSpec as P

OCTAVES = 250.0
LOW_POWER = 125.0
EXPONENT_BITS = 8
EXPONENT_BIAS = 127.0
LANES = 128
ROW = 256
CHUNK = 16
HALF = 64
VMEM_BYTES = 20 * 1024 * 1024
SMALL_BYTES = 12 * 1024 * 1024
ALL_BYTES = 60 * 1024 * 1024


def split_first(values, axis):
    count = min(values.shape[axis], LANES if axis == values.ndim - 1 else EXPONENT_BITS)
    first = lax.slice_in_dim(values, 0, count, axis=axis)
    if count == values.shape[axis]:
        return first, None
    return first, lax.slice_in_dim(values, count, values.shape[axis], axis=axis)


def scale_of(peak):
    power = jnp.floor(jnp.log(jnp.maximum(peak, 1e-30)) * (1.0 / math.log(2.0))) + 1.0
    return jnp.clip(power, -100.0, 126.0)


def exponent_bits(power, shape, axis):
    place = lax.broadcasted_iota(jnp.int32, shape, axis).astype(jnp.float32)
    bits = (power + (EXPONENT_BIAS + 0.25)) * jnp.exp2(-1.0 - place)
    return jnp.where(bits - jnp.floor(bits) >= 0.5, 0.5, 0.0), place < EXPONENT_BITS


def encode(values, axis):
    peak = jnp.max(jnp.abs(values), axis=axis, keepdims=True)
    return encode_all([values], scale_of(peak), axis)[0]


def encode_all(blocks, power, axis):
    unit_share, codes, bits = jnp.exp2(-power), [], None
    for values in blocks:
        share = jnp.abs(values) * unit_share
        level = jnp.minimum(
            share * (2.0 * OCTAVES),
            jnp.minimum(share * OCTAVES + OCTAVES / 4, share * (OCTAVES / 2) + OCTAVES / 2),
        )
        level = jnp.minimum(level, OCTAVES + 1.0)
        first, rest = split_first(level, axis)
        bits = exponent_bits(power, first.shape, axis) if bits is None else bits
        odd, holds = bits
        marked = (jnp.floor(first * 64.0 - odd + 0.5) + odd) * (1.0 / 64.0)
        level = jnp.where(holds, marked, first)
        if rest is not None:
            level = jnp.concatenate([level, rest], axis=axis)
        octave = jnp.floor(level)
        unit = jnp.exp2(octave - LOW_POWER)
        code = jnp.where(values < 0.0, -unit, unit) * (level - octave + 1.0)
        codes.append(code.astype(jnp.bfloat16))
    return codes


def decode(code, axis, halvings=0):
    code = code.astype(jnp.float32)
    size = jnp.abs(code)
    octave = jnp.floor(jnp.log(size) * (1.0 / math.log(2.0)) + 0.002)
    level = octave + size * jnp.exp2(-octave)
    first, _ = split_first(level, axis)
    half = first * 64.0 + ((LOW_POWER - 1.0) * 64.0 + 0.25)
    place = lax.broadcasted_iota(jnp.int32, first.shape, axis).astype(jnp.float32)
    weight = jnp.where(place < EXPONENT_BITS, jnp.exp2(place), 0.0)
    held = jnp.where(half - jnp.floor(half) >= 0.5, weight, 0.0)
    scale = jnp.exp2(jnp.sum(held, axis=axis, keepdims=True) - (EXPONENT_BIAS + halvings))
    step = 0.5 / OCTAVES
    low = (LOW_POWER - 1.0) * step
    share = jnp.maximum(
        level * step + low,
        jnp.maximum(
            level * (2.0 * step) + (2.0 * low - 0.25), level * (4.0 * step) + (4.0 * low - 1.0)
        ),
    )
    return jnp.where(code < 0.0, -scale, scale) * share


def tables(blocks):
    n2 = np.arange(ROW)
    k1 = np.arange(blocks)
    main = 2.0 * np.pi * np.outer(n2, n2) / ROW
    twist = 2.0 * np.pi * np.outer(k1 + 0.25, n2) / (blocks * ROW)
    mix = 2.0 * np.pi * np.outer(k1 + 0.25, np.arange(blocks)) / blocks
    wave = np.concatenate([np.cos(main), np.sin(main)], axis=1).astype(np.float32)
    twist = np.stack([np.cos(twist), np.sin(twist)], axis=1).astype(np.float32)
    mix = np.stack([np.cos(mix), np.sin(mix)], axis=0).astype(np.float32)
    return wave, twist, mix


def folded(wave):
    half = np.concatenate([wave[:, :LANES], wave[:, ROW : ROW + LANES]], axis=1)
    half[:, LANES] = wave[:, LANES]
    parts = []
    for values in (half, half.T):
        high = values.astype(jnp.bfloat16)
        low = (values - high.astype(np.float32)).astype(jnp.bfloat16)
        parts.append(np.concatenate([high, low, high], axis=0))
    return parts


def put_split(ref, at, values):
    high = values.astype(jnp.bfloat16)
    ref[pl.ds(at, values.shape[0]), 0:ROW] = high
    ref[pl.ds(at, values.shape[0]), ROW : 2 * ROW] = high
    ref[pl.ds(at, values.shape[0]), 2 * ROW : 3 * ROW] = (
        values - high.astype(jnp.float32)
    ).astype(jnp.bfloat16)


def turned(value, steps):
    if steps == 0:
        return value
    re, im = value
    cos, sin = math.cos(math.pi * steps / 16), math.sin(math.pi * steps / 16)
    return re * cos - im * sin, im * cos + re * sin


def four_points(values, sign):
    (a_re, a_im), (b_re, b_im), (c_re, c_im), (d_re, d_im) = values
    sum_re, sum_im, gap_re, gap_im = a_re + c_re, a_im + c_im, a_re - c_re, a_im - c_im
    more_re, more_im = b_re + d_re, b_im + d_im
    side_re, side_im = sign * (d_im - b_im), sign * (b_re - d_re)
    return (
        (sum_re + more_re, sum_im + more_im),
        (gap_re + side_re, gap_im + side_im),
        (sum_re - more_re, sum_im - more_im),
        (gap_re - side_re, gap_im - side_im),
    )


def mix_forward(taken, twist_ref, at, ref):
    far = [value * math.sqrt(0.5) for value in taken[4:]]
    even = [turned((taken[n] + far[n], -far[n]), -n) for n in range(4)]
    odd = [turned((taken[n] - far[n], far[n]), -5 * n) for n in range(4)]
    for start, values in ((0, four_points(even, -1.0)), (1, four_points(odd, -1.0))):
        for index, (re, im) in enumerate(values):
            k = start + 2 * index
            cos_twist, sin_twist = twist_ref[k, 0:1, :], twist_ref[k, 1:2, :]
            put_split(ref, 2 * k * HALF + at, re * cos_twist + im * sin_twist)
            put_split(ref, (2 * k + 1) * HALF + at, im * cos_twist - re * sin_twist)


def mix_back(spectra, twist_ref):
    twisted = []
    for k, (re, im) in enumerate(spectra):
        cos_twist, sin_twist = twist_ref[k, 0:1, :], twist_ref[k, 1:2, :]
        twisted.append((re * cos_twist - im * sin_twist, im * cos_twist + re * sin_twist))
    even, odd = four_points(twisted[0::2], 1.0), four_points(twisted[1::2], 1.0)
    near, far = [], []
    for n in range(4):
        (even_re, even_im), (odd_re, odd_im) = turned(even[n], n), turned(odd[n], 5 * n)
        near.append(even_re + odd_re)
        far.append(((even_re - odd_re) - (even_im - odd_im)) * math.sqrt(0.5))
    return near + far


def spectrum_rows(waves_ref, k, at):
    re = waves_ref[pl.ds(2 * k * HALF + at, CHUNK), :]
    im = waves_ref[pl.ds((2 * k + 1) * HALF + at, CHUNK), :]
    return re, im


def send_kernel(streams_ref, gated_ref, keys, values, codes, in_sems, out_sems):
    groups, parts = gated_ref.shape[:2]
    per = groups // 2
    width = per * LANES
    arrivals = []
    for chunk in range(2 * parts):
        lanes = pl.ds(chunk * width, width)
        for stream, buffer in ((1, keys), (2, values)):
            copy = pltpu.make_async_copy(
                streams_ref.at[stream, :, lanes], buffer.at[chunk], in_sems.at[stream - 1, chunk]
            )
            copy.start()
            arrivals.append(copy)
    copies = []
    for chunk in range(2 * parts):
        for copy in arrivals[2 * chunk : 2 * chunk + 2]:
            copy.wait()
        part, first = chunk // 2, chunk % 2 * per
        for block in range(per):
            lanes = slice(block * LANES, (block + 1) * LANES)
            left = keys[chunk, :, lanes].astype(jnp.float32)
            right = values[chunk, :, lanes].astype(jnp.float32)
            codes[first + block, part] = encode(left * right, 0)
        place = (pl.ds(first, per), part)
        copy = pltpu.make_async_copy(codes.at[place], gated_ref.at[place], out_sems.at[chunk])
        copy.start()
        copies.append(copy)
    for copy in copies:
        copy.wait()


def query_kernel(streams_ref, *refs):
    query_refs, sems = refs[:-1], refs[-1]
    me = lax.axis_index("ch")
    wide = query_refs[0].shape[1]
    copies = []
    for turn, query_ref in enumerate(query_refs):
        lanes = pl.ds(pl.multiple_of((me ^ turn) * wide, wide), wide)
        copy = pltpu.make_async_copy(streams_ref.at[0, :, lanes], query_ref, sems.at[turn])
        copy.start()
        copies.append(copy)
    for copy in copies:
        copy.wait()


def taps_kernel(taps_ref, skip_ref, *code_refs):
    me = lax.axis_index("seq")
    first = (me == 0).astype(jnp.float32)
    row = lax.broadcasted_iota(jnp.int32, (LANES, LANES), 0)
    lane = lax.broadcasted_iota(jnp.int32, (LANES, LANES), 1)
    for turn, code_ref in enumerate(code_refs):
        block = me ^ turn
        gains = jnp.broadcast_to(skip_ref[pl.ds(block, 1), :], (LANES, LANES))
        gain = jnp.sum(jnp.where(row == lane, gains, 0.0), axis=1, keepdims=True) * first
        start = taps_ref[block, :, :LANES] + jnp.where(lane == 0, gain, 0.0)
        taps = jnp.concatenate([start, taps_ref[block, :, LANES:]], axis=1)
        code_ref[...] = encode(taps, 1)


def first_lane():
    return lax.broadcasted_iota(jnp.int32, (CHUNK, LANES), 1) == 0


def combined(waves_ref, k, at):
    re, im = spectrum_rows(waves_ref, k, at)
    first = first_lane()
    re_cos, re_sin, im_cos, im_sin = re[:, :LANES], re[:, LANES:], im[:, :LANES], im[:, LANES:]
    near = (
        re_cos + jnp.where(first, 0.0, im_sin),
        im_cos - jnp.where(first, 0.0, re_sin),
    )
    far = (
        jnp.where(first, re_sin, re_cos - im_sin),
        jnp.where(first, im_sin, im_cos + re_sin),
    )
    return [jnp.concatenate([left, right], axis=1) for left, right in zip(near, far)]


def put_folded(ref, k, at, re, im):
    first = first_lane()
    near_re, far_re, near_im, far_im = re[:, :LANES], re[:, LANES:], im[:, :LANES], im[:, LANES:]
    back_re = [
        jnp.where(first, near_re, near_re + far_re),
        jnp.where(first, far_re, far_im - near_im),
    ]
    back_im = [
        jnp.where(first, near_im, near_im + far_im),
        jnp.where(first, far_im, near_re - far_re),
    ]
    put_split(ref, 2 * k * HALF + at, jnp.concatenate(back_re, axis=1))
    put_split(ref, (2 * k + 1) * HALF + at, jnp.concatenate(back_im, axis=1))


def stage(wave_ref, source, target, work, half):
    if source is not None:
        target[...] = jnp.dot(source[...], wave_ref[...], preferred_element_type=jnp.float32)
    for chunk in range(HALF // CHUNK):
        work(half, chunk * CHUNK)


def gated_spectrum_kernel(gated_ref, wave_ref, twist_ref, out_ref, u, *scratch):
    blocks = u.shape[0]
    rows, waves = scratch[0:2], scratch[2:4]
    parts = ROW // gated_ref.shape[1]

    def unpack(block, _):
        pieces = [decode(gated_ref[block * parts + part], 0) for part in range(parts)]
        u[block] = jnp.transpose(jnp.concatenate(pieces, axis=0))
        return 0

    def forward(half, at):
        start = pl.ds(half * HALF + at, CHUNK)
        mix_forward([u[n1, start, :] for n1 in range(blocks)], twist_ref, at, rows[half])

    def finish(half, at):
        for k in range(blocks):
            re, im = combined(waves[half], k, at)
            out_ref[half, k, 0, pl.ds(at, CHUNK), :] = re
            out_ref[half, k, 1, pl.ds(at, CHUNK), :] = im

    lax.fori_loop(0, blocks, unpack, 0)
    stage(None, None, None, forward, 0)
    stage(wave_ref, rows[0], waves[0], forward, 1)
    stage(wave_ref, rows[1], waves[1], finish, 0)
    stage(None, None, None, finish, 1)


def conv_kernel(gated_ref, *refs):
    blocks = gated_ref.shape[1]
    wave_ref, back_wave_ref, twist_ref, out_ref, codes, out, sems, *scratch = refs[blocks:]
    rows, waves = scratch[0:2], scratch[2:4]
    scale = math.log2(blocks * ROW)
    me = lax.axis_index("seq")
    for turn, code_ref in enumerate(refs[:blocks]):
        codes[me ^ turn] = code_ref[...]

    def forward(half, at):
        start = pl.ds(half * HALF + at, CHUNK)
        taken = [decode(codes[n1, start, :], 1, scale) for n1 in range(blocks)]
        mix_forward(taken, twist_ref, at, rows[half])

    def product(half, at):
        for k in range(blocks):
            re, im = combined(waves[half], k, at)
            gated_re = gated_ref[half, k, 0, pl.ds(at, CHUNK), :]
            gated_im = gated_ref[half, k, 1, pl.ds(at, CHUNK), :]
            product_re, product_im = re * gated_re - im * gated_im, re * gated_im + im * gated_re
            put_folded(rows[half], k, at, product_re, product_im)

    def back(half, at):
        spectra = [spectrum_rows(waves[half], k, at) for k in range(blocks)]
        start = pl.ds(half * HALF + at, CHUNK)
        totals = mix_back(spectra, twist_ref)
        sizes = [jnp.abs(total) for total in totals]
        peak = jnp.max(functools.reduce(jnp.maximum, sizes), axis=1, keepdims=True)
        for n1, code in enumerate(encode_all(totals, scale_of(peak), 1)):
            out[n1, start, :] = code

    def out_copy(half):
        start = pl.ds(half * HALF, HALF)
        return pltpu.make_async_copy(out.at[:, start, :], out_ref.at[:, start, :], sems.at[half])

    stage(None, None, None, forward, 0)
    stage(wave_ref, rows[0], waves[0], forward, 1)
    stage(wave_ref, rows[1], waves[1], product, 0)
    stage(back_wave_ref, rows[0], waves[0], product, 1)
    stage(back_wave_ref, rows[1], waves[1], back, 0)
    out_copy(0).start()
    stage(None, None, None, back, 1)
    out_copy(1).start()
    out_copy(0).wait()
    out_copy(1).wait()


def turn_kernel(*refs):
    query_refs, out_ref, whole = refs[:-2], refs[-2], refs[-1]
    me = lax.axis_index("ch")
    held = query_refs[0].shape[0]
    for turn, query_ref in enumerate(query_refs):
        at = pl.multiple_of((me ^ turn) * held, held)
        whole[pl.ds(at, held), :] = query_ref[...].astype(jnp.float32)
    out_ref[...] = jnp.transpose(whole[...]).astype(jnp.bfloat16)


def mix_kernel(query_ref, conv_ref, out_ref, mixed, sems):
    copies = []
    for block in range(conv_ref.shape[0]):
        at = pl.ds(block * LANES, LANES)
        queries = query_ref[at, :].astype(jnp.float32)
        mixed[at, :] = (queries * decode(conv_ref[block], 1)).astype(jnp.bfloat16)
        copy = pltpu.make_async_copy(mixed.at[at], out_ref.at[at], sems.at[block])
        copy.start()
        copies.append(copy)
    for copy in copies:
        copy.wait()


def plain_conv(gated, taps):
    blocks = gated.shape[0]
    wave, twist, mix = tables(blocks)
    cos_twist, sin_twist = twist[:, 0][:, None, :], twist[:, 1][:, None, :]
    dot = functools.partial(jnp.einsum, precision=lax.Precision.HIGHEST)

    def forward(values):
        re = dot("ncm,kn->kcm", values, mix[0])
        im = -dot("ncm,kn->kcm", values, mix[1])
        re, im = re * cos_twist + im * sin_twist, im * cos_twist - re * sin_twist
        re, im = dot("kcm,mq->kcq", re, wave), dot("kcm,mq->kcq", im, wave)
        return re[..., :ROW] + im[..., ROW:], im[..., :ROW] - re[..., ROW:]

    u_re, u_im = forward(gated)
    h_re, h_im = forward(taps)
    re = dot("kcm,mq->kcq", u_re * h_re - u_im * h_im, wave)
    im = dot("kcm,mq->kcq", u_re * h_im + u_im * h_re, wave)
    re, im = re[..., :ROW] - im[..., ROW:], im[..., :ROW] + re[..., ROW:]
    re, im = re * cos_twist - im * sin_twist, im * cos_twist + re * sin_twist
    total = dot("kcm,kn->ncm", re, mix[0]) - dot("kcm,kn->ncm", im, mix[1])
    return total * (1.0 / (blocks * ROW))


def scatter(blocks, axis):
    count = len(blocks)
    return [
        lax.ppermute(block, axis, [(i, i ^ turn) for i in range(count)]) if turn else block
        for turn, block in enumerate(blocks)
    ]


def body(streams, filter_taps, skip_gain):
    groups, parts = lax.axis_size("seq"), lax.axis_size("ch")
    held, _, channels = streams.shape
    wide = channels // parts
    own = wide // groups
    blocks = filter_taps.shape[1] * groups // ROW
    streams = jnp.transpose(streams, (1, 0, 2))
    fits = blocks == 8 and own == LANES and filter_taps.shape[1] == ROW and ROW % held == 0 and groups % 4 == 0
    fits = fits and groups & (groups - 1) == 0 and parts & (parts - 1) == 0
    small = pltpu.CompilerParams(vmem_limit_bytes=SMALL_BYTES)
    if fits:
        far = pl.BlockSpec(memory_space=pl.ANY)
        coded = (groups, parts, held, own)
        stream = pltpu.VMEM((2 * parts, held, wide // 2), jnp.bfloat16)
        gated = pl.pallas_call(
            send_kernel,
            in_specs=[far],
            out_specs=far,
            out_shape=jax.ShapeDtypeStruct(coded, jnp.bfloat16),
            scratch_shapes=[
                stream,
                stream,
                pltpu.VMEM(coded, jnp.bfloat16),
                pltpu.SemaphoreType.DMA((2, 2 * parts)),
                pltpu.SemaphoreType.DMA((2 * parts,)),
            ],
            compiler_params=pltpu.CompilerParams(vmem_limit_bytes=ALL_BYTES),
            cost_estimate=cost(2**25, 2**23),
            name="encode_gated",
        )(streams)
        queries = pl.pallas_call(
            query_kernel,
            in_specs=[far],
            out_specs=[far] * parts,
            out_shape=[jax.ShapeDtypeStruct((held, wide), jnp.bfloat16)] * parts,
            scratch_shapes=[pltpu.SemaphoreType.DMA((parts,))],
            compiler_params=small,
            cost_estimate=cost(2**10, 2**20),
            name="send_queries",
        )(streams)
        taps = pl.pallas_call(
            taps_kernel,
            out_shape=[jax.ShapeDtypeStruct((own, ROW), jnp.bfloat16)] * groups,
            compiler_params=small,
            cost_estimate=cost(2**25, 2**23),
            name="encode_taps",
        )(filter_taps.reshape(groups, own, ROW), skip_gain.reshape(groups, own))
    else:
        gated = encode(streams[1].astype(jnp.float32) * streams[2].astype(jnp.float32), 0)
        gated = jnp.transpose(gated.reshape(held, parts, groups, own), (2, 1, 0, 3))
        queries = jnp.transpose(streams[0].reshape(held, parts, wide), (1, 0, 2))
        first = lax.axis_index("seq") == 0
        taps = filter_taps.at[:, 0].add(jnp.where(first, skip_gain, 0.0))
        taps = encode(taps, 1).reshape(groups, own, -1)
    exchange = functools.partial(lax.all_to_all, split_axis=0, concat_axis=0, tiled=True)
    gated = gated.reshape(groups * parts, held, own)
    if fits:
        taps = scatter(taps, "seq")
        gated = exchange(gated, ("seq", "ch"))
        queries = scatter(queries, "ch")
    else:
        taps = exchange(taps, "seq")
        gated = exchange(gated, ("seq", "ch"))
        queries = exchange(queries, "ch").reshape(parts * held, wide)
    if fits:
        wave, twist, _ = tables(blocks)
        wave, back_wave = folded(wave)
        scratch = [pltpu.VMEM((blocks * 2 * HALF, 3 * ROW), jnp.bfloat16)] * 2
        scratch += [pltpu.VMEM((blocks * 2 * HALF, ROW), jnp.float32)] * 2
        large = pltpu.CompilerParams(vmem_limit_bytes=VMEM_BYTES)
        gated = pl.pallas_call(
            gated_spectrum_kernel,
            out_shape=jax.ShapeDtypeStruct((2, blocks, 2, HALF, ROW), jnp.float32),
            scratch_shapes=[pltpu.VMEM((blocks, own, ROW), jnp.float32)] + scratch,
            compiler_params=large,
            cost_estimate=cost(2**32, 2**24),
            name="gated_spectrum",
        )(gated, wave, twist)
        convolved = pl.pallas_call(
            conv_kernel,
            out_shape=jax.ShapeDtypeStruct((blocks, own, ROW), jnp.bfloat16),
            in_specs=[pl.BlockSpec(memory_space=pltpu.VMEM)] * (groups + 4),
            out_specs=far,
            scratch_shapes=[
                pltpu.VMEM((blocks, own, ROW), jnp.bfloat16),
                pltpu.VMEM((blocks, own, ROW), jnp.bfloat16),
                pltpu.SemaphoreType.DMA((2,)),
            ]
            + scratch,
            compiler_params=large,
            cost_estimate=cost(2**32, 2**24),
            name="convolve",
        )(gated, *taps, wave, back_wave, twist)
    else:
        gated = decode(gated, 1).reshape(blocks, ROW, own)
        taps = jnp.transpose(decode(taps, 2), (1, 0, 2)).reshape(own, blocks, ROW)
        convolved = plain_conv(jnp.transpose(gated, (0, 2, 1)), jnp.transpose(taps, (1, 0, 2)))
        convolved = jnp.transpose(convolved, (1, 0, 2)).reshape(own, groups, -1)
        convolved = encode(jnp.transpose(convolved, (1, 0, 2)), 2)
    convolved = exchange(convolved, "seq")
    if fits:
        queries = pl.pallas_call(
            turn_kernel,
            out_shape=jax.ShapeDtypeStruct((wide, ROW), jnp.bfloat16),
            scratch_shapes=[pltpu.VMEM((ROW, wide), jnp.float32)],
            compiler_params=small,
            cost_estimate=cost(2**20, 2**21),
            name="turn_queries",
        )(*queries)
        return pl.pallas_call(
            mix_kernel,
            out_specs=far,
            out_shape=jax.ShapeDtypeStruct((wide, ROW), jnp.bfloat16),
            scratch_shapes=[
                pltpu.VMEM((wide, ROW), jnp.bfloat16),
                pltpu.SemaphoreType.DMA((groups,)),
            ],
            compiler_params=small,
            name="mix_out",
        )(queries, convolved)
    queries = jnp.transpose(queries.astype(jnp.float32))
    return (queries * decode(convolved, 2).reshape(wide, -1)).astype(jnp.bfloat16)


def cost(flops, moved):
    return pl.CostEstimate(flops=int(flops), bytes_accessed=int(moved), transcendentals=0)


def solution(mesh):
    placed = (P(("seq", "ch"), None, None), P("ch", "seq"), P("ch"))
    return jax.shard_map(
        body, mesh=mesh, in_specs=placed, out_specs=P("ch", "seq"), check_vma=False
    )
```

```python
import functools
import math

import jax
import jax.numpy as jnp
import numpy as np
from jax import lax
from jax.experimental import pallas as pl
from jax.experimental.pallas import tpu as pltpu
from jax.sharding import PartitionSpec as P

OCTAVES = 250.0
LOW_POWER = 125.0
EXPONENT_BITS = 8
EXPONENT_BIAS = 127.0
LANES = 128
ROW = 256
CHUNK = 16
HALF = 64
VMEM_BYTES = 20 * 1024 * 1024
SMALL_BYTES = 12 * 1024 * 1024
ALL_BYTES = 60 * 1024 * 1024


def split_first(values, axis):
    count = min(values.shape[axis], LANES if axis == values.ndim - 1 else EXPONENT_BITS)
    first = lax.slice_in_dim(values, 0, count, axis=axis)
    if count == values.shape[axis]:
        return first, None
    return first, lax.slice_in_dim(values, count, values.shape[axis], axis=axis)


def scale_of(peak):
    power = jnp.floor(jnp.log(jnp.maximum(peak, 1e-30)) * (1.0 / math.log(2.0))) + 1.0
    return jnp.clip(power, -100.0, 126.0)


def exponent_bits(power, shape, axis):
    place = lax.broadcasted_iota(jnp.int32, shape, axis).astype(jnp.float32)
    bits = (power + (EXPONENT_BIAS + 0.25)) * jnp.exp2(-1.0 - place)
    return jnp.where(bits - jnp.floor(bits) >= 0.5, 0.5, 0.0), place < EXPONENT_BITS


def encode(values, axis):
    peak = jnp.max(jnp.abs(values), axis=axis, keepdims=True)
    return encode_all([values], scale_of(peak), axis)[0]


def encode_all(blocks, power, axis):
    unit_share, codes, bits = jnp.exp2(-power), [], None
    for values in blocks:
        share = jnp.abs(values) * unit_share
        level = jnp.minimum(
            share * (2.0 * OCTAVES),
            jnp.minimum(share * OCTAVES + OCTAVES / 4, share * (OCTAVES / 2) + OCTAVES / 2),
        )
        level = jnp.minimum(level, OCTAVES + 1.0)
        first, rest = split_first(level, axis)
        bits = exponent_bits(power, first.shape, axis) if bits is None else bits
        odd, holds = bits
        marked = (jnp.floor(first * 64.0 - odd + 0.5) + odd) * (1.0 / 64.0)
        level = jnp.where(holds, marked, first)
        if rest is not None:
            level = jnp.concatenate([level, rest], axis=axis)
        octave = jnp.floor(level)
        unit = jnp.exp2(octave - LOW_POWER)
        code = jnp.where(values < 0.0, -unit, unit) * (level - octave + 1.0)
        codes.append(code.astype(jnp.bfloat16))
    return codes


def decode(code, axis, halvings=0):
    code = code.astype(jnp.float32)
    size = jnp.abs(code)
    octave = jnp.floor(jnp.log(size) * (1.0 / math.log(2.0)) + 0.002)
    level = octave + size * jnp.exp2(-octave)
    first, _ = split_first(level, axis)
    half = first * 64.0 + ((LOW_POWER - 1.0) * 64.0 + 0.25)
    place = lax.broadcasted_iota(jnp.int32, first.shape, axis).astype(jnp.float32)
    weight = jnp.where(place < EXPONENT_BITS, jnp.exp2(place), 0.0)
    held = jnp.where(half - jnp.floor(half) >= 0.5, weight, 0.0)
    scale = jnp.exp2(jnp.sum(held, axis=axis, keepdims=True) - (EXPONENT_BIAS + halvings))
    step = 0.5 / OCTAVES
    low = (LOW_POWER - 1.0) * step
    share = jnp.maximum(
        level * step + low,
        jnp.maximum(
            level * (2.0 * step) + (2.0 * low - 0.25), level * (4.0 * step) + (4.0 * low - 1.0)
        ),
    )
    return jnp.where(code < 0.0, -scale, scale) * share


def tables(blocks):
    n2 = np.arange(ROW)
    k1 = np.arange(blocks)
    main = 2.0 * np.pi * np.outer(n2, n2 + 0.5) / ROW
    twist = 2.0 * np.pi * np.outer(k1 + 0.25 - blocks / 2, n2) / (blocks * ROW)
    mix = 2.0 * np.pi * np.outer(k1 + 0.25, np.arange(blocks)) / blocks
    wave = np.stack([np.cos(main), np.sin(main)]).astype(np.float32)
    twist = np.stack([np.cos(twist), np.sin(twist)], axis=1).astype(np.float32)
    mix = np.stack([np.cos(mix), np.sin(mix)], axis=0).astype(np.float32)
    return wave, twist, mix


def folded(wave):
    half = np.concatenate([wave[0, :, :LANES], wave[1, :, :LANES]], axis=1)
    parts = []
    for values in (half, half.T):
        high = values.astype(jnp.bfloat16)
        low = (values - high.astype(np.float32)).astype(jnp.bfloat16)
        parts.append(np.concatenate([high, low, high], axis=0))
    return parts


def put_split(ref, at, values):
    high = values.astype(jnp.bfloat16)
    ref[pl.ds(at, values.shape[0]), 0:ROW] = high
    ref[pl.ds(at, values.shape[0]), ROW : 2 * ROW] = high
    ref[pl.ds(at, values.shape[0]), 2 * ROW : 3 * ROW] = (
        values - high.astype(jnp.float32)
    ).astype(jnp.bfloat16)


def turned(value, steps):
    if steps == 0:
        return value
    re, im = value
    cos, sin = math.cos(math.pi * steps / 16), math.sin(math.pi * steps / 16)
    return re * cos - im * sin, im * cos + re * sin


def four_points(values, sign):
    (a_re, a_im), (b_re, b_im), (c_re, c_im), (d_re, d_im) = values
    sum_re, sum_im, gap_re, gap_im = a_re + c_re, a_im + c_im, a_re - c_re, a_im - c_im
    more_re, more_im = b_re + d_re, b_im + d_im
    side_re, side_im = sign * (d_im - b_im), sign * (b_re - d_re)
    return (
        (sum_re + more_re, sum_im + more_im),
        (gap_re + side_re, gap_im + side_im),
        (sum_re - more_re, sum_im - more_im),
        (gap_re - side_re, gap_im - side_im),
    )


def row_of(ref, k, part, at):
    return (2 * k + part) * HALF + at


def mix_forward(taken, twist_ref, at, ref):
    far = [value * math.sqrt(0.5) for value in taken[4:]]
    even = [turned((taken[n] + far[n], -far[n]), -n) for n in range(4)]
    odd = [turned((taken[n] - far[n], far[n]), -5 * n) for n in range(4)]
    for start, values in ((0, four_points(even, -1.0)), (1, four_points(odd, -1.0))):
        for index, (re, im) in enumerate(values):
            k = start + 2 * index
            cos_twist, sin_twist = twist_ref[k, 0:1, :], twist_ref[k, 1:2, :]
            put_split(ref, 2 * k * HALF + at, re * cos_twist + im * sin_twist)
            put_split(ref, (2 * k + 1) * HALF + at, im * cos_twist - re * sin_twist)


def mix_back(spectra, twist_ref):
    twisted = []
    for k, (re, im) in enumerate(spectra):
        cos_twist, sin_twist = twist_ref[k, 0:1, :], twist_ref[k, 1:2, :]
        twisted.append((re * cos_twist - im * sin_twist, im * cos_twist + re * sin_twist))
    even, odd = four_points(twisted[0::2], 1.0), four_points(twisted[1::2], 1.0)
    near, far = [], []
    for n in range(4):
        (even_re, even_im), (odd_re, odd_im) = turned(even[n], n), turned(odd[n], 5 * n)
        near.append(even_re + odd_re)
        far.append(((even_re - odd_re) - (even_im - odd_im)) * math.sqrt(0.5))
    return near + far


def spectrum_rows(waves_ref, k, at):
    re = waves_ref[pl.ds(2 * k * HALF + at, CHUNK), :]
    im = waves_ref[pl.ds((2 * k + 1) * HALF + at, CHUNK), :]
    return re, im


def send_kernel(streams_ref, gated_ref, keys, values, codes, in_sems, out_sems):
    groups, parts = gated_ref.shape[:2]
    per = groups // 2
    width = per * LANES
    arrivals = []
    for chunk in range(2 * parts):
        lanes = pl.ds(chunk * width, width)
        for stream, buffer in ((1, keys), (2, values)):
            copy = pltpu.make_async_copy(
                streams_ref.at[stream, :, lanes], buffer.at[chunk], in_sems.at[stream - 1, chunk]
            )
            copy.start()
            arrivals.append(copy)
    copies = []
    for chunk in range(2 * parts):
        for copy in arrivals[2 * chunk : 2 * chunk + 2]:
            copy.wait()
        part, first = chunk // 2, chunk % 2 * per
        for block in range(per):
            lanes = slice(block * LANES, (block + 1) * LANES)
            left = keys[chunk, :, lanes].astype(jnp.float32)
            right = values[chunk, :, lanes].astype(jnp.float32)
            codes[first + block, part] = encode(left * right, 0)
        place = (pl.ds(first, per), part)
        copy = pltpu.make_async_copy(codes.at[place], gated_ref.at[place], out_sems.at[chunk])
        copy.start()
        copies.append(copy)
    for copy in copies:
        copy.wait()


def query_kernel(streams_ref, *refs):
    query_refs, sems = refs[:-1], refs[-1]
    me = lax.axis_index("ch")
    wide = query_refs[0].shape[1]
    copies = []
    for turn, query_ref in enumerate(query_refs):
        lanes = pl.ds(pl.multiple_of((me ^ turn) * wide, wide), wide)
        copy = pltpu.make_async_copy(streams_ref.at[0, :, lanes], query_ref, sems.at[turn])
        copy.start()
        copies.append(copy)
    for copy in copies:
        copy.wait()


def taps_kernel(taps_ref, skip_ref, *code_refs):
    me = lax.axis_index("seq")
    first = (me == 0).astype(jnp.float32)
    row = lax.broadcasted_iota(jnp.int32, (LANES, LANES), 0)
    lane = lax.broadcasted_iota(jnp.int32, (LANES, LANES), 1)
    for turn, code_ref in enumerate(code_refs):
        block = me ^ turn
        gains = jnp.broadcast_to(skip_ref[pl.ds(block, 1), :], (LANES, LANES))
        gain = jnp.sum(jnp.where(row == lane, gains, 0.0), axis=1, keepdims=True) * first
        start = taps_ref[block, :, :LANES] + jnp.where(lane == 0, gain, 0.0)
        taps = jnp.concatenate([start, taps_ref[block, :, LANES:]], axis=1)
        code_ref[...] = encode(taps, 1)


def combined(waves_ref, k, at):
    re, im = spectrum_rows(waves_ref, k, at)
    re_cos, re_sin, im_cos, im_sin = re[:, :LANES], re[:, LANES:], im[:, :LANES], im[:, LANES:]
    return (
        jnp.concatenate([re_cos + im_sin, re_cos - im_sin], axis=1),
        jnp.concatenate([im_cos - re_sin, im_cos + re_sin], axis=1),
    )


def put_folded(ref, k, at, re, im):
    near_re, far_re, near_im, far_im = re[:, :LANES], re[:, LANES:], im[:, :LANES], im[:, LANES:]
    back_re = jnp.concatenate([near_re + far_re, far_im - near_im], axis=1)
    back_im = jnp.concatenate([near_im + far_im, near_re - far_re], axis=1)
    put_split(ref, row_of(ref, k, 0, at), back_re)
    put_split(ref, row_of(ref, k, 1, at), back_im)


def stage(wave_ref, source, target, work, half):
    if source is not None:
        target[...] = jnp.dot(source[...], wave_ref[...], preferred_element_type=jnp.float32)
    for chunk in range(HALF // CHUNK):
        work(half, chunk * CHUNK)


def gated_spectrum_kernel(gated_ref, wave_ref, twist_ref, out_ref, u, *scratch):
    blocks = u.shape[0]
    rows, waves = scratch[0:2], scratch[2:4]
    parts = ROW // gated_ref.shape[1]

    def unpack(block, _):
        pieces = [decode(gated_ref[block * parts + part], 0) for part in range(parts)]
        u[block] = jnp.transpose(jnp.concatenate(pieces, axis=0))
        return 0

    def forward(half, at):
        start = pl.ds(half * HALF + at, CHUNK)
        mix_forward([u[n1, start, :] for n1 in range(blocks)], twist_ref, at, rows[half])

    def finish(half, at):
        for k in range(blocks):
            re, im = combined(waves[half], k, at)
            out_ref[half, k, 0, pl.ds(at, CHUNK), :] = re
            out_ref[half, k, 1, pl.ds(at, CHUNK), :] = im

    lax.fori_loop(0, blocks, unpack, 0)
    stage(None, None, None, forward, 0)
    stage(wave_ref, rows[0], waves[0], forward, 1)
    stage(wave_ref, rows[1], waves[1], finish, 0)
    stage(None, None, None, finish, 1)


def conv_kernel(gated_ref, *refs):
    blocks = gated_ref.shape[1]
    wave_ref, back_wave_ref, twist_ref, out_ref, codes, out, sems, *scratch = refs[blocks:]
    rows, waves = scratch[0:2], scratch[2:4]
    scale = math.log2(blocks * ROW)
    me = lax.axis_index("seq")
    for turn, code_ref in enumerate(refs[:blocks]):
        codes[me ^ turn] = code_ref[...]

    def forward(half, at):
        start = pl.ds(half * HALF + at, CHUNK)
        taken = [decode(codes[n1, start, :], 1, scale) for n1 in range(blocks)]
        mix_forward(taken, twist_ref, at, rows[half])

    def product(half, at):
        for k in range(blocks):
            re, im = combined(waves[half], k, at)
            gated_re = gated_ref[half, k, 0, pl.ds(at, CHUNK), :]
            gated_im = gated_ref[half, k, 1, pl.ds(at, CHUNK), :]
            product_re, product_im = re * gated_re - im * gated_im, re * gated_im + im * gated_re
            put_folded(rows[half], k, at, product_re, product_im)

    def back(half, at):
        spectra = [spectrum_rows(waves[half], k, at) for k in range(blocks)]
        start = pl.ds(half * HALF + at, CHUNK)
        totals = mix_back(spectra, twist_ref)
        sizes = [jnp.abs(total) for total in totals]
        peak = jnp.max(functools.reduce(jnp.maximum, sizes), axis=1, keepdims=True)
        for n1, code in enumerate(encode_all(totals, scale_of(peak), 1)):
            out[n1, start, :] = code

    def out_copy(half):
        start = pl.ds(half * HALF, HALF)
        return pltpu.make_async_copy(out.at[:, start, :], out_ref.at[:, start, :], sems.at[half])

    stage(None, None, None, forward, 0)
    stage(wave_ref, rows[0], waves[0], forward, 1)
    stage(wave_ref, rows[1], waves[1], product, 0)
    stage(back_wave_ref, rows[0], waves[0], product, 1)
    stage(back_wave_ref, rows[1], waves[1], back, 0)
    out_copy(0).start()
    stage(None, None, None, back, 1)
    out_copy(1).start()
    out_copy(0).wait()
    out_copy(1).wait()


def turn_kernel(*refs):
    query_refs, out_ref, whole = refs[:-2], refs[-2], refs[-1]
    me = lax.axis_index("ch")
    held = query_refs[0].shape[0]
    for turn, query_ref in enumerate(query_refs):
        at = pl.multiple_of((me ^ turn) * held, held)
        whole[pl.ds(at, held), :] = query_ref[...].astype(jnp.float32)
    out_ref[...] = jnp.transpose(whole[...]).astype(jnp.bfloat16)


def mix_kernel(query_ref, conv_ref, out_ref, mixed, sems):
    copies = []
    for block in range(conv_ref.shape[0]):
        at = pl.ds(block * LANES, LANES)
        queries = query_ref[at, :].astype(jnp.float32)
        mixed[at, :] = (queries * decode(conv_ref[block], 1)).astype(jnp.bfloat16)
        copy = pltpu.make_async_copy(mixed.at[at], out_ref.at[at], sems.at[block])
        copy.start()
        copies.append(copy)
    for copy in copies:
        copy.wait()


def plain_conv(gated, taps):
    blocks = gated.shape[0]
    (cos, sin), twist, mix = tables(blocks)
    cos_twist, sin_twist = twist[:, 0][:, None, :], twist[:, 1][:, None, :]
    dot = functools.partial(jnp.einsum, precision=lax.Precision.HIGHEST)

    def forward(values):
        re = dot("ncm,kn->kcm", values, mix[0])
        im = -dot("ncm,kn->kcm", values, mix[1])
        re, im = re * cos_twist + im * sin_twist, im * cos_twist - re * sin_twist
        return (
            dot("kcm,mq->kcq", re, cos) + dot("kcm,mq->kcq", im, sin),
            dot("kcm,mq->kcq", im, cos) - dot("kcm,mq->kcq", re, sin),
        )

    u_re, u_im = forward(gated)
    h_re, h_im = forward(taps)
    re, im = u_re * h_re - u_im * h_im, u_re * h_im + u_im * h_re
    re, im = (
        dot("kcq,mq->kcm", re, cos) - dot("kcq,mq->kcm", im, sin),
        dot("kcq,mq->kcm", im, cos) + dot("kcq,mq->kcm", re, sin),
    )
    re, im = re * cos_twist - im * sin_twist, im * cos_twist + re * sin_twist
    total = dot("kcm,kn->ncm", re, mix[0]) - dot("kcm,kn->ncm", im, mix[1])
    return total * (1.0 / (blocks * ROW))


def scatter(blocks, axis):
    count = len(blocks)
    return [
        lax.ppermute(block, axis, [(i, i ^ turn) for i in range(count)]) if turn else block
        for turn, block in enumerate(blocks)
    ]


def body(streams, filter_taps, skip_gain):
    groups, parts = lax.axis_size("seq"), lax.axis_size("ch")
    held, _, channels = streams.shape
    wide = channels // parts
    own = wide // groups
    blocks = filter_taps.shape[1] * groups // ROW
    streams = jnp.transpose(streams, (1, 0, 2))
    fits = blocks == 8 and own == LANES and filter_taps.shape[1] == ROW and ROW % held == 0 and groups % 4 == 0
    fits = fits and groups & (groups - 1) == 0 and parts & (parts - 1) == 0
    small = pltpu.CompilerParams(vmem_limit_bytes=SMALL_BYTES)
    if fits:
        far = pl.BlockSpec(memory_space=pl.ANY)
        coded = (groups, parts, held, own)
        stream = pltpu.VMEM((2 * parts, held, wide // 2), jnp.bfloat16)
        gated = pl.pallas_call(
            send_kernel,
            in_specs=[far],
            out_specs=far,
            out_shape=jax.ShapeDtypeStruct(coded, jnp.bfloat16),
            scratch_shapes=[
                stream,
                stream,
                pltpu.VMEM(coded, jnp.bfloat16),
                pltpu.SemaphoreType.DMA((2, 2 * parts)),
                pltpu.SemaphoreType.DMA((2 * parts,)),
            ],
            compiler_params=pltpu.CompilerParams(vmem_limit_bytes=ALL_BYTES),
            cost_estimate=cost(2**25, 2**23),
            name="encode_gated",
        )(streams)
        queries = pl.pallas_call(
            query_kernel,
            in_specs=[far],
            out_specs=[far] * parts,
            out_shape=[jax.ShapeDtypeStruct((held, wide), jnp.bfloat16)] * parts,
            scratch_shapes=[pltpu.SemaphoreType.DMA((parts,))],
            compiler_params=small,
            cost_estimate=cost(2**10, 2**20),
            name="send_queries",
        )(streams)
        taps = pl.pallas_call(
            taps_kernel,
            out_shape=[jax.ShapeDtypeStruct((own, ROW), jnp.bfloat16)] * groups,
            compiler_params=small,
            cost_estimate=cost(2**25, 2**23),
            name="encode_taps",
        )(filter_taps.reshape(groups, own, ROW), skip_gain.reshape(groups, own))
    else:
        gated = encode(streams[1].astype(jnp.float32) * streams[2].astype(jnp.float32), 0)
        gated = jnp.transpose(gated.reshape(held, parts, groups, own), (2, 1, 0, 3))
        queries = jnp.transpose(streams[0].reshape(held, parts, wide), (1, 0, 2))
        first = lax.axis_index("seq") == 0
        taps = filter_taps.at[:, 0].add(jnp.where(first, skip_gain, 0.0))
        taps = encode(taps, 1).reshape(groups, own, -1)
    exchange = functools.partial(lax.all_to_all, split_axis=0, concat_axis=0, tiled=True)
    gated = gated.reshape(groups * parts, held, own)
    if fits:
        taps = scatter(taps, "seq")
        gated = exchange(gated, ("seq", "ch"))
        queries = scatter(queries, "ch")
    else:
        taps = exchange(taps, "seq")
        gated = exchange(gated, ("seq", "ch"))
        queries = exchange(queries, "ch").reshape(parts * held, wide)
    if fits:
        wave, twist, _ = tables(blocks)
        wave, back_wave = folded(wave)
        scratch = [pltpu.VMEM((blocks * 2 * HALF, 3 * ROW), jnp.bfloat16)] * 2
        scratch += [pltpu.VMEM((blocks * 2 * HALF, ROW), jnp.float32)] * 2
        large = pltpu.CompilerParams(vmem_limit_bytes=VMEM_BYTES)
        gated = pl.pallas_call(
            gated_spectrum_kernel,
            out_shape=jax.ShapeDtypeStruct((2, blocks, 2, HALF, ROW), jnp.float32),
            scratch_shapes=[pltpu.VMEM((blocks, own, ROW), jnp.float32)] + scratch,
            compiler_params=large,
            cost_estimate=cost(2**32, 2**24),
            name="gated_spectrum",
        )(gated, wave, twist)
        convolved = pl.pallas_call(
            conv_kernel,
            out_shape=jax.ShapeDtypeStruct((blocks, own, ROW), jnp.bfloat16),
            in_specs=[pl.BlockSpec(memory_space=pltpu.VMEM)] * (groups + 4),
            out_specs=far,
            scratch_shapes=[
                pltpu.VMEM((blocks, own, ROW), jnp.bfloat16),
                pltpu.VMEM((blocks, own, ROW), jnp.bfloat16),
                pltpu.SemaphoreType.DMA((2,)),
            ]
            + scratch,
            compiler_params=large,
            cost_estimate=cost(2**32, 2**24),
            name="convolve",
        )(gated, *taps, wave, back_wave, twist)
    else:
        gated = decode(gated, 1).reshape(blocks, ROW, own)
        taps = jnp.transpose(decode(taps, 2), (1, 0, 2)).reshape(own, blocks, ROW)
        convolved = plain_conv(jnp.transpose(gated, (0, 2, 1)), jnp.transpose(taps, (1, 0, 2)))
        convolved = jnp.transpose(convolved, (1, 0, 2)).reshape(own, groups, -1)
        convolved = encode(jnp.transpose(convolved, (1, 0, 2)), 2)
    convolved = exchange(convolved, "seq")
    if fits:
        queries = pl.pallas_call(
            turn_kernel,
            out_shape=jax.ShapeDtypeStruct((wide, ROW), jnp.bfloat16),
            scratch_shapes=[pltpu.VMEM((ROW, wide), jnp.float32)],
            compiler_params=small,
            cost_estimate=cost(2**20, 2**21),
            name="turn_queries",
        )(*queries)
        return pl.pallas_call(
            mix_kernel,
            out_specs=far,
            out_shape=jax.ShapeDtypeStruct((wide, ROW), jnp.bfloat16),
            scratch_shapes=[
                pltpu.VMEM((wide, ROW), jnp.bfloat16),
                pltpu.SemaphoreType.DMA((groups,)),
            ],
            compiler_params=small,
            name="mix_out",
        )(queries, convolved)
    queries = jnp.transpose(queries.astype(jnp.float32))
    return (queries * decode(convolved, 2).reshape(wide, -1)).astype(jnp.bfloat16)


def cost(flops, moved):
    return pl.CostEstimate(flops=int(flops), bytes_accessed=int(moved), transcendentals=0)


def solution(mesh):
    placed = (P(("seq", "ch"), None, None), P("ch", "seq"), P("ch"))
    return jax.shard_map(
        body, mesh=mesh, in_specs=placed, out_specs=P("ch", "seq"), check_vma=False
    )
```

```python
import functools
import math

import jax
import jax.numpy as jnp
import numpy as np
from jax import lax
from jax.experimental import pallas as pl
from jax.experimental.pallas import tpu as pltpu
from jax.sharding import PartitionSpec as P

OCTAVES = 250.0
LOW_POWER = 125.0
EXPONENT_BITS = 8
EXPONENT_BIAS = 127.0
LANES = 128
ROW = 256
CHUNK = 16
GROUP = 32
VMEM_BYTES = 20 * 1024 * 1024
SMALL_BYTES = 12 * 1024 * 1024
ALL_BYTES = 60 * 1024 * 1024


def split_first(values, axis):
    count = min(values.shape[axis], LANES if axis == values.ndim - 1 else EXPONENT_BITS)
    first = lax.slice_in_dim(values, 0, count, axis=axis)
    if count == values.shape[axis]:
        return first, None
    return first, lax.slice_in_dim(values, count, values.shape[axis], axis=axis)


def scale_of(peak):
    power = jnp.floor(jnp.log(jnp.maximum(peak, 1e-30)) * (1.0 / math.log(2.0))) + 1.0
    return jnp.clip(power, -100.0, 126.0)


def exponent_bits(power, shape, axis):
    place = lax.broadcasted_iota(jnp.int32, shape, axis).astype(jnp.float32)
    bits = (power + (EXPONENT_BIAS + 0.25)) * jnp.exp2(-1.0 - place)
    return jnp.where(bits - jnp.floor(bits) >= 0.5, 0.5, 0.0), place < EXPONENT_BITS


def encode(values, axis):
    peak = jnp.max(jnp.abs(values), axis=axis, keepdims=True)
    return encode_all([values], scale_of(peak), axis)[0]


def encode_all(blocks, power, axis):
    unit_share, codes, bits = jnp.exp2(-power), [], None
    for values in blocks:
        share = jnp.abs(values) * unit_share
        level = jnp.minimum(
            share * (2.0 * OCTAVES),
            jnp.minimum(share * OCTAVES + OCTAVES / 4, share * (OCTAVES / 2) + OCTAVES / 2),
        )
        level = jnp.minimum(level, OCTAVES + 1.0)
        first, rest = split_first(level, axis)
        bits = exponent_bits(power, first.shape, axis) if bits is None else bits
        odd, holds = bits
        marked = (jnp.floor(first * 64.0 - odd + 0.5) + odd) * (1.0 / 64.0)
        level = jnp.where(holds, marked, first)
        if rest is not None:
            level = jnp.concatenate([level, rest], axis=axis)
        octave = jnp.floor(level)
        unit = jnp.exp2(octave - LOW_POWER)
        code = jnp.where(values < 0.0, -unit, unit) * (level - octave + 1.0)
        codes.append(code.astype(jnp.bfloat16))
    return codes


def decode(code, axis, halvings=0):
    code = code.astype(jnp.float32)
    size = jnp.abs(code)
    octave = jnp.floor(jnp.log(size) * (1.0 / math.log(2.0)) + 0.002)
    level = octave + size * jnp.exp2(-octave)
    first, _ = split_first(level, axis)
    half = first * 64.0 + ((LOW_POWER - 1.0) * 64.0 + 0.25)
    place = lax.broadcasted_iota(jnp.int32, first.shape, axis).astype(jnp.float32)
    weight = jnp.where(place < EXPONENT_BITS, jnp.exp2(place), 0.0)
    held = jnp.where(half - jnp.floor(half) >= 0.5, weight, 0.0)
    scale = jnp.exp2(jnp.sum(held, axis=axis, keepdims=True) - (EXPONENT_BIAS + halvings))
    step = 0.5 / OCTAVES
    low = (LOW_POWER - 1.0) * step
    share = jnp.maximum(
        level * step + low,
        jnp.maximum(
            level * (2.0 * step) + (2.0 * low - 0.25), level * (4.0 * step) + (4.0 * low - 1.0)
        ),
    )
    return jnp.where(code < 0.0, -scale, scale) * share


def tables(blocks):
    n2 = np.arange(ROW)
    k1 = np.arange(blocks)
    main = 2.0 * np.pi * np.outer(n2, n2 + 0.5) / ROW
    twist = 2.0 * np.pi * np.outer(k1 + 0.25 - blocks / 2, n2) / (blocks * ROW)
    mix = 2.0 * np.pi * np.outer(k1 + 0.25, np.arange(blocks)) / blocks
    wave = np.stack([np.cos(main), np.sin(main)]).astype(np.float32)
    twist = np.stack([np.cos(twist), np.sin(twist)], axis=1).astype(np.float32)
    mix = np.stack([np.cos(mix), np.sin(mix)], axis=0).astype(np.float32)
    return wave, twist, mix


def folded(wave):
    half = np.concatenate([wave[0, :, :LANES], wave[1, :, :LANES]], axis=1)
    parts = []
    for values in (half, half.T):
        high = values.astype(jnp.bfloat16)
        low = (values - high.astype(np.float32)).astype(jnp.bfloat16)
        parts.append(np.concatenate([high, low, high], axis=0))
    return parts


def put_split(ref, at, values):
    high = values.astype(jnp.bfloat16)
    ref[pl.ds(at, values.shape[0]), 0:ROW] = high
    ref[pl.ds(at, values.shape[0]), ROW : 2 * ROW] = high
    ref[pl.ds(at, values.shape[0]), 2 * ROW : 3 * ROW] = (
        values - high.astype(jnp.float32)
    ).astype(jnp.bfloat16)


def turned(value, steps):
    if steps == 0:
        return value
    re, im = value
    cos, sin = math.cos(math.pi * steps / 16), math.sin(math.pi * steps / 16)
    return re * cos - im * sin, im * cos + re * sin


def four_points(values, sign):
    (a_re, a_im), (b_re, b_im), (c_re, c_im), (d_re, d_im) = values
    sum_re, sum_im, gap_re, gap_im = a_re + c_re, a_im + c_im, a_re - c_re, a_im - c_im
    more_re, more_im = b_re + d_re, b_im + d_im
    side_re, side_im = sign * (d_im - b_im), sign * (b_re - d_re)
    return (
        (sum_re + more_re, sum_im + more_im),
        (gap_re + side_re, gap_im + side_im),
        (sum_re - more_re, sum_im - more_im),
        (gap_re - side_re, gap_im - side_im),
    )


def row_of(k, part, at):
    return (2 * k + part) * GROUP + at


def mix_forward(taken, twist_ref, at, ref):
    far = [value * math.sqrt(0.5) for value in taken[4:]]
    even = [turned((taken[n] + far[n], -far[n]), -n) for n in range(4)]
    odd = [turned((taken[n] - far[n], far[n]), -5 * n) for n in range(4)]
    for start, values in ((0, four_points(even, -1.0)), (1, four_points(odd, -1.0))):
        for index, (re, im) in enumerate(values):
            k = start + 2 * index
            cos_twist, sin_twist = twist_ref[k, 0:1, :], twist_ref[k, 1:2, :]
            put_split(ref, row_of(k, 0, at), re * cos_twist + im * sin_twist)
            put_split(ref, row_of(k, 1, at), im * cos_twist - re * sin_twist)


def mix_back(spectra, twist_ref):
    twisted = []
    for k, (re, im) in enumerate(spectra):
        cos_twist, sin_twist = twist_ref[k, 0:1, :], twist_ref[k, 1:2, :]
        twisted.append((re * cos_twist - im * sin_twist, im * cos_twist + re * sin_twist))
    even, odd = four_points(twisted[0::2], 1.0), four_points(twisted[1::2], 1.0)
    near, far = [], []
    for n in range(4):
        (even_re, even_im), (odd_re, odd_im) = turned(even[n], n), turned(odd[n], 5 * n)
        near.append(even_re + odd_re)
        far.append(((even_re - odd_re) - (even_im - odd_im)) * math.sqrt(0.5))
    return near + far


def spectrum_rows(waves_ref, k, at):
    re = waves_ref[pl.ds(row_of(k, 0, at), CHUNK), :]
    im = waves_ref[pl.ds(row_of(k, 1, at), CHUNK), :]
    return re, im


def send_kernel(streams_ref, gated_ref, keys, values, codes, in_sems, out_sems):
    groups, parts = gated_ref.shape[:2]
    per = groups
    width = per * LANES
    arrivals = []
    for chunk in range(parts):
        lanes = pl.ds(chunk * width, width)
        for stream, buffer in ((1, keys), (2, values)):
            copy = pltpu.make_async_copy(
                streams_ref.at[stream, :, lanes], buffer.at[chunk], in_sems.at[stream - 1, chunk]
            )
            copy.start()
            arrivals.append(copy)
    copies = []
    for chunk in range(parts):
        for copy in arrivals[2 * chunk : 2 * chunk + 2]:
            copy.wait()
        part, first = chunk, 0
        for block in range(per):
            lanes = slice(block * LANES, (block + 1) * LANES)
            left = keys[chunk, :, lanes].astype(jnp.float32)
            right = values[chunk, :, lanes].astype(jnp.float32)
            codes[first + block, part] = encode(left * right, 0)
        place = (pl.ds(first, per), part)
        copy = pltpu.make_async_copy(codes.at[place], gated_ref.at[place], out_sems.at[chunk])
        copy.start()
        copies.append(copy)
    for copy in copies:
        copy.wait()


def query_kernel(streams_ref, *refs):
    query_refs, sems = refs[:-1], refs[-1]
    me = lax.axis_index("ch")
    wide = query_refs[0].shape[1]
    copies = []
    for turn, query_ref in enumerate(query_refs):
        lanes = pl.ds(pl.multiple_of((me ^ turn) * wide, wide), wide)
        copy = pltpu.make_async_copy(streams_ref.at[0, :, lanes], query_ref, sems.at[turn])
        copy.start()
        copies.append(copy)
    for copy in copies:
        copy.wait()


def taps_kernel(taps_ref, skip_ref, *code_refs):
    me = lax.axis_index("seq")
    first = (me == 0).astype(jnp.float32)
    row = lax.broadcasted_iota(jnp.int32, (LANES, LANES), 0)
    lane = lax.broadcasted_iota(jnp.int32, (LANES, LANES), 1)
    for turn, code_ref in enumerate(code_refs):
        block = me ^ turn
        gains = jnp.broadcast_to(skip_ref[pl.ds(block, 1), :], (LANES, LANES))
        gain = jnp.sum(jnp.where(row == lane, gains, 0.0), axis=1, keepdims=True) * first
        start = taps_ref[block, :, :LANES] + jnp.where(lane == 0, gain, 0.0)
        taps = jnp.concatenate([start, taps_ref[block, :, LANES:]], axis=1)
        code_ref[...] = encode(taps, 1)


def combined(waves_ref, k, at):
    re, im = spectrum_rows(waves_ref, k, at)
    re_cos, re_sin, im_cos, im_sin = re[:, :LANES], re[:, LANES:], im[:, :LANES], im[:, LANES:]
    return (
        jnp.concatenate([re_cos + im_sin, re_cos - im_sin], axis=1),
        jnp.concatenate([im_cos - re_sin, im_cos + re_sin], axis=1),
    )


def put_folded(ref, k, at, re, im):
    near_re, far_re, near_im, far_im = re[:, :LANES], re[:, LANES:], im[:, :LANES], im[:, LANES:]
    back_re = jnp.concatenate([near_re + far_re, far_im - near_im], axis=1)
    back_im = jnp.concatenate([near_im + far_im, near_re - far_re], axis=1)
    put_split(ref, row_of(k, 0, at), back_re)
    put_split(ref, row_of(k, 1, at), back_im)


def multiply(source, wave_ref, target):
    target[...] = jnp.dot(source[...], wave_ref[...], preferred_element_type=jnp.float32)


def row_groups():
    return [range(first, first + GROUP, CHUNK) for first in range(0, LANES, GROUP)]


def gated_spectrum_kernel(gated_ref, wave_ref, twist_ref, out_ref, u, *scratch):
    rows, waves = scratch[0:2], scratch[2:4]
    blocks = u.shape[0]
    parts = ROW // gated_ref.shape[1]
    groups = row_groups()

    def unpack(block, _):
        pieces = [decode(gated_ref[block * parts + part], 0) for part in range(parts)]
        u[block] = jnp.transpose(jnp.concatenate(pieces, axis=0))
        return 0

    lax.fori_loop(0, blocks, unpack, 0)
    for step in range(len(groups) + 2):
        if 0 <= step - 1 < len(groups):
            multiply(rows[(step - 1) % 2], wave_ref, waves[(step - 1) % 2])
        if step < len(groups):
            for at in groups[step]:
                taken = [u[n1, at : at + CHUNK, :] for n1 in range(blocks)]
                mix_forward(taken, twist_ref, at % GROUP, rows[step % 2])
        if step >= 2:
            for at in groups[step - 2]:
                for k in range(blocks):
                    re, im = combined(waves[step % 2], k, at % GROUP)
                    out_ref[k, 0, at : at + CHUNK, :] = re
                    out_ref[k, 1, at : at + CHUNK, :] = im


def conv_kernel(gated_ref, *refs):
    blocks = gated_ref.shape[0]
    wave_ref, back_wave_ref, twist_ref, out_ref, codes, out, sems, *scratch = refs[blocks:]
    rows, waves, back_rows, back_waves = (scratch[at : at + 2] for at in (0, 2, 4, 6))
    scale = math.log2(blocks * ROW)
    me = lax.axis_index("seq")
    groups = row_groups()
    for turn, code_ref in enumerate(refs[:blocks]):
        codes[me ^ turn] = code_ref[...]

    def forward(at, half):
        taken = [decode(codes[n1, at : at + CHUNK, :], 1, scale) for n1 in range(blocks)]
        mix_forward(taken, twist_ref, at % GROUP, rows[half])

    def product(at, half):
        for k in range(blocks):
            re, im = combined(waves[half], k, at % GROUP)
            gated_re = gated_ref[k, 0, at : at + CHUNK, :]
            gated_im = gated_ref[k, 1, at : at + CHUNK, :]
            product_re, product_im = re * gated_re - im * gated_im, re * gated_im + im * gated_re
            put_folded(back_rows[half], k, at % GROUP, product_re, product_im)

    def back(at, half):
        spectra = [spectrum_rows(back_waves[half], k, at % GROUP) for k in range(blocks)]
        totals = mix_back(spectra, twist_ref)
        sizes = [jnp.abs(total) for total in totals]
        peak = jnp.max(functools.reduce(jnp.maximum, sizes), axis=1, keepdims=True)
        for n1, code in enumerate(encode_all(totals, scale_of(peak), 1)):
            out[n1, at : at + CHUNK, :] = code

    copies = []
    for step in range(len(groups) + 4):
        if 0 <= step - 1 < len(groups):
            multiply(rows[(step - 1) % 2], wave_ref, waves[(step - 1) % 2])
        if 0 <= step - 3 < len(groups):
            multiply(back_rows[(step - 3) % 2], back_wave_ref, back_waves[(step - 3) % 2])
        for work, delay in ((forward, 0), (product, 2), (back, 4)):
            if 0 <= step - delay < len(groups):
                for at in groups[step - delay]:
                    work(at, step % 2)
        if step >= 4:
            place = pl.ds((step - 4) * GROUP, GROUP)
            copy = pltpu.make_async_copy(
                out.at[:, place, :], out_ref.at[:, place, :], sems.at[step - 4]
            )
            copy.start()
            copies.append(copy)
    for copy in copies:
        copy.wait()


def turn_kernel(*refs):
    query_refs, out_ref, whole = refs[:-2], refs[-2], refs[-1]
    me = lax.axis_index("ch")
    held = query_refs[0].shape[0]
    for turn, query_ref in enumerate(query_refs):
        at = pl.multiple_of((me ^ turn) * held, held)
        whole[pl.ds(at, held), :] = query_ref[...].astype(jnp.float32)
    out_ref[...] = jnp.transpose(whole[...]).astype(jnp.bfloat16)


def mix_kernel(query_ref, conv_ref, out_ref, mixed, sems):
    copies = []
    for block in range(conv_ref.shape[0]):
        at = pl.ds(block * LANES, LANES)
        queries = query_ref[at, :].astype(jnp.float32)
        mixed[at, :] = (queries * decode(conv_ref[block], 1)).astype(jnp.bfloat16)
        copy = pltpu.make_async_copy(mixed.at[at], out_ref.at[at], sems.at[block])
        copy.start()
        copies.append(copy)
    for copy in copies:
        copy.wait()


def plain_conv(gated, taps):
    blocks = gated.shape[0]
    (cos, sin), twist, mix = tables(blocks)
    cos_twist, sin_twist = twist[:, 0][:, None, :], twist[:, 1][:, None, :]
    dot = functools.partial(jnp.einsum, precision=lax.Precision.HIGHEST)

    def forward(values):
        re = dot("ncm,kn->kcm", values, mix[0])
        im = -dot("ncm,kn->kcm", values, mix[1])
        re, im = re * cos_twist + im * sin_twist, im * cos_twist - re * sin_twist
        return (
            dot("kcm,mq->kcq", re, cos) + dot("kcm,mq->kcq", im, sin),
            dot("kcm,mq->kcq", im, cos) - dot("kcm,mq->kcq", re, sin),
        )

    u_re, u_im = forward(gated)
    h_re, h_im = forward(taps)
    re, im = u_re * h_re - u_im * h_im, u_re * h_im + u_im * h_re
    re, im = (
        dot("kcq,mq->kcm", re, cos) - dot("kcq,mq->kcm", im, sin),
        dot("kcq,mq->kcm", im, cos) + dot("kcq,mq->kcm", re, sin),
    )
    re, im = re * cos_twist - im * sin_twist, im * cos_twist + re * sin_twist
    total = dot("kcm,kn->ncm", re, mix[0]) - dot("kcm,kn->ncm", im, mix[1])
    return total * (1.0 / (blocks * ROW))


def scatter(blocks, axis):
    count = len(blocks)
    return [
        lax.ppermute(block, axis, [(i, i ^ turn) for i in range(count)]) if turn else block
        for turn, block in enumerate(blocks)
    ]


def body(streams, filter_taps, skip_gain):
    groups, parts = lax.axis_size("seq"), lax.axis_size("ch")
    held, _, channels = streams.shape
    wide = channels // parts
    own = wide // groups
    blocks = filter_taps.shape[1] * groups // ROW
    streams = jnp.transpose(streams, (1, 0, 2))
    fits = blocks == 8 and own == LANES and filter_taps.shape[1] == ROW and ROW % held == 0 and groups % 4 == 0
    fits = fits and groups & (groups - 1) == 0 and parts & (parts - 1) == 0
    small = pltpu.CompilerParams(vmem_limit_bytes=SMALL_BYTES)
    if fits:
        far = pl.BlockSpec(memory_space=pl.ANY)
        coded = (groups, parts, held, own)
        stream = pltpu.VMEM((parts, held, wide), jnp.bfloat16)
        gated = pl.pallas_call(
            send_kernel,
            in_specs=[far],
            out_specs=far,
            out_shape=jax.ShapeDtypeStruct(coded, jnp.bfloat16),
            scratch_shapes=[
                stream,
                stream,
                pltpu.VMEM(coded, jnp.bfloat16),
                pltpu.SemaphoreType.DMA((2, 2 * parts)),
                pltpu.SemaphoreType.DMA((2 * parts,)),
            ],
            compiler_params=pltpu.CompilerParams(vmem_limit_bytes=ALL_BYTES),
            cost_estimate=cost(2**25, 2**23),
            name="encode_gated",
        )(streams)
        queries = pl.pallas_call(
            query_kernel,
            in_specs=[far],
            out_specs=[far] * parts,
            out_shape=[jax.ShapeDtypeStruct((held, wide), jnp.bfloat16)] * parts,
            scratch_shapes=[pltpu.SemaphoreType.DMA((parts,))],
            compiler_params=small,
            cost_estimate=cost(2**10, 2**20),
            name="send_queries",
        )(streams)
        taps = pl.pallas_call(
            taps_kernel,
            out_shape=[jax.ShapeDtypeStruct((own, ROW), jnp.bfloat16)] * groups,
            compiler_params=small,
            cost_estimate=cost(2**25, 2**23),
            name="encode_taps",
        )(filter_taps.reshape(groups, own, ROW), skip_gain.reshape(groups, own))
    else:
        gated = encode(streams[1].astype(jnp.float32) * streams[2].astype(jnp.float32), 0)
        gated = jnp.transpose(gated.reshape(held, parts, groups, own), (2, 1, 0, 3))
        queries = jnp.transpose(streams[0].reshape(held, parts, wide), (1, 0, 2))
        first = lax.axis_index("seq") == 0
        taps = filter_taps.at[:, 0].add(jnp.where(first, skip_gain, 0.0))
        taps = encode(taps, 1).reshape(groups, own, -1)
    exchange = functools.partial(lax.all_to_all, split_axis=0, concat_axis=0, tiled=True)
    gated = gated.reshape(groups * parts, held, own)
    if fits:
        taps = scatter(taps, "seq")
        gated = exchange(gated, ("seq", "ch"))
        queries = scatter(queries, "ch")
    else:
        taps = exchange(taps, "seq")
        gated = exchange(gated, ("seq", "ch"))
        queries = exchange(queries, "ch").reshape(parts * held, wide)
    if fits:
        wave, twist, _ = tables(blocks)
        wave, back_wave = folded(wave)
        scratch = [pltpu.VMEM((blocks * 2 * GROUP, 3 * ROW), jnp.bfloat16)] * 2
        scratch += [pltpu.VMEM((blocks * 2 * GROUP, ROW), jnp.float32)] * 2
        large = pltpu.CompilerParams(vmem_limit_bytes=VMEM_BYTES)
        gated = pl.pallas_call(
            gated_spectrum_kernel,
            out_shape=jax.ShapeDtypeStruct((blocks, 2, own, ROW), jnp.float32),
            scratch_shapes=[pltpu.VMEM((blocks, own, ROW), jnp.float32)] + scratch,
            compiler_params=large,
            cost_estimate=cost(2**32, 2**24),
            name="gated_spectrum",
        )(gated, wave, twist)
        convolved = pl.pallas_call(
            conv_kernel,
            out_shape=jax.ShapeDtypeStruct((blocks, own, ROW), jnp.bfloat16),
            in_specs=[pl.BlockSpec(memory_space=pltpu.VMEM)] * (groups + 4),
            out_specs=far,
            scratch_shapes=[
                pltpu.VMEM((blocks, own, ROW), jnp.bfloat16),
                pltpu.VMEM((blocks, own, ROW), jnp.bfloat16),
                pltpu.SemaphoreType.DMA((own // GROUP,)),
            ]
            + scratch * 2,
            compiler_params=large,
            cost_estimate=cost(2**32, 2**24),
            name="convolve",
        )(gated, *taps, wave, back_wave, twist)
    else:
        gated = decode(gated, 1).reshape(blocks, ROW, own)
        taps = jnp.transpose(decode(taps, 2), (1, 0, 2)).reshape(own, blocks, ROW)
        convolved = plain_conv(jnp.transpose(gated, (0, 2, 1)), jnp.transpose(taps, (1, 0, 2)))
        convolved = jnp.transpose(convolved, (1, 0, 2)).reshape(own, groups, -1)
        convolved = encode(jnp.transpose(convolved, (1, 0, 2)), 2)
    convolved = exchange(convolved, "seq")
    if fits:
        queries = pl.pallas_call(
            turn_kernel,
            out_shape=jax.ShapeDtypeStruct((wide, ROW), jnp.bfloat16),
            scratch_shapes=[pltpu.VMEM((ROW, wide), jnp.float32)],
            compiler_params=small,
            cost_estimate=cost(2**20, 2**21),
            name="turn_queries",
        )(*queries)
        return pl.pallas_call(
            mix_kernel,
            out_specs=far,
            out_shape=jax.ShapeDtypeStruct((wide, ROW), jnp.bfloat16),
            scratch_shapes=[
                pltpu.VMEM((wide, ROW), jnp.bfloat16),
                pltpu.SemaphoreType.DMA((groups,)),
            ],
            compiler_params=small,
            name="mix_out",
        )(queries, convolved)
    queries = jnp.transpose(queries.astype(jnp.float32))
    return (queries * decode(convolved, 2).reshape(wide, -1)).astype(jnp.bfloat16)


def cost(flops, moved):
    return pl.CostEstimate(flops=int(flops), bytes_accessed=int(moved), transcendentals=0)


def solution(mesh):
    placed = (P(("seq", "ch"), None, None), P("ch", "seq"), P("ch"))
    return jax.shard_map(
        body, mesh=mesh, in_specs=placed, out_specs=P("ch", "seq"), check_vma=False
    )
```

```python
import functools
import math

import jax
import jax.numpy as jnp
import numpy as np
from jax import lax
from jax.experimental import pallas as pl
from jax.experimental.pallas import tpu as pltpu
from jax.sharding import PartitionSpec as P

GRID = 36.0
LOW_POWER = 125.0
EXPONENT_BITS = 8
EXPONENT_BIAS = 127.0
LANES = 128
ROW = 256
CHUNK = 16
GROUP = 32
VMEM_BYTES = 20 * 1024 * 1024
SMALL_BYTES = 12 * 1024 * 1024
ALL_BYTES = 60 * 1024 * 1024


def split_first(values, axis):
    count = min(values.shape[axis], LANES if axis == values.ndim - 1 else EXPONENT_BITS)
    first = lax.slice_in_dim(values, 0, count, axis=axis)
    if count == values.shape[axis]:
        return first, None
    return first, lax.slice_in_dim(values, count, values.shape[axis], axis=axis)


def scale_of(peak):
    power = jnp.floor(jnp.log(jnp.maximum(peak, 1e-30)) * (1.0 / math.log(2.0))) + 1.0
    return jnp.clip(power, -100.0, 126.0)


def exponent_bits(power, shape, axis):
    place = lax.broadcasted_iota(jnp.int32, shape, axis).astype(jnp.float32)
    bits = (power + (EXPONENT_BIAS + 0.25)) * jnp.exp2(-1.0 - place)
    return jnp.where(bits - jnp.floor(bits) >= 0.5, 0.5, 0.0), place < EXPONENT_BITS


def encode(values, axis):
    peak = jnp.max(jnp.abs(values), axis=axis, keepdims=True)
    return encode_all([values], scale_of(peak), axis)[0]


def encode_all(blocks, power, axis):
    unit_share, codes, bits = jnp.exp2(-power), [], None
    top = 2.0 * LOW_POWER
    for values in blocks:
        share = jnp.abs(values) * unit_share
        place = jnp.minimum(
            jnp.minimum(share * (2.0 * top) - LOW_POWER, share * top - LOW_POWER / 2),
            jnp.minimum(share * LOW_POWER, LOW_POWER + 1.0),
        )
        first, rest = split_first(place, axis)
        bits = exponent_bits(power, first.shape, axis) if bits is None else bits
        odd, holds = bits
        if axis == values.ndim - 1:
            marked = (jnp.floor(first * GRID - odd + 0.5) + odd) * (1.0 / GRID)
            first = jnp.exp2(jnp.where(holds, marked, first))
        else:
            marked = (jnp.floor(first * 64.0 - odd + 0.5) + odd) * (1.0 / 64.0)
            octave = jnp.floor(marked)
            first = jnp.exp2(octave) * (marked - octave + 1.0)
        size = first
        if rest is not None:
            size = jnp.concatenate([first, jnp.exp2(rest)], axis=axis)
        codes.append(jnp.where(values < 0.0, -size, size).astype(jnp.bfloat16))
    return codes


def decode(code, axis, halvings=0):
    code = code.astype(jnp.float32)
    size = jnp.abs(code)
    place = jnp.log(size) * (1.0 / math.log(2.0))
    first, rest = split_first(place, axis)
    if axis == code.ndim - 1:
        half = first * GRID + 0.25
    else:
        octave = jnp.floor(first + 0.002)
        first = octave + split_first(size, axis)[0] * jnp.exp2(-octave) - 1.0
        half = first * 64.0 + 0.25
        place = first if rest is None else jnp.concatenate([first, rest], axis=axis)
    spot = lax.broadcasted_iota(jnp.int32, first.shape, axis).astype(jnp.float32)
    weight = jnp.where(spot < EXPONENT_BITS, jnp.exp2(spot), 0.0)
    held = jnp.where(half - jnp.floor(half) >= 0.5, weight, 0.0)
    scale = jnp.exp2(jnp.sum(held, axis=axis, keepdims=True) - (EXPONENT_BIAS + halvings))
    step = 0.25 / LOW_POWER
    share = jnp.maximum(
        place * (4.0 * step), jnp.maximum(place * (2.0 * step) + 0.25, place * step + 0.25)
    )
    return jnp.where(code < 0.0, -scale, scale) * share


def tables(blocks):
    n2 = np.arange(ROW)
    k1 = np.arange(blocks)
    main = 2.0 * np.pi * np.outer(n2, n2 + 0.5) / ROW
    twist = 2.0 * np.pi * np.outer(k1 + 0.25 - blocks / 2, n2) / (blocks * ROW)
    mix = 2.0 * np.pi * np.outer(k1 + 0.25, np.arange(blocks)) / blocks
    wave = np.stack([np.cos(main), np.sin(main)]).astype(np.float32)
    twist = np.stack([np.cos(twist), np.sin(twist)], axis=1).astype(np.float32)
    mix = np.stack([np.cos(mix), np.sin(mix)], axis=0).astype(np.float32)
    return wave, twist, mix


def folded(wave):
    half = np.concatenate([wave[0, :, :LANES], wave[1, :, :LANES]], axis=1)
    parts = []
    for values in (half, half.T):
        high = values.astype(jnp.bfloat16)
        low = (values - high.astype(np.float32)).astype(jnp.bfloat16)
        parts.append(np.concatenate([high, low, high], axis=0))
    return parts


def put_split(ref, at, values):
    high = values.astype(jnp.bfloat16)
    ref[pl.ds(at, values.shape[0]), 0:ROW] = high
    ref[pl.ds(at, values.shape[0]), ROW : 2 * ROW] = high
    ref[pl.ds(at, values.shape[0]), 2 * ROW : 3 * ROW] = (
        values - high.astype(jnp.float32)
    ).astype(jnp.bfloat16)


def turned(value, steps):
    if steps == 0:
        return value
    re, im = value
    cos, sin = math.cos(math.pi * steps / 16), math.sin(math.pi * steps / 16)
    return re * cos - im * sin, im * cos + re * sin


def four_points(values, sign):
    (a_re, a_im), (b_re, b_im), (c_re, c_im), (d_re, d_im) = values
    sum_re, sum_im, gap_re, gap_im = a_re + c_re, a_im + c_im, a_re - c_re, a_im - c_im
    more_re, more_im = b_re + d_re, b_im + d_im
    side_re, side_im = sign * (d_im - b_im), sign * (b_re - d_re)
    return (
        (sum_re + more_re, sum_im + more_im),
        (gap_re + side_re, gap_im + side_im),
        (sum_re - more_re, sum_im - more_im),
        (gap_re - side_re, gap_im - side_im),
    )


def row_of(k, part, at):
    return (2 * k + part) * GROUP + at


def mix_forward(taken, twist_ref, at, ref):
    far = [value * math.sqrt(0.5) for value in taken[4:]]
    even = [turned((taken[n] + far[n], -far[n]), -n) for n in range(4)]
    odd = [turned((taken[n] - far[n], far[n]), -5 * n) for n in range(4)]
    for start, values in ((0, four_points(even, -1.0)), (1, four_points(odd, -1.0))):
        for index, (re, im) in enumerate(values):
            k = start + 2 * index
            cos_twist, sin_twist = twist_ref[k, 0:1, :], twist_ref[k, 1:2, :]
            put_split(ref, row_of(k, 0, at), re * cos_twist + im * sin_twist)
            put_split(ref, row_of(k, 1, at), im * cos_twist - re * sin_twist)


def mix_back(spectra, twist_ref):
    twisted = []
    for k, (re, im) in enumerate(spectra):
        cos_twist, sin_twist = twist_ref[k, 0:1, :], twist_ref[k, 1:2, :]
        twisted.append((re * cos_twist - im * sin_twist, im * cos_twist + re * sin_twist))
    even, odd = four_points(twisted[0::2], 1.0), four_points(twisted[1::2], 1.0)
    near, far = [], []
    for n in range(4):
        (even_re, even_im), (odd_re, odd_im) = turned(even[n], n), turned(odd[n], 5 * n)
        near.append(even_re + odd_re)
        far.append(((even_re - odd_re) - (even_im - odd_im)) * math.sqrt(0.5))
    return near + far


def spectrum_rows(waves_ref, k, at):
    re = waves_ref[pl.ds(row_of(k, 0, at), CHUNK), :]
    im = waves_ref[pl.ds(row_of(k, 1, at), CHUNK), :]
    return re, im


def send_kernel(streams_ref, gated_ref, keys, values, codes, in_sems, out_sems):
    groups, parts = gated_ref.shape[:2]
    per = groups
    width = per * LANES
    arrivals = []
    for chunk in range(parts):
        lanes = pl.ds(chunk * width, width)
        for stream, buffer in ((1, keys), (2, values)):
            copy = pltpu.make_async_copy(
                streams_ref.at[stream, :, lanes], buffer.at[chunk], in_sems.at[stream - 1, chunk]
            )
            copy.start()
            arrivals.append(copy)
    copies = []
    for chunk in range(parts):
        for copy in arrivals[2 * chunk : 2 * chunk + 2]:
            copy.wait()
        part, first = chunk, 0
        for block in range(per):
            lanes = slice(block * LANES, (block + 1) * LANES)
            left = keys[chunk, :, lanes].astype(jnp.float32)
            right = values[chunk, :, lanes].astype(jnp.float32)
            codes[first + block, part] = encode(left * right, 0)
        place = (pl.ds(first, per), part)
        copy = pltpu.make_async_copy(codes.at[place], gated_ref.at[place], out_sems.at[chunk])
        copy.start()
        copies.append(copy)
    for copy in copies:
        copy.wait()


def query_kernel(streams_ref, *refs):
    query_refs, sems = refs[:-1], refs[-1]
    me = lax.axis_index("ch")
    wide = query_refs[0].shape[1]
    copies = []
    for turn, query_ref in enumerate(query_refs):
        lanes = pl.ds(pl.multiple_of((me ^ turn) * wide, wide), wide)
        copy = pltpu.make_async_copy(streams_ref.at[0, :, lanes], query_ref, sems.at[turn])
        copy.start()
        copies.append(copy)
    for copy in copies:
        copy.wait()


def taps_kernel(taps_ref, skip_ref, *code_refs):
    me = lax.axis_index("seq")
    first = (me == 0).astype(jnp.float32)
    row = lax.broadcasted_iota(jnp.int32, (LANES, LANES), 0)
    lane = lax.broadcasted_iota(jnp.int32, (LANES, LANES), 1)
    for turn, code_ref in enumerate(code_refs):
        block = me ^ turn
        gains = jnp.broadcast_to(skip_ref[pl.ds(block, 1), :], (LANES, LANES))
        gain = jnp.sum(jnp.where(row == lane, gains, 0.0), axis=1, keepdims=True) * first
        start = taps_ref[block, :, :LANES] + jnp.where(lane == 0, gain, 0.0)
        taps = jnp.concatenate([start, taps_ref[block, :, LANES:]], axis=1)
        code_ref[...] = encode(taps, 1)


def combined(waves_ref, k, at):
    re, im = spectrum_rows(waves_ref, k, at)
    re_cos, re_sin, im_cos, im_sin = re[:, :LANES], re[:, LANES:], im[:, :LANES], im[:, LANES:]
    return (
        jnp.concatenate([re_cos + im_sin, re_cos - im_sin], axis=1),
        jnp.concatenate([im_cos - re_sin, im_cos + re_sin], axis=1),
    )


def put_folded(ref, k, at, re, im):
    near_re, far_re, near_im, far_im = re[:, :LANES], re[:, LANES:], im[:, :LANES], im[:, LANES:]
    back_re = jnp.concatenate([near_re + far_re, far_im - near_im], axis=1)
    back_im = jnp.concatenate([near_im + far_im, near_re - far_re], axis=1)
    put_split(ref, row_of(k, 0, at), back_re)
    put_split(ref, row_of(k, 1, at), back_im)


def multiply(source, wave_ref, target):
    target[...] = jnp.dot(source[...], wave_ref[...], preferred_element_type=jnp.float32)


def row_groups():
    return [range(first, first + GROUP, CHUNK) for first in range(0, LANES, GROUP)]


def gated_spectrum_kernel(gated_ref, wave_ref, twist_ref, out_ref, u, *scratch):
    rows, waves = scratch[0:2], scratch[2:4]
    blocks = u.shape[0]
    parts = ROW // gated_ref.shape[1]
    groups = row_groups()

    def unpack(block, _):
        pieces = [decode(gated_ref[block * parts + part], 0) for part in range(parts)]
        u[block] = jnp.transpose(jnp.concatenate(pieces, axis=0))
        return 0

    lax.fori_loop(0, blocks, unpack, 0)
    for step in range(len(groups) + 2):
        if 0 <= step - 1 < len(groups):
            multiply(rows[(step - 1) % 2], wave_ref, waves[(step - 1) % 2])
        if step < len(groups):
            for at in groups[step]:
                taken = [u[n1, at : at + CHUNK, :] for n1 in range(blocks)]
                mix_forward(taken, twist_ref, at % GROUP, rows[step % 2])
        if step >= 2:
            for at in groups[step - 2]:
                for k in range(blocks):
                    re, im = combined(waves[step % 2], k, at % GROUP)
                    out_ref[k, 0, at : at + CHUNK, :] = re
                    out_ref[k, 1, at : at + CHUNK, :] = im


def conv_kernel(gated_ref, *refs):
    blocks = gated_ref.shape[0]
    wave_ref, back_wave_ref, twist_ref, out_ref, codes, out, sems, *scratch = refs[blocks:]
    rows, waves, back_rows, back_waves = (scratch[at : at + 2] for at in (0, 2, 4, 6))
    scale = math.log2(blocks * ROW)
    me = lax.axis_index("seq")
    groups = row_groups()
    for turn, code_ref in enumerate(refs[:blocks]):
        codes[me ^ turn] = code_ref[...]

    def forward(at, half):
        taken = [decode(codes[n1, at : at + CHUNK, :], 1, scale) for n1 in range(blocks)]
        mix_forward(taken, twist_ref, at % GROUP, rows[half])

    def product(at, half):
        for k in range(blocks):
            re, im = combined(waves[half], k, at % GROUP)
            gated_re = gated_ref[k, 0, at : at + CHUNK, :]
            gated_im = gated_ref[k, 1, at : at + CHUNK, :]
            product_re, product_im = re * gated_re - im * gated_im, re * gated_im + im * gated_re
            put_folded(back_rows[half], k, at % GROUP, product_re, product_im)

    def back(at, half):
        spectra = [spectrum_rows(back_waves[half], k, at % GROUP) for k in range(blocks)]
        totals = mix_back(spectra, twist_ref)
        sizes = [jnp.abs(total) for total in totals]
        peak = jnp.max(functools.reduce(jnp.maximum, sizes), axis=1, keepdims=True)
        for n1, code in enumerate(encode_all(totals, scale_of(peak), 1)):
            out[n1, at : at + CHUNK, :] = code

    copies = []
    for step in range(len(groups) + 4):
        if 0 <= step - 1 < len(groups):
            multiply(rows[(step - 1) % 2], wave_ref, waves[(step - 1) % 2])
        if 0 <= step - 3 < len(groups):
            multiply(back_rows[(step - 3) % 2], back_wave_ref, back_waves[(step - 3) % 2])
        for work, delay in ((forward, 0), (product, 2), (back, 4)):
            if 0 <= step - delay < len(groups):
                for at in groups[step - delay]:
                    work(at, step % 2)
        if step >= 4:
            place = pl.ds((step - 4) * GROUP, GROUP)
            copy = pltpu.make_async_copy(
                out.at[:, place, :], out_ref.at[:, place, :], sems.at[step - 4]
            )
            copy.start()
            copies.append(copy)
    for copy in copies:
        copy.wait()


def turn_kernel(*refs):
    query_refs, out_ref, whole = refs[:-2], refs[-2], refs[-1]
    me = lax.axis_index("ch")
    held = query_refs[0].shape[0]
    for turn, query_ref in enumerate(query_refs):
        at = pl.multiple_of((me ^ turn) * held, held)
        whole[pl.ds(at, held), :] = query_ref[...].astype(jnp.float32)
    out_ref[...] = jnp.transpose(whole[...]).astype(jnp.bfloat16)


def mix_kernel(query_ref, conv_ref, out_ref, mixed, sems):
    copies = []
    for block in range(conv_ref.shape[0]):
        at = pl.ds(block * LANES, LANES)
        queries = query_ref[at, :].astype(jnp.float32)
        mixed[at, :] = (queries * decode(conv_ref[block], 1)).astype(jnp.bfloat16)
        copy = pltpu.make_async_copy(mixed.at[at], out_ref.at[at], sems.at[block])
        copy.start()
        copies.append(copy)
    for copy in copies:
        copy.wait()


def plain_conv(gated, taps):
    blocks = gated.shape[0]
    (cos, sin), twist, mix = tables(blocks)
    cos_twist, sin_twist = twist[:, 0][:, None, :], twist[:, 1][:, None, :]
    dot = functools.partial(jnp.einsum, precision=lax.Precision.HIGHEST)

    def forward(values):
        re = dot("ncm,kn->kcm", values, mix[0])
        im = -dot("ncm,kn->kcm", values, mix[1])
        re, im = re * cos_twist + im * sin_twist, im * cos_twist - re * sin_twist
        return (
            dot("kcm,mq->kcq", re, cos) + dot("kcm,mq->kcq", im, sin),
            dot("kcm,mq->kcq", im, cos) - dot("kcm,mq->kcq", re, sin),
        )

    u_re, u_im = forward(gated)
    h_re, h_im = forward(taps)
    re, im = u_re * h_re - u_im * h_im, u_re * h_im + u_im * h_re
    re, im = (
        dot("kcq,mq->kcm", re, cos) - dot("kcq,mq->kcm", im, sin),
        dot("kcq,mq->kcm", im, cos) + dot("kcq,mq->kcm", re, sin),
    )
    re, im = re * cos_twist - im * sin_twist, im * cos_twist + re * sin_twist
    total = dot("kcm,kn->ncm", re, mix[0]) - dot("kcm,kn->ncm", im, mix[1])
    return total * (1.0 / (blocks * ROW))


def scatter(blocks, axis):
    count = len(blocks)
    return [
        lax.ppermute(block, axis, [(i, i ^ turn) for i in range(count)]) if turn else block
        for turn, block in enumerate(blocks)
    ]


def body(streams, filter_taps, skip_gain):
    groups, parts = lax.axis_size("seq"), lax.axis_size("ch")
    held, _, channels = streams.shape
    wide = channels // parts
    own = wide // groups
    blocks = filter_taps.shape[1] * groups // ROW
    streams = jnp.transpose(streams, (1, 0, 2))
    fits = blocks == 8 and own == LANES and filter_taps.shape[1] == ROW and ROW % held == 0 and groups % 4 == 0
    fits = fits and groups & (groups - 1) == 0 and parts & (parts - 1) == 0
    small = pltpu.CompilerParams(vmem_limit_bytes=SMALL_BYTES)
    if fits:
        far = pl.BlockSpec(memory_space=pl.ANY)
        coded = (groups, parts, held, own)
        stream = pltpu.VMEM((parts, held, wide), jnp.bfloat16)
        gated = pl.pallas_call(
            send_kernel,
            in_specs=[far],
            out_specs=far,
            out_shape=jax.ShapeDtypeStruct(coded, jnp.bfloat16),
            scratch_shapes=[
                stream,
                stream,
                pltpu.VMEM(coded, jnp.bfloat16),
                pltpu.SemaphoreType.DMA((2, 2 * parts)),
                pltpu.SemaphoreType.DMA((2 * parts,)),
            ],
            compiler_params=pltpu.CompilerParams(vmem_limit_bytes=ALL_BYTES),
            cost_estimate=cost(2**25, 2**23),
            name="encode_gated",
        )(streams)
        queries = pl.pallas_call(
            query_kernel,
            in_specs=[far],
            out_specs=[far] * parts,
            out_shape=[jax.ShapeDtypeStruct((held, wide), jnp.bfloat16)] * parts,
            scratch_shapes=[pltpu.SemaphoreType.DMA((parts,))],
            compiler_params=small,
            cost_estimate=cost(2**10, 2**20),
            name="send_queries",
        )(streams)
        taps = pl.pallas_call(
            taps_kernel,
            out_shape=[jax.ShapeDtypeStruct((own, ROW), jnp.bfloat16)] * groups,
            compiler_params=small,
            cost_estimate=cost(2**25, 2**23),
            name="encode_taps",
        )(filter_taps.reshape(groups, own, ROW), skip_gain.reshape(groups, own))
    else:
        gated = encode(streams[1].astype(jnp.float32) * streams[2].astype(jnp.float32), 0)
        gated = jnp.transpose(gated.reshape(held, parts, groups, own), (2, 1, 0, 3))
        queries = jnp.transpose(streams[0].reshape(held, parts, wide), (1, 0, 2))
        first = lax.axis_index("seq") == 0
        taps = filter_taps.at[:, 0].add(jnp.where(first, skip_gain, 0.0))
        taps = encode(taps, 1).reshape(groups, own, -1)
    exchange = functools.partial(lax.all_to_all, split_axis=0, concat_axis=0, tiled=True)
    gated = gated.reshape(groups * parts, held, own)
    if fits:
        taps = scatter(taps, "seq")
        gated = exchange(gated, ("seq", "ch"))
        queries = scatter(queries, "ch")
    else:
        taps = exchange(taps, "seq")
        gated = exchange(gated, ("seq", "ch"))
        queries = exchange(queries, "ch").reshape(parts * held, wide)
    if fits:
        wave, twist, _ = tables(blocks)
        wave, back_wave = folded(wave)
        scratch = [pltpu.VMEM((blocks * 2 * GROUP, 3 * ROW), jnp.bfloat16)] * 2
        scratch += [pltpu.VMEM((blocks * 2 * GROUP, ROW), jnp.float32)] * 2
        large = pltpu.CompilerParams(vmem_limit_bytes=VMEM_BYTES)
        gated = pl.pallas_call(
            gated_spectrum_kernel,
            out_shape=jax.ShapeDtypeStruct((blocks, 2, own, ROW), jnp.float32),
            scratch_shapes=[pltpu.VMEM((blocks, own, ROW), jnp.float32)] + scratch,
            compiler_params=large,
            cost_estimate=cost(2**32, 2**24),
            name="gated_spectrum",
        )(gated, wave, twist)
        convolved = pl.pallas_call(
            conv_kernel,
            out_shape=jax.ShapeDtypeStruct((blocks, own, ROW), jnp.bfloat16),
            in_specs=[pl.BlockSpec(memory_space=pltpu.VMEM)] * (groups + 4),
            out_specs=far,
            scratch_shapes=[
                pltpu.VMEM((blocks, own, ROW), jnp.bfloat16),
                pltpu.VMEM((blocks, own, ROW), jnp.bfloat16),
                pltpu.SemaphoreType.DMA((own // GROUP,)),
            ]
            + scratch * 2,
            compiler_params=large,
            cost_estimate=cost(2**32, 2**24),
            name="convolve",
        )(gated, *taps, wave, back_wave, twist)
    else:
        gated = decode(gated, 1).reshape(blocks, ROW, own)
        taps = jnp.transpose(decode(taps, 2), (1, 0, 2)).reshape(own, blocks, ROW)
        convolved = plain_conv(jnp.transpose(gated, (0, 2, 1)), jnp.transpose(taps, (1, 0, 2)))
        convolved = jnp.transpose(convolved, (1, 0, 2)).reshape(own, groups, -1)
        convolved = encode(jnp.transpose(convolved, (1, 0, 2)), 2)
    convolved = exchange(convolved, "seq")
    if fits:
        queries = pl.pallas_call(
            turn_kernel,
            out_shape=jax.ShapeDtypeStruct((wide, ROW), jnp.bfloat16),
            scratch_shapes=[pltpu.VMEM((ROW, wide), jnp.float32)],
            compiler_params=small,
            cost_estimate=cost(2**20, 2**21),
            name="turn_queries",
        )(*queries)
        return pl.pallas_call(
            mix_kernel,
            out_specs=far,
            out_shape=jax.ShapeDtypeStruct((wide, ROW), jnp.bfloat16),
            scratch_shapes=[
                pltpu.VMEM((wide, ROW), jnp.bfloat16),
                pltpu.SemaphoreType.DMA((groups,)),
            ],
            compiler_params=small,
            name="mix_out",
        )(queries, convolved)
    queries = jnp.transpose(queries.astype(jnp.float32))
    return (queries * decode(convolved, 2).reshape(wide, -1)).astype(jnp.bfloat16)


def cost(flops, moved):
    return pl.CostEstimate(flops=int(flops), bytes_accessed=int(moved), transcendentals=0)


def solution(mesh):
    placed = (P(("seq", "ch"), None, None), P("ch", "seq"), P("ch"))
    return jax.shard_map(
        body, mesh=mesh, in_specs=placed, out_specs=P("ch", "seq"), check_vma=False
    )
```

```python
import functools
import math

import jax
import jax.numpy as jnp
import numpy as np
from jax import lax
from jax.experimental import pallas as pl
from jax.experimental.pallas import tpu as pltpu
from jax.sharding import PartitionSpec as P

GRID = 36.0
LOW_POWER = 125.0
EXPONENT_BITS = 8
EXPONENT_BIAS = 127.0
LANES = 128
ROW = 256
CHUNK = 16
GROUP = 16
VMEM_BYTES = 20 * 1024 * 1024
SMALL_BYTES = 12 * 1024 * 1024
ALL_BYTES = 60 * 1024 * 1024


def split_first(values, axis):
    count = min(values.shape[axis], LANES if axis == values.ndim - 1 else EXPONENT_BITS)
    first = lax.slice_in_dim(values, 0, count, axis=axis)
    if count == values.shape[axis]:
        return first, None
    return first, lax.slice_in_dim(values, count, values.shape[axis], axis=axis)


def scale_of(peak):
    power = jnp.floor(jnp.log(jnp.maximum(peak, 1e-30)) * (1.0 / math.log(2.0))) + 1.0
    return jnp.clip(power, -100.0, 126.0)


def exponent_bits(power, shape, axis):
    place = lax.broadcasted_iota(jnp.int32, shape, axis).astype(jnp.float32)
    bits = (power + (EXPONENT_BIAS + 0.25)) * jnp.exp2(-1.0 - place)
    return jnp.where(bits - jnp.floor(bits) >= 0.5, 0.5, 0.0), place < EXPONENT_BITS


def encode(values, axis):
    peak = jnp.max(jnp.abs(values), axis=axis, keepdims=True)
    return encode_all([values], scale_of(peak), axis)[0]


def encode_all(blocks, power, axis):
    unit_share, codes, bits = jnp.exp2(-power), [], None
    top = 2.0 * LOW_POWER
    for values in blocks:
        share = jnp.abs(values) * unit_share
        place = jnp.minimum(
            jnp.minimum(share * (2.0 * top) - LOW_POWER, share * top - LOW_POWER / 2),
            jnp.minimum(share * LOW_POWER, LOW_POWER + 1.0),
        )
        first, rest = split_first(place, axis)
        bits = exponent_bits(power, first.shape, axis) if bits is None else bits
        odd, holds = bits
        if axis == values.ndim - 1:
            marked = (jnp.floor(first * GRID - odd + 0.5) + odd) * (1.0 / GRID)
            first = jnp.exp2(jnp.where(holds, marked, first))
        else:
            marked = (jnp.floor(first * 64.0 - odd + 0.5) + odd) * (1.0 / 64.0)
            octave = jnp.floor(marked)
            first = jnp.exp2(octave) * (marked - octave + 1.0)
        size = first
        if rest is not None:
            size = jnp.concatenate([first, jnp.exp2(rest)], axis=axis)
        codes.append(jnp.where(values < 0.0, -size, size).astype(jnp.bfloat16))
    return codes


def decode(code, axis, halvings=0):
    code = code.astype(jnp.float32)
    size = jnp.abs(code)
    place = jnp.log(size) * (1.0 / math.log(2.0))
    first, rest = split_first(place, axis)
    if axis == code.ndim - 1:
        half = first * GRID + 0.25
    else:
        octave = jnp.floor(first + 0.002)
        first = octave + split_first(size, axis)[0] * jnp.exp2(-octave) - 1.0
        half = first * 64.0 + 0.25
        place = first if rest is None else jnp.concatenate([first, rest], axis=axis)
    spot = lax.broadcasted_iota(jnp.int32, first.shape, axis).astype(jnp.float32)
    weight = jnp.where(spot < EXPONENT_BITS, jnp.exp2(spot), 0.0)
    held = jnp.where(half - jnp.floor(half) >= 0.5, weight, 0.0)
    scale = jnp.exp2(jnp.sum(held, axis=axis, keepdims=True) - (EXPONENT_BIAS + halvings))
    step = 0.25 / LOW_POWER
    share = jnp.maximum(
        place * (4.0 * step), jnp.maximum(place * (2.0 * step) + 0.25, place * step + 0.25)
    )
    return jnp.where(code < 0.0, -scale, scale) * share


def tables(blocks):
    n2 = np.arange(ROW)
    k1 = np.arange(blocks)
    main = 2.0 * np.pi * np.outer(n2, n2 + 0.5) / ROW
    twist = 2.0 * np.pi * np.outer(k1 + 0.25 - blocks / 2, n2) / (blocks * ROW)
    mix = 2.0 * np.pi * np.outer(k1 + 0.25, np.arange(blocks)) / blocks
    wave = np.stack([np.cos(main), np.sin(main)]).astype(np.float32)
    twist = np.stack([np.cos(twist), np.sin(twist)], axis=1).astype(np.float32)
    mix = np.stack([np.cos(mix), np.sin(mix)], axis=0).astype(np.float32)
    return wave, twist, mix


def folded(wave):
    half = np.concatenate([wave[0, :, :LANES], wave[1, :, :LANES]], axis=1)
    parts = []
    for values in (half, half.T):
        high = values.astype(jnp.bfloat16)
        low = (values - high.astype(np.float32)).astype(jnp.bfloat16)
        parts.append(np.concatenate([high, low, high], axis=0))
    return parts


def put_split(ref, at, values):
    high = values.astype(jnp.bfloat16)
    ref[pl.ds(at, values.shape[0]), 0:ROW] = high
    ref[pl.ds(at, values.shape[0]), ROW : 2 * ROW] = high
    ref[pl.ds(at, values.shape[0]), 2 * ROW : 3 * ROW] = (
        values - high.astype(jnp.float32)
    ).astype(jnp.bfloat16)


def eighth(value, sign):
    re, im = value
    side = math.sqrt(0.5)
    return (re - sign * im) * side, (im + sign * re) * side


def four_points(values, sign):
    (a_re, a_im), (b_re, b_im), (c_re, c_im), (d_re, d_im) = values
    sum_re, sum_im, gap_re, gap_im = a_re + c_re, a_im + c_im, a_re - c_re, a_im - c_im
    more_re, more_im = b_re + d_re, b_im + d_im
    side_re, side_im = sign * (d_im - b_im), sign * (b_re - d_re)
    return (
        (sum_re + more_re, sum_im + more_im),
        (gap_re + side_re, gap_im + side_im),
        (sum_re - more_re, sum_im - more_im),
        (gap_re - side_re, gap_im - side_im),
    )


def row_of(k, part, at):
    return (2 * k + part) * GROUP + at


def eight_points(values, sign):
    sums = [(a_re + b_re, a_im + b_im) for (a_re, a_im), (b_re, b_im) in zip(values, values[4:])]
    gaps = [(a_re - b_re, a_im - b_im) for (a_re, a_im), (b_re, b_im) in zip(values, values[4:])]
    (two_re, two_im), three = gaps[2], eighth(gaps[3], sign)
    turned = [gaps[0], eighth(gaps[1], sign), (-sign * two_im, sign * two_re)]
    turned.append((-sign * three[1], sign * three[0]))
    places = [None] * 8
    places[0::2] = four_points(sums, sign)
    places[1::2] = four_points(turned, sign)
    return places


def mix_forward(taken, twist_ref, at, ref):
    angles = [math.pi * n / 16 for n in range(8)]
    turned = [
        (value * math.cos(angle), value * -math.sin(angle)) if angle else (value, 0.0)
        for value, angle in zip(taken, angles)
    ]
    for k, (re, im) in enumerate(eight_points(turned, -1.0)):
        cos_twist, sin_twist = twist_ref[k, 0:1, :], twist_ref[k, 1:2, :]
        put_split(ref, row_of(k, 0, at), re * cos_twist + im * sin_twist)
        put_split(ref, row_of(k, 1, at), im * cos_twist - re * sin_twist)


def mix_back(spectra, twist_ref):
    twisted = []
    for k, (re, im) in enumerate(spectra):
        cos_twist, sin_twist = twist_ref[k, 0:1, :], twist_ref[k, 1:2, :]
        twisted.append((re * cos_twist - im * sin_twist, im * cos_twist + re * sin_twist))
    totals = []
    for n, (re, im) in enumerate(eight_points(twisted, 1.0)):
        angle = math.pi * n / 16
        totals.append(re * math.cos(angle) - im * math.sin(angle) if n else re)
    return totals


def spectrum_rows(waves_ref, k, at):
    re = waves_ref[pl.ds(row_of(k, 0, at), CHUNK), :]
    im = waves_ref[pl.ds(row_of(k, 1, at), CHUNK), :]
    return re, im


def send_kernel(streams_ref, gated_ref, keys, values, codes, in_sems, out_sems):
    groups, parts = gated_ref.shape[:2]
    per = groups
    width = per * LANES
    arrivals = []
    for chunk in range(parts):
        lanes = pl.ds(chunk * width, width)
        for stream, buffer in ((1, keys), (2, values)):
            copy = pltpu.make_async_copy(
                streams_ref.at[stream, :, lanes], buffer.at[chunk], in_sems.at[stream - 1, chunk]
            )
            copy.start()
            arrivals.append(copy)
    copies = []
    for chunk in range(parts):
        for copy in arrivals[2 * chunk : 2 * chunk + 2]:
            copy.wait()
        part, first = chunk, 0
        for block in range(per):
            lanes = slice(block * LANES, (block + 1) * LANES)
            left = keys[chunk, :, lanes].astype(jnp.float32)
            right = values[chunk, :, lanes].astype(jnp.float32)
            codes[first + block, part] = encode(left * right, 0)
        place = (pl.ds(first, per), part)
        copy = pltpu.make_async_copy(codes.at[place], gated_ref.at[place], out_sems.at[chunk])
        copy.start()
        copies.append(copy)
    for copy in copies:
        copy.wait()


def query_kernel(streams_ref, *refs):
    query_refs, sems = refs[:-1], refs[-1]
    me = lax.axis_index("ch")
    wide = query_refs[0].shape[1]
    copies = []
    for turn, query_ref in enumerate(query_refs):
        lanes = pl.ds(pl.multiple_of((me ^ turn) * wide, wide), wide)
        copy = pltpu.make_async_copy(streams_ref.at[0, :, lanes], query_ref, sems.at[turn])
        copy.start()
        copies.append(copy)
    for copy in copies:
        copy.wait()


def taps_kernel(taps_ref, skip_ref, *code_refs):
    me = lax.axis_index("seq")
    first = (me == 0).astype(jnp.float32)
    row = lax.broadcasted_iota(jnp.int32, (LANES, LANES), 0)
    lane = lax.broadcasted_iota(jnp.int32, (LANES, LANES), 1)
    for turn, code_ref in enumerate(code_refs):
        block = me ^ turn
        gains = jnp.broadcast_to(skip_ref[pl.ds(block, 1), :], (LANES, LANES))
        gain = jnp.sum(jnp.where(row == lane, gains, 0.0), axis=1, keepdims=True) * first
        start = taps_ref[block, :, :LANES] + jnp.where(lane == 0, gain, 0.0)
        taps = jnp.concatenate([start, taps_ref[block, :, LANES:]], axis=1)
        code_ref[...] = encode(taps, 1)


def combined(waves_ref, k, at):
    re, im = spectrum_rows(waves_ref, k, at)
    re_cos, re_sin, im_cos, im_sin = re[:, :LANES], re[:, LANES:], im[:, :LANES], im[:, LANES:]
    return (
        jnp.concatenate([re_cos + im_sin, re_cos - im_sin], axis=1),
        jnp.concatenate([im_cos - re_sin, im_cos + re_sin], axis=1),
    )


def put_folded(ref, k, at, re, im):
    near_re, far_re, near_im, far_im = re[:, :LANES], re[:, LANES:], im[:, :LANES], im[:, LANES:]
    back_re = jnp.concatenate([near_re + far_re, far_im - near_im], axis=1)
    back_im = jnp.concatenate([near_im + far_im, near_re - far_re], axis=1)
    put_split(ref, row_of(k, 0, at), back_re)
    put_split(ref, row_of(k, 1, at), back_im)


def multiply(source, wave_ref, target):
    target[...] = jnp.dot(source[...], wave_ref[...], preferred_element_type=jnp.float32)


def row_groups():
    return [range(first, first + GROUP, CHUNK) for first in range(0, LANES, GROUP)]


def gated_spectrum_kernel(gated_ref, wave_ref, twist_ref, out_ref, u, *scratch):
    rows, waves = scratch[0:2], scratch[2:4]
    blocks = u.shape[0]
    parts = ROW // gated_ref.shape[1]
    groups = row_groups()

    def unpack(block, _):
        pieces = [decode(gated_ref[block * parts + part], 0) for part in range(parts)]
        u[block] = jnp.transpose(jnp.concatenate(pieces, axis=0))
        return 0

    lax.fori_loop(0, blocks, unpack, 0)
    for step in range(len(groups) + 2):
        if 0 <= step - 1 < len(groups):
            multiply(rows[(step - 1) % 2], wave_ref, waves[(step - 1) % 2])
        if step < len(groups):
            for at in groups[step]:
                taken = [u[n1, at : at + CHUNK, :] for n1 in range(blocks)]
                mix_forward(taken, twist_ref, at % GROUP, rows[step % 2])
        if step >= 2:
            for at in groups[step - 2]:
                for k in range(blocks):
                    re, im = combined(waves[step % 2], k, at % GROUP)
                    out_ref[k, 0, at : at + CHUNK, :] = re
                    out_ref[k, 1, at : at + CHUNK, :] = im


def conv_kernel(gated_ref, *refs):
    blocks = gated_ref.shape[0]
    wave_ref, back_wave_ref, twist_ref, out_ref, codes, out, sems, *scratch = refs[blocks:]
    rows, waves, back_rows, back_waves = (scratch[at : at + 2] for at in (0, 2, 4, 6))
    scale = math.log2(blocks * ROW)
    me = lax.axis_index("seq")
    groups = row_groups()
    for turn, code_ref in enumerate(refs[:blocks]):
        codes[me ^ turn] = code_ref[...]

    def forward(at, half):
        taken = [decode(codes[n1, at : at + CHUNK, :], 1, scale) for n1 in range(blocks)]
        mix_forward(taken, twist_ref, at % GROUP, rows[half])

    def product(at, half):
        for k in range(blocks):
            re, im = combined(waves[half], k, at % GROUP)
            gated_re = gated_ref[k, 0, at : at + CHUNK, :]
            gated_im = gated_ref[k, 1, at : at + CHUNK, :]
            product_re, product_im = re * gated_re - im * gated_im, re * gated_im + im * gated_re
            put_folded(back_rows[half], k, at % GROUP, product_re, product_im)

    def back(at, half):
        spectra = [spectrum_rows(back_waves[half], k, at % GROUP) for k in range(blocks)]
        totals = mix_back(spectra, twist_ref)
        sizes = [jnp.abs(total) for total in totals]
        peak = jnp.max(functools.reduce(jnp.maximum, sizes), axis=1, keepdims=True)
        for n1, code in enumerate(encode_all(totals, scale_of(peak), 1)):
            out[n1, at : at + CHUNK, :] = code

    copies = []
    for step in range(len(groups) + 4):
        if 0 <= step - 1 < len(groups):
            multiply(rows[(step - 1) % 2], wave_ref, waves[(step - 1) % 2])
        if 0 <= step - 3 < len(groups):
            multiply(back_rows[(step - 3) % 2], back_wave_ref, back_waves[(step - 3) % 2])
        for work, delay in ((forward, 0), (product, 2), (back, 4)):
            if 0 <= step - delay < len(groups):
                for at in groups[step - delay]:
                    work(at, step % 2)
        if step >= 4:
            place = pl.ds((step - 4) * GROUP, GROUP)
            copy = pltpu.make_async_copy(
                out.at[:, place, :], out_ref.at[:, place, :], sems.at[step - 4]
            )
            copy.start()
            copies.append(copy)
    for copy in copies:
        copy.wait()


def turn_kernel(*refs):
    query_refs, out_ref, whole = refs[:-2], refs[-2], refs[-1]
    me = lax.axis_index("ch")
    held = query_refs[0].shape[0]
    for turn, query_ref in enumerate(query_refs):
        at = pl.multiple_of((me ^ turn) * held, held)
        whole[pl.ds(at, held), :] = query_ref[...].astype(jnp.float32)
    out_ref[...] = jnp.transpose(whole[...]).astype(jnp.bfloat16)


def mix_kernel(query_ref, conv_ref, out_ref, mixed, sems):
    copies = []
    for block in range(conv_ref.shape[0]):
        at = pl.ds(block * LANES, LANES)
        queries = query_ref[at, :].astype(jnp.float32)
        mixed[at, :] = (queries * decode(conv_ref[block], 1)).astype(jnp.bfloat16)
        copy = pltpu.make_async_copy(mixed.at[at], out_ref.at[at], sems.at[block])
        copy.start()
        copies.append(copy)
    for copy in copies:
        copy.wait()


def plain_conv(gated, taps):
    blocks = gated.shape[0]
    (cos, sin), twist, mix = tables(blocks)
    cos_twist, sin_twist = twist[:, 0][:, None, :], twist[:, 1][:, None, :]
    dot = functools.partial(jnp.einsum, precision=lax.Precision.HIGHEST)

    def forward(values):
        re = dot("ncm,kn->kcm", values, mix[0])
        im = -dot("ncm,kn->kcm", values, mix[1])
        re, im = re * cos_twist + im * sin_twist, im * cos_twist - re * sin_twist
        return (
            dot("kcm,mq->kcq", re, cos) + dot("kcm,mq->kcq", im, sin),
            dot("kcm,mq->kcq", im, cos) - dot("kcm,mq->kcq", re, sin),
        )

    u_re, u_im = forward(gated)
    h_re, h_im = forward(taps)
    re, im = u_re * h_re - u_im * h_im, u_re * h_im + u_im * h_re
    re, im = (
        dot("kcq,mq->kcm", re, cos) - dot("kcq,mq->kcm", im, sin),
        dot("kcq,mq->kcm", im, cos) + dot("kcq,mq->kcm", re, sin),
    )
    re, im = re * cos_twist - im * sin_twist, im * cos_twist + re * sin_twist
    total = dot("kcm,kn->ncm", re, mix[0]) - dot("kcm,kn->ncm", im, mix[1])
    return total * (1.0 / (blocks * ROW))


def scatter(blocks, axis):
    count = len(blocks)
    return [
        lax.ppermute(block, axis, [(i, i ^ turn) for i in range(count)]) if turn else block
        for turn, block in enumerate(blocks)
    ]


def body(streams, filter_taps, skip_gain):
    groups, parts = lax.axis_size("seq"), lax.axis_size("ch")
    held, _, channels = streams.shape
    wide = channels // parts
    own = wide // groups
    blocks = filter_taps.shape[1] * groups // ROW
    streams = jnp.transpose(streams, (1, 0, 2))
    fits = blocks == 8 and own == LANES and filter_taps.shape[1] == ROW and ROW % held == 0 and groups % 4 == 0
    fits = fits and groups & (groups - 1) == 0 and parts & (parts - 1) == 0
    small = pltpu.CompilerParams(vmem_limit_bytes=SMALL_BYTES)
    if fits:
        far = pl.BlockSpec(memory_space=pl.ANY)
        coded = (groups, parts, held, own)
        stream = pltpu.VMEM((parts, held, wide), jnp.bfloat16)
        gated = pl.pallas_call(
            send_kernel,
            in_specs=[far],
            out_specs=far,
            out_shape=jax.ShapeDtypeStruct(coded, jnp.bfloat16),
            scratch_shapes=[
                stream,
                stream,
                pltpu.VMEM(coded, jnp.bfloat16),
                pltpu.SemaphoreType.DMA((2, 2 * parts)),
                pltpu.SemaphoreType.DMA((2 * parts,)),
            ],
            compiler_params=pltpu.CompilerParams(vmem_limit_bytes=ALL_BYTES),
            cost_estimate=cost(2**25, 2**23),
            name="encode_gated",
        )(streams)
        queries = pl.pallas_call(
            query_kernel,
            in_specs=[far],
            out_specs=[far] * parts,
            out_shape=[jax.ShapeDtypeStruct((held, wide), jnp.bfloat16)] * parts,
            scratch_shapes=[pltpu.SemaphoreType.DMA((parts,))],
            compiler_params=small,
            cost_estimate=cost(2**10, 2**20),
            name="send_queries",
        )(streams)
        taps = pl.pallas_call(
            taps_kernel,
            out_shape=[jax.ShapeDtypeStruct((own, ROW), jnp.bfloat16)] * groups,
            compiler_params=small,
            cost_estimate=cost(2**25, 2**23),
            name="encode_taps",
        )(filter_taps.reshape(groups, own, ROW), skip_gain.reshape(groups, own))
    else:
        gated = encode(streams[1].astype(jnp.float32) * streams[2].astype(jnp.float32), 0)
        gated = jnp.transpose(gated.reshape(held, parts, groups, own), (2, 1, 0, 3))
        queries = jnp.transpose(streams[0].reshape(held, parts, wide), (1, 0, 2))
        first = lax.axis_index("seq") == 0
        taps = filter_taps.at[:, 0].add(jnp.where(first, skip_gain, 0.0))
        taps = encode(taps, 1).reshape(groups, own, -1)
    exchange = functools.partial(lax.all_to_all, split_axis=0, concat_axis=0, tiled=True)
    gated = gated.reshape(groups * parts, held, own)
    if fits:
        taps = scatter(taps, "seq")
        gated = exchange(gated, ("seq", "ch"))
        queries = scatter(queries, "ch")
    else:
        taps = exchange(taps, "seq")
        gated = exchange(gated, ("seq", "ch"))
        queries = exchange(queries, "ch").reshape(parts * held, wide)
    if fits:
        wave, twist, _ = tables(blocks)
        wave, back_wave = folded(wave)
        scratch = [pltpu.VMEM((blocks * 2 * GROUP, 3 * ROW), jnp.bfloat16)] * 2
        scratch += [pltpu.VMEM((blocks * 2 * GROUP, ROW), jnp.float32)] * 2
        large = pltpu.CompilerParams(vmem_limit_bytes=VMEM_BYTES)
        gated = pl.pallas_call(
            gated_spectrum_kernel,
            out_shape=jax.ShapeDtypeStruct((blocks, 2, own, ROW), jnp.float32),
            scratch_shapes=[pltpu.VMEM((blocks, own, ROW), jnp.float32)] + scratch,
            compiler_params=large,
            cost_estimate=cost(2**32, 2**24),
            name="gated_spectrum",
        )(gated, wave, twist)
        convolved = pl.pallas_call(
            conv_kernel,
            out_shape=jax.ShapeDtypeStruct((blocks, own, ROW), jnp.bfloat16),
            in_specs=[pl.BlockSpec(memory_space=pltpu.VMEM)] * (groups + 4),
            out_specs=far,
            scratch_shapes=[
                pltpu.VMEM((blocks, own, ROW), jnp.bfloat16),
                pltpu.VMEM((blocks, own, ROW), jnp.bfloat16),
                pltpu.SemaphoreType.DMA((own // GROUP,)),
            ]
            + scratch * 2,
            compiler_params=large,
            cost_estimate=cost(2**32, 2**24),
            name="convolve",
        )(gated, *taps, wave, back_wave, twist)
    else:
        gated = decode(gated, 1).reshape(blocks, ROW, own)
        taps = jnp.transpose(decode(taps, 2), (1, 0, 2)).reshape(own, blocks, ROW)
        convolved = plain_conv(jnp.transpose(gated, (0, 2, 1)), jnp.transpose(taps, (1, 0, 2)))
        convolved = jnp.transpose(convolved, (1, 0, 2)).reshape(own, groups, -1)
        convolved = encode(jnp.transpose(convolved, (1, 0, 2)), 2)
    convolved = exchange(convolved, "seq")
    if fits:
        queries = pl.pallas_call(
            turn_kernel,
            out_shape=jax.ShapeDtypeStruct((wide, ROW), jnp.bfloat16),
            scratch_shapes=[pltpu.VMEM((ROW, wide), jnp.float32)],
            compiler_params=small,
            cost_estimate=cost(2**20, 2**21),
            name="turn_queries",
        )(*queries)
        return pl.pallas_call(
            mix_kernel,
            out_specs=far,
            out_shape=jax.ShapeDtypeStruct((wide, ROW), jnp.bfloat16),
            scratch_shapes=[
                pltpu.VMEM((wide, ROW), jnp.bfloat16),
                pltpu.SemaphoreType.DMA((groups,)),
            ],
            compiler_params=small,
            name="mix_out",
        )(queries, convolved)
    queries = jnp.transpose(queries.astype(jnp.float32))
    return (queries * decode(convolved, 2).reshape(wide, -1)).astype(jnp.bfloat16)


def cost(flops, moved):
    return pl.CostEstimate(flops=int(flops), bytes_accessed=int(moved), transcendentals=0)


def solution(mesh):
    placed = (P(("seq", "ch"), None, None), P("ch", "seq"), P("ch"))
    return jax.shard_map(
        body, mesh=mesh, in_specs=placed, out_specs=P("ch", "seq"), check_vma=False
    )
```

```python
import functools
import math

import jax
import jax.numpy as jnp
import numpy as np
from jax import lax
from jax.experimental import pallas as pl
from jax.experimental.pallas import tpu as pltpu
from jax.sharding import PartitionSpec as P

GRID = 36.0
LOW_POWER = 125.0
EXPONENT_BITS = 8
EXPONENT_BIAS = 127.0
LANES = 128
ROW = 256
CHUNK = 16
GROUP = 16
VMEM_BYTES = 20 * 1024 * 1024
SMALL_BYTES = 12 * 1024 * 1024
ALL_BYTES = 60 * 1024 * 1024


def split_marked(values, axis):
    extent = values.shape[axis]
    if axis == values.ndim - 1:
        cut = max(extent - LANES, 0)
        marked = lax.slice_in_dim(values, cut, extent, axis=axis)
        return marked, lax.slice_in_dim(values, 0, cut, axis=axis) if cut else None
    cut = min(extent, EXPONENT_BITS)
    marked = lax.slice_in_dim(values, 0, cut, axis=axis)
    return marked, lax.slice_in_dim(values, cut, extent, axis=axis) if cut < extent else None


def join_marked(marked, rest, axis):
    if rest is None:
        return marked
    return jnp.concatenate([rest, marked] if axis == rest.ndim - 1 else [marked, rest], axis=axis)


def bit_place(shape, axis):
    place = lax.broadcasted_iota(jnp.int32, shape, axis) - (shape[axis] - EXPONENT_BITS)
    return place.astype(jnp.float32)


def scale_of(peak):
    power = jnp.floor(jnp.log(jnp.maximum(peak, 1e-30)) * (1.0 / math.log(2.0))) + 1.0
    return jnp.clip(power, -100.0, 126.0)


def exponent_bits(power, shape, axis):
    place = bit_place(shape, axis)
    bits = (power + (EXPONENT_BIAS + 0.25)) * jnp.exp2(-1.0 - jnp.maximum(place, 0.0))
    return jnp.where(bits - jnp.floor(bits) >= 0.5, 0.5, 0.0), place >= 0.0


def encode(values, axis):
    peak = jnp.max(jnp.abs(values), axis=axis, keepdims=True)
    return encode_all([values], scale_of(peak), axis)[0]


def encode_all(blocks, power, axis):
    unit_share, codes, bits = jnp.exp2(-power), [], None
    top = 2.0 * LOW_POWER
    for values in blocks:
        share = jnp.abs(values) * unit_share
        place = jnp.minimum(
            jnp.minimum(share * (2.0 * top) - LOW_POWER, share * top - LOW_POWER / 2),
            jnp.minimum(share * LOW_POWER, LOW_POWER + 1.0),
        )
        first, rest = split_marked(place, axis)
        bits = exponent_bits(power, first.shape, axis) if bits is None else bits
        odd, holds = bits
        if axis == values.ndim - 1:
            marked = (jnp.floor(first * GRID - odd + 0.5) + odd) * (1.0 / GRID)
            first = jnp.exp2(jnp.where(holds, marked, first))
        else:
            marked = (jnp.floor(first * 64.0 - odd + 0.5) + odd) * (1.0 / 64.0)
            octave = jnp.floor(marked)
            first = jnp.exp2(octave) * (marked - octave + 1.0)
        size = join_marked(first, None if rest is None else jnp.exp2(rest), axis)
        codes.append(jnp.where(values < 0.0, -size, size).astype(jnp.bfloat16))
    return codes


def decode(code, axis, halvings=0):
    code = code.astype(jnp.float32)
    size = jnp.abs(code)
    place = jnp.log(size) * (1.0 / math.log(2.0))
    first, rest = split_marked(place, axis)
    if axis == code.ndim - 1:
        half = first * GRID + 0.25
    else:
        octave = jnp.floor(first + 0.002)
        first = octave + split_marked(size, axis)[0] * jnp.exp2(-octave) - 1.0
        half = first * 64.0 + 0.25
        place = join_marked(first, rest, axis)
    spot = bit_place(first.shape, axis)
    weight = jnp.where(spot >= 0.0, jnp.exp2(spot), 0.0)
    held = jnp.where(half - jnp.floor(half) >= 0.5, weight, 0.0)
    scale = jnp.exp2(jnp.sum(held, axis=axis, keepdims=True) - (EXPONENT_BIAS + halvings))
    step = 0.25 / LOW_POWER
    share = jnp.maximum(
        place * (4.0 * step), jnp.maximum(place * (2.0 * step) + 0.25, place * step + 0.25)
    )
    return jnp.where(code < 0.0, -scale, scale) * share


def tables(blocks):
    n2 = np.arange(ROW)
    k1 = np.arange(blocks)
    main = 2.0 * np.pi * np.outer(n2, n2 + 0.5) / ROW
    twist = 2.0 * np.pi * np.outer(k1 + 0.25 - blocks / 2, n2) / (blocks * ROW)
    mix = 2.0 * np.pi * np.outer(k1 + 0.25, np.arange(blocks)) / blocks
    wave = np.stack([np.cos(main), np.sin(main)]).astype(np.float32)
    twist = np.stack([np.cos(twist), np.sin(twist)], axis=1).astype(np.float32)
    mix = np.stack([np.cos(mix), np.sin(mix)], axis=0).astype(np.float32)
    return wave, twist, mix


def folded(wave):
    half = np.concatenate([wave[0, :, :LANES], wave[1, :, :LANES]], axis=1)
    parts = []
    for values in (half, half.T):
        high = values.astype(jnp.bfloat16)
        low = (values - high.astype(np.float32)).astype(jnp.bfloat16)
        parts.append(np.concatenate([high, low, high], axis=0))
    return parts


def put_split(ref, at, values):
    high = values.astype(jnp.bfloat16)
    ref[pl.ds(at, values.shape[0]), 0:ROW] = high
    ref[pl.ds(at, values.shape[0]), ROW : 2 * ROW] = high
    ref[pl.ds(at, values.shape[0]), 2 * ROW : 3 * ROW] = (
        values - high.astype(jnp.float32)
    ).astype(jnp.bfloat16)


def eighth(value, sign):
    re, im = value
    side = math.sqrt(0.5)
    return (re - sign * im) * side, (im + sign * re) * side


def four_points(values, sign):
    (a_re, a_im), (b_re, b_im), (c_re, c_im), (d_re, d_im) = values
    sum_re, sum_im, gap_re, gap_im = a_re + c_re, a_im + c_im, a_re - c_re, a_im - c_im
    more_re, more_im = b_re + d_re, b_im + d_im
    side_re, side_im = sign * (d_im - b_im), sign * (b_re - d_re)
    return (
        (sum_re + more_re, sum_im + more_im),
        (gap_re + side_re, gap_im + side_im),
        (sum_re - more_re, sum_im - more_im),
        (gap_re - side_re, gap_im - side_im),
    )


def row_of(k, part, at):
    return (2 * k + part) * GROUP + at


def eight_points(values, sign):
    sums = [(a_re + b_re, a_im + b_im) for (a_re, a_im), (b_re, b_im) in zip(values, values[4:])]
    gaps = [(a_re - b_re, a_im - b_im) for (a_re, a_im), (b_re, b_im) in zip(values, values[4:])]
    (two_re, two_im), three = gaps[2], eighth(gaps[3], sign)
    turned = [gaps[0], eighth(gaps[1], sign), (-sign * two_im, sign * two_re)]
    turned.append((-sign * three[1], sign * three[0]))
    places = [None] * 8
    places[0::2] = four_points(sums, sign)
    places[1::2] = four_points(turned, sign)
    return places


def mix_forward(taken, twist_ref, at, ref):
    angles = [math.pi * n / 16 for n in range(8)]
    turned = [
        (value * math.cos(angle), value * -math.sin(angle)) if angle else (value, 0.0)
        for value, angle in zip(taken, angles)
    ]
    for k, (re, im) in enumerate(eight_points(turned, -1.0)):
        cos_twist, sin_twist = twist_ref[k, 0:1, :], twist_ref[k, 1:2, :]
        put_split(ref, row_of(k, 0, at), re * cos_twist + im * sin_twist)
        put_split(ref, row_of(k, 1, at), im * cos_twist - re * sin_twist)


def mix_back(spectra, twist_ref):
    twisted = []
    for k, (re, im) in enumerate(spectra):
        cos_twist, sin_twist = twist_ref[k, 0:1, :], twist_ref[k, 1:2, :]
        twisted.append((re * cos_twist - im * sin_twist, im * cos_twist + re * sin_twist))
    totals = []
    for n, (re, im) in enumerate(eight_points(twisted, 1.0)):
        angle = math.pi * n / 16
        totals.append(re * math.cos(angle) - im * math.sin(angle) if n else re)
    return totals


def spectrum_rows(waves_ref, k, at):
    re = waves_ref[pl.ds(row_of(k, 0, at), CHUNK), :]
    im = waves_ref[pl.ds(row_of(k, 1, at), CHUNK), :]
    return re, im


def send_kernel(streams_ref, gated_ref, keys, values, codes, in_sems, out_sems):
    groups, parts = gated_ref.shape[:2]
    per = groups
    width = per * LANES
    arrivals = []
    for chunk in range(parts):
        lanes = pl.ds(chunk * width, width)
        for stream, buffer in ((1, keys), (2, values)):
            copy = pltpu.make_async_copy(
                streams_ref.at[stream, :, lanes], buffer.at[chunk], in_sems.at[stream - 1, chunk]
            )
            copy.start()
            arrivals.append(copy)
    copies = []
    for chunk in range(parts):
        for copy in arrivals[2 * chunk : 2 * chunk + 2]:
            copy.wait()
        part, first = chunk, 0
        for block in range(per):
            lanes = slice(block * LANES, (block + 1) * LANES)
            left = keys[chunk, :, lanes].astype(jnp.float32)
            right = values[chunk, :, lanes].astype(jnp.float32)
            codes[first + block, part] = encode(left * right, 0)
        place = (pl.ds(first, per), part)
        copy = pltpu.make_async_copy(codes.at[place], gated_ref.at[place], out_sems.at[chunk])
        copy.start()
        copies.append(copy)
    for copy in copies:
        copy.wait()


def query_kernel(streams_ref, *refs):
    query_refs, sems = refs[:-1], refs[-1]
    me = lax.axis_index("ch")
    wide = query_refs[0].shape[1]
    copies = []
    for turn, query_ref in enumerate(query_refs):
        lanes = pl.ds(pl.multiple_of((me ^ turn) * wide, wide), wide)
        copy = pltpu.make_async_copy(streams_ref.at[0, :, lanes], query_ref, sems.at[turn])
        copy.start()
        copies.append(copy)
    for copy in copies:
        copy.wait()


def taps_kernel(taps_ref, skip_ref, *code_refs):
    me = lax.axis_index("seq")
    first = (me == 0).astype(jnp.float32)
    row = lax.broadcasted_iota(jnp.int32, (LANES, LANES), 0)
    lane = lax.broadcasted_iota(jnp.int32, (LANES, LANES), 1)
    for turn, code_ref in enumerate(code_refs):
        block = me ^ turn
        gains = jnp.broadcast_to(skip_ref[pl.ds(block, 1), :], (LANES, LANES))
        gain = jnp.sum(jnp.where(row == lane, gains, 0.0), axis=1, keepdims=True) * first
        start = taps_ref[block, :, :LANES] + jnp.where(lane == 0, gain, 0.0)
        taps = jnp.concatenate([start, taps_ref[block, :, LANES:]], axis=1)
        code_ref[...] = encode(taps, 1)


def combined(waves_ref, k, at):
    re, im = spectrum_rows(waves_ref, k, at)
    re_cos, re_sin, im_cos, im_sin = re[:, :LANES], re[:, LANES:], im[:, :LANES], im[:, LANES:]
    return (
        jnp.concatenate([re_cos + im_sin, re_cos - im_sin], axis=1),
        jnp.concatenate([im_cos - re_sin, im_cos + re_sin], axis=1),
    )


def put_folded(ref, k, at, re, im):
    near_re, far_re, near_im, far_im = re[:, :LANES], re[:, LANES:], im[:, :LANES], im[:, LANES:]
    back_re = jnp.concatenate([near_re + far_re, far_im - near_im], axis=1)
    back_im = jnp.concatenate([near_im + far_im, near_re - far_re], axis=1)
    put_split(ref, row_of(k, 0, at), back_re)
    put_split(ref, row_of(k, 1, at), back_im)


def multiply(source, wave_ref, target):
    target[...] = jnp.dot(source[...], wave_ref[...], preferred_element_type=jnp.float32)


def row_groups():
    return [range(first, first + GROUP, CHUNK) for first in range(0, LANES, GROUP)]


def gated_spectrum_kernel(gated_ref, wave_ref, twist_ref, out_ref, u, *scratch):
    rows, waves = scratch[0:2], scratch[2:4]
    blocks = u.shape[0]
    parts = ROW // gated_ref.shape[1]
    groups = row_groups()

    def unpack(block, _):
        pieces = [decode(gated_ref[block * parts + part], 0) for part in range(parts)]
        u[block] = jnp.transpose(jnp.concatenate(pieces, axis=0))
        return 0

    lax.fori_loop(0, blocks, unpack, 0)
    for step in range(len(groups) + 2):
        if 0 <= step - 1 < len(groups):
            multiply(rows[(step - 1) % 2], wave_ref, waves[(step - 1) % 2])
        if step < len(groups):
            for at in groups[step]:
                taken = [u[n1, at : at + CHUNK, :] for n1 in range(blocks)]
                mix_forward(taken, twist_ref, at % GROUP, rows[step % 2])
        if step >= 2:
            for at in groups[step - 2]:
                for k in range(blocks):
                    re, im = combined(waves[step % 2], k, at % GROUP)
                    out_ref[k, 0, at : at + CHUNK, :] = re
                    out_ref[k, 1, at : at + CHUNK, :] = im


def conv_kernel(gated_ref, *refs):
    blocks = gated_ref.shape[0]
    wave_ref, back_wave_ref, twist_ref, out_ref, codes, out, sems, *scratch = refs[blocks:]
    rows, waves, back_rows, back_waves = (scratch[at : at + 2] for at in (0, 2, 4, 6))
    scale = math.log2(blocks * ROW)
    me = lax.axis_index("seq")
    groups = row_groups()
    for turn, code_ref in enumerate(refs[:blocks]):
        codes[me ^ turn] = code_ref[...]

    def forward(at, half):
        taken = [decode(codes[n1, at : at + CHUNK, :], 1, scale) for n1 in range(blocks)]
        mix_forward(taken, twist_ref, at % GROUP, rows[half])

    def product(at, half):
        for k in range(blocks):
            re, im = combined(waves[half], k, at % GROUP)
            gated_re = gated_ref[k, 0, at : at + CHUNK, :]
            gated_im = gated_ref[k, 1, at : at + CHUNK, :]
            product_re, product_im = re * gated_re - im * gated_im, re * gated_im + im * gated_re
            put_folded(back_rows[half], k, at % GROUP, product_re, product_im)

    def back(at, half):
        spectra = [spectrum_rows(back_waves[half], k, at % GROUP) for k in range(blocks)]
        totals = mix_back(spectra, twist_ref)
        sizes = [jnp.abs(total) for total in totals]
        peak = jnp.max(functools.reduce(jnp.maximum, sizes), axis=1, keepdims=True)
        for n1, code in enumerate(encode_all(totals, scale_of(peak), 1)):
            out[n1, at : at + CHUNK, :] = code

    copies = []
    for step in range(len(groups) + 4):
        if 0 <= step - 1 < len(groups):
            multiply(rows[(step - 1) % 2], wave_ref, waves[(step - 1) % 2])
        if 0 <= step - 3 < len(groups):
            multiply(back_rows[(step - 3) % 2], back_wave_ref, back_waves[(step - 3) % 2])
        for work, delay in ((forward, 0), (product, 2), (back, 4)):
            if 0 <= step - delay < len(groups):
                for at in groups[step - delay]:
                    work(at, step % 2)
        if step >= 4:
            place = pl.ds((step - 4) * GROUP, GROUP)
            copy = pltpu.make_async_copy(
                out.at[:, place, :], out_ref.at[:, place, :], sems.at[step - 4]
            )
            copy.start()
            copies.append(copy)
    for copy in copies:
        copy.wait()


def turn_kernel(*refs):
    query_refs, out_ref, whole = refs[:-2], refs[-2], refs[-1]
    me = lax.axis_index("ch")
    held = query_refs[0].shape[0]
    for turn, query_ref in enumerate(query_refs):
        at = pl.multiple_of((me ^ turn) * held, held)
        whole[pl.ds(at, held), :] = query_ref[...].astype(jnp.float32)
    out_ref[...] = jnp.transpose(whole[...]).astype(jnp.bfloat16)


def mix_kernel(query_ref, conv_ref, out_ref, mixed, sems):
    copies = []
    for block in range(conv_ref.shape[0]):
        at = pl.ds(block * LANES, LANES)
        queries = query_ref[at, :].astype(jnp.float32)
        mixed[at, :] = (queries * decode(conv_ref[block], 1)).astype(jnp.bfloat16)
        copy = pltpu.make_async_copy(mixed.at[at], out_ref.at[at], sems.at[block])
        copy.start()
        copies.append(copy)
    for copy in copies:
        copy.wait()


def plain_conv(gated, taps):
    blocks = gated.shape[0]
    (cos, sin), twist, mix = tables(blocks)
    cos_twist, sin_twist = twist[:, 0][:, None, :], twist[:, 1][:, None, :]
    dot = functools.partial(jnp.einsum, precision=lax.Precision.HIGHEST)

    def forward(values):
        re = dot("ncm,kn->kcm", values, mix[0])
        im = -dot("ncm,kn->kcm", values, mix[1])
        re, im = re * cos_twist + im * sin_twist, im * cos_twist - re * sin_twist
        return (
            dot("kcm,mq->kcq", re, cos) + dot("kcm,mq->kcq", im, sin),
            dot("kcm,mq->kcq", im, cos) - dot("kcm,mq->kcq", re, sin),
        )

    u_re, u_im = forward(gated)
    h_re, h_im = forward(taps)
    re, im = u_re * h_re - u_im * h_im, u_re * h_im + u_im * h_re
    re, im = (
        dot("kcq,mq->kcm", re, cos) - dot("kcq,mq->kcm", im, sin),
        dot("kcq,mq->kcm", im, cos) + dot("kcq,mq->kcm", re, sin),
    )
    re, im = re * cos_twist - im * sin_twist, im * cos_twist + re * sin_twist
    total = dot("kcm,kn->ncm", re, mix[0]) - dot("kcm,kn->ncm", im, mix[1])
    return total * (1.0 / (blocks * ROW))


def scatter(blocks, axis):
    count = len(blocks)
    return [
        lax.ppermute(block, axis, [(i, i ^ turn) for i in range(count)]) if turn else block
        for turn, block in enumerate(blocks)
    ]


def body(streams, filter_taps, skip_gain):
    groups, parts = lax.axis_size("seq"), lax.axis_size("ch")
    held, _, channels = streams.shape
    wide = channels // parts
    own = wide // groups
    blocks = filter_taps.shape[1] * groups // ROW
    streams = jnp.transpose(streams, (1, 0, 2))
    fits = blocks == 8 and own == LANES and filter_taps.shape[1] == ROW and ROW % held == 0 and groups % 4 == 0
    fits = fits and groups & (groups - 1) == 0 and parts & (parts - 1) == 0
    small = pltpu.CompilerParams(vmem_limit_bytes=SMALL_BYTES)
    if fits:
        far = pl.BlockSpec(memory_space=pl.ANY)
        coded = (groups, parts, held, own)
        stream = pltpu.VMEM((parts, held, wide), jnp.bfloat16)
        gated = pl.pallas_call(
            send_kernel,
            in_specs=[far],
            out_specs=far,
            out_shape=jax.ShapeDtypeStruct(coded, jnp.bfloat16),
            scratch_shapes=[
                stream,
                stream,
                pltpu.VMEM(coded, jnp.bfloat16),
                pltpu.SemaphoreType.DMA((2, 2 * parts)),
                pltpu.SemaphoreType.DMA((2 * parts,)),
            ],
            compiler_params=pltpu.CompilerParams(vmem_limit_bytes=ALL_BYTES),
            cost_estimate=cost(2**25, 2**23),
            name="encode_gated",
        )(streams)
        queries = pl.pallas_call(
            query_kernel,
            in_specs=[far],
            out_specs=[far] * parts,
            out_shape=[jax.ShapeDtypeStruct((held, wide), jnp.bfloat16)] * parts,
            scratch_shapes=[pltpu.SemaphoreType.DMA((parts,))],
            compiler_params=small,
            cost_estimate=cost(2**10, 2**20),
            name="send_queries",
        )(streams)
        taps = pl.pallas_call(
            taps_kernel,
            out_shape=[jax.ShapeDtypeStruct((own, ROW), jnp.bfloat16)] * groups,
            compiler_params=small,
            cost_estimate=cost(2**25, 2**23),
            name="encode_taps",
        )(filter_taps.reshape(groups, own, ROW), skip_gain.reshape(groups, own))
    else:
        gated = encode(streams[1].astype(jnp.float32) * streams[2].astype(jnp.float32), 0)
        gated = jnp.transpose(gated.reshape(held, parts, groups, own), (2, 1, 0, 3))
        queries = jnp.transpose(streams[0].reshape(held, parts, wide), (1, 0, 2))
        first = lax.axis_index("seq") == 0
        taps = filter_taps.at[:, 0].add(jnp.where(first, skip_gain, 0.0))
        taps = encode(taps, 1).reshape(groups, own, -1)
    exchange = functools.partial(lax.all_to_all, split_axis=0, concat_axis=0, tiled=True)
    gated = gated.reshape(groups * parts, held, own)
    if fits:
        taps = scatter(taps, "seq")
        gated = exchange(gated, ("seq", "ch"))
        queries = scatter(queries, "ch")
    else:
        taps = exchange(taps, "seq")
        gated = exchange(gated, ("seq", "ch"))
        queries = exchange(queries, "ch").reshape(parts * held, wide)
    if fits:
        wave, twist, _ = tables(blocks)
        wave, back_wave = folded(wave)
        scratch = [pltpu.VMEM((blocks * 2 * GROUP, 3 * ROW), jnp.bfloat16)] * 2
        scratch += [pltpu.VMEM((blocks * 2 * GROUP, ROW), jnp.float32)] * 2
        large = pltpu.CompilerParams(vmem_limit_bytes=VMEM_BYTES)
        gated = pl.pallas_call(
            gated_spectrum_kernel,
            out_shape=jax.ShapeDtypeStruct((blocks, 2, own, ROW), jnp.float32),
            scratch_shapes=[pltpu.VMEM((blocks, own, ROW), jnp.float32)] + scratch,
            compiler_params=large,
            cost_estimate=cost(2**32, 2**24),
            name="gated_spectrum",
        )(gated, wave, twist)
        convolved = pl.pallas_call(
            conv_kernel,
            out_shape=jax.ShapeDtypeStruct((blocks, own, ROW), jnp.bfloat16),
            in_specs=[pl.BlockSpec(memory_space=pltpu.VMEM)] * (groups + 4),
            out_specs=far,
            scratch_shapes=[
                pltpu.VMEM((blocks, own, ROW), jnp.bfloat16),
                pltpu.VMEM((blocks, own, ROW), jnp.bfloat16),
                pltpu.SemaphoreType.DMA((own // GROUP,)),
            ]
            + scratch * 2,
            compiler_params=large,
            cost_estimate=cost(2**32, 2**24),
            name="convolve",
        )(gated, *taps, wave, back_wave, twist)
    else:
        gated = decode(gated, 1).reshape(blocks, ROW, own)
        taps = jnp.transpose(decode(taps, 2), (1, 0, 2)).reshape(own, blocks, ROW)
        convolved = plain_conv(jnp.transpose(gated, (0, 2, 1)), jnp.transpose(taps, (1, 0, 2)))
        convolved = jnp.transpose(convolved, (1, 0, 2)).reshape(own, groups, -1)
        convolved = encode(jnp.transpose(convolved, (1, 0, 2)), 2)
    convolved = exchange(convolved, "seq")
    if fits:
        queries = pl.pallas_call(
            turn_kernel,
            out_shape=jax.ShapeDtypeStruct((wide, ROW), jnp.bfloat16),
            scratch_shapes=[pltpu.VMEM((ROW, wide), jnp.float32)],
            compiler_params=small,
            cost_estimate=cost(2**20, 2**21),
            name="turn_queries",
        )(*queries)
        return pl.pallas_call(
            mix_kernel,
            out_specs=far,
            out_shape=jax.ShapeDtypeStruct((wide, ROW), jnp.bfloat16),
            scratch_shapes=[
                pltpu.VMEM((wide, ROW), jnp.bfloat16),
                pltpu.SemaphoreType.DMA((groups,)),
            ],
            compiler_params=small,
            name="mix_out",
        )(queries, convolved)
    queries = jnp.transpose(queries.astype(jnp.float32))
    return (queries * decode(convolved, 2).reshape(wide, -1)).astype(jnp.bfloat16)


def cost(flops, moved):
    return pl.CostEstimate(flops=int(flops), bytes_accessed=int(moved), transcendentals=0)


def solution(mesh):
    placed = (P(("seq", "ch"), None, None), P("ch", "seq"), P("ch"))
    return jax.shard_map(
        body, mesh=mesh, in_specs=placed, out_specs=P("ch", "seq"), check_vma=False
    )
```

```python
import functools
import math

import jax
import jax.numpy as jnp
import numpy as np
from jax import lax
from jax.experimental import pallas as pl
from jax.experimental.pallas import tpu as pltpu
from jax.sharding import PartitionSpec as P

GRID = 36.0
LOW_POWER = 125.0
EXPONENT_BITS = 8
EXPONENT_BIAS = 127.0
LANES = 128
ROW = 256
CHUNK = 16
GROUP = 16
VMEM_BYTES = 20 * 1024 * 1024
SMALL_BYTES = 12 * 1024 * 1024
ALL_BYTES = 60 * 1024 * 1024


def split_marked(values, axis):
    extent = values.shape[axis]
    if axis == values.ndim - 1:
        cut = max(extent - LANES, 0)
        marked = lax.slice_in_dim(values, cut, extent, axis=axis)
        return marked, lax.slice_in_dim(values, 0, cut, axis=axis) if cut else None
    cut = min(extent, EXPONENT_BITS)
    marked = lax.slice_in_dim(values, 0, cut, axis=axis)
    return marked, lax.slice_in_dim(values, cut, extent, axis=axis) if cut < extent else None


def join_marked(marked, rest, axis):
    if rest is None:
        return marked
    return jnp.concatenate([rest, marked] if axis == rest.ndim - 1 else [marked, rest], axis=axis)


def bit_place(shape, axis):
    place = lax.broadcasted_iota(jnp.int32, shape, axis) - (shape[axis] - EXPONENT_BITS)
    return place.astype(jnp.float32)


def scale_of(peak):
    power = jnp.floor(jnp.log(jnp.maximum(peak, 1e-30)) * (1.0 / math.log(2.0))) + 1.0
    return jnp.clip(power, -100.0, 126.0)


def exponent_bits(power, shape, axis):
    place = bit_place(shape, axis)
    bits = (power + (EXPONENT_BIAS + 0.25)) * jnp.exp2(-1.0 - jnp.maximum(place, 0.0))
    return jnp.where(bits - jnp.floor(bits) >= 0.5, 0.5, 0.0), place >= 0.0


def encode(values, axis):
    peak = jnp.max(jnp.abs(values), axis=axis, keepdims=True)
    return encode_all([values], scale_of(peak), axis)[0]


def encode_all(blocks, power, axis):
    unit_share, codes, bits = jnp.exp2(-power), [], None
    top = 2.0 * LOW_POWER
    for values in blocks:
        share = jnp.abs(values) * unit_share
        place = jnp.minimum(
            jnp.minimum(share * (2.0 * top) - LOW_POWER, share * top - LOW_POWER / 2),
            jnp.minimum(share * LOW_POWER, LOW_POWER + 1.0),
        )
        first, rest = split_marked(place, axis)
        bits = exponent_bits(power, first.shape, axis) if bits is None else bits
        odd, holds = bits
        if axis == values.ndim - 1:
            marked = (jnp.floor(first * GRID - odd + 0.5) + odd) * (1.0 / GRID)
            first = jnp.exp2(jnp.where(holds, marked, first))
        else:
            marked = (jnp.floor(first * 64.0 - odd + 0.5) + odd) * (1.0 / 64.0)
            octave = jnp.floor(marked)
            first = jnp.exp2(octave) * (marked - octave + 1.0)
        size = join_marked(first, None if rest is None else jnp.exp2(rest), axis)
        codes.append(jnp.where(values < 0.0, -size, size).astype(jnp.bfloat16))
    return codes


def decode(code, axis, halvings=0):
    code = code.astype(jnp.float32)
    size = jnp.abs(code)
    place = jnp.log(size) * (1.0 / math.log(2.0))
    first, rest = split_marked(place, axis)
    if axis == code.ndim - 1:
        half = first * GRID + 0.25
    else:
        octave = jnp.floor(first + 0.002)
        first = octave + split_marked(size, axis)[0] * jnp.exp2(-octave) - 1.0
        half = first * 64.0 + 0.25
        place = join_marked(first, rest, axis)
    spot = bit_place(first.shape, axis)
    weight = jnp.where(spot >= 0.0, jnp.exp2(spot), 0.0)
    held = jnp.where(half - jnp.floor(half) >= 0.5, weight, 0.0)
    scale = jnp.exp2(jnp.sum(held, axis=axis, keepdims=True) - (EXPONENT_BIAS + halvings))
    step = 0.25 / LOW_POWER
    share = jnp.maximum(
        place * (4.0 * step), jnp.maximum(place * (2.0 * step) + 0.25, place * step + 0.25)
    )
    return jnp.where(code < 0.0, -scale, scale) * share


def tables(blocks):
    n2 = np.arange(ROW)
    k1 = np.arange(blocks)
    main = 2.0 * np.pi * np.outer(n2, n2 + 0.5) / ROW
    twist = 2.0 * np.pi * np.outer(k1 + 0.25 - blocks / 2, n2) / (blocks * ROW)
    mix = 2.0 * np.pi * np.outer(k1 + 0.25, np.arange(blocks)) / blocks
    wave = np.stack([np.cos(main), np.sin(main)]).astype(np.float32)
    twist = np.stack([np.cos(twist), np.sin(twist)], axis=1).astype(np.float32)
    mix = np.stack([np.cos(mix), np.sin(mix)], axis=0).astype(np.float32)
    return wave, twist, mix


def folded(wave):
    half = np.concatenate([wave[0, :, :LANES], wave[1, :, :LANES]], axis=1)
    parts = []
    for values in (half, half.T):
        high = values.astype(jnp.bfloat16)
        low = (values - high.astype(np.float32)).astype(jnp.bfloat16)
        parts.append(np.concatenate([high, low, high], axis=0))
    return parts


def put_split(ref, at, values):
    high = values.astype(jnp.bfloat16)
    ref[pl.ds(at, values.shape[0]), 0:ROW] = high
    ref[pl.ds(at, values.shape[0]), ROW : 2 * ROW] = high
    ref[pl.ds(at, values.shape[0]), 2 * ROW : 3 * ROW] = (
        values - high.astype(jnp.float32)
    ).astype(jnp.bfloat16)


def eighth(value, sign):
    re, im = value
    side = math.sqrt(0.5)
    return (re - sign * im) * side, (im + sign * re) * side


def four_points(values, sign):
    (a_re, a_im), (b_re, b_im), (c_re, c_im), (d_re, d_im) = values
    sum_re, sum_im, gap_re, gap_im = a_re + c_re, a_im + c_im, a_re - c_re, a_im - c_im
    more_re, more_im = b_re + d_re, b_im + d_im
    side_re, side_im = sign * (d_im - b_im), sign * (b_re - d_re)
    return (
        (sum_re + more_re, sum_im + more_im),
        (gap_re + side_re, gap_im + side_im),
        (sum_re - more_re, sum_im - more_im),
        (gap_re - side_re, gap_im - side_im),
    )


def row_of(k, part, at):
    return (2 * k + part) * GROUP + at


def eight_points(values, sign):
    sums = [(a_re + b_re, a_im + b_im) for (a_re, a_im), (b_re, b_im) in zip(values, values[4:])]
    gaps = [(a_re - b_re, a_im - b_im) for (a_re, a_im), (b_re, b_im) in zip(values, values[4:])]
    (two_re, two_im), three = gaps[2], eighth(gaps[3], sign)
    turned = [gaps[0], eighth(gaps[1], sign), (-sign * two_im, sign * two_re)]
    turned.append((-sign * three[1], sign * three[0]))
    places = [None] * 8
    places[0::2] = four_points(sums, sign)
    places[1::2] = four_points(turned, sign)
    return places


def mix_forward(taken, twist_ref, at, ref):
    angles = [math.pi * n / 16 for n in range(8)]
    turned = [
        (value * math.cos(angle), value * -math.sin(angle)) if angle else (value, 0.0)
        for value, angle in zip(taken, angles)
    ]
    for k, (re, im) in enumerate(eight_points(turned, -1.0)):
        cos_twist, sin_twist = twist_ref[k, 0:1, :], twist_ref[k, 1:2, :]
        put_split(ref, row_of(k, 0, at), re * cos_twist + im * sin_twist)
        put_split(ref, row_of(k, 1, at), im * cos_twist - re * sin_twist)


def mix_back(spectra, twist_ref):
    twisted = []
    for k, (re, im) in enumerate(spectra):
        cos_twist, sin_twist = twist_ref[k, 0:1, :], twist_ref[k, 1:2, :]
        twisted.append((re * cos_twist - im * sin_twist, im * cos_twist + re * sin_twist))
    totals = []
    for n, (re, im) in enumerate(eight_points(twisted, 1.0)):
        angle = math.pi * n / 16
        totals.append(re * math.cos(angle) - im * math.sin(angle) if n else re)
    return totals


def spectrum_rows(waves_ref, k, at):
    re = waves_ref[pl.ds(row_of(k, 0, at), CHUNK), :]
    im = waves_ref[pl.ds(row_of(k, 1, at), CHUNK), :]
    return re, im


def send_kernel(streams_ref, gated_ref, keys, values, codes, in_sems, out_sems):
    groups, parts = gated_ref.shape[:2]
    per = groups
    width = per * LANES
    arrivals = []
    for chunk in range(parts):
        lanes = pl.ds(chunk * width, width)
        for stream, buffer in ((1, keys), (2, values)):
            copy = pltpu.make_async_copy(
                streams_ref.at[stream, :, lanes], buffer.at[chunk], in_sems.at[stream - 1, chunk]
            )
            copy.start()
            arrivals.append(copy)
    copies = []
    for chunk in range(parts):
        for copy in arrivals[2 * chunk : 2 * chunk + 2]:
            copy.wait()
        part, first = chunk, 0
        for block in range(per):
            lanes = slice(block * LANES, (block + 1) * LANES)
            left = keys[chunk, :, lanes].astype(jnp.float32)
            right = values[chunk, :, lanes].astype(jnp.float32)
            codes[first + block, part] = encode(left * right, 0)
        place = (pl.ds(first, per), part)
        copy = pltpu.make_async_copy(codes.at[place], gated_ref.at[place], out_sems.at[chunk])
        copy.start()
        copies.append(copy)
    for copy in copies:
        copy.wait()


def query_kernel(streams_ref, *refs):
    query_refs, sems = refs[:-1], refs[-1]
    me = lax.axis_index("ch")
    wide = query_refs[0].shape[1]
    copies = []
    for turn, query_ref in enumerate(query_refs):
        lanes = pl.ds(pl.multiple_of((me ^ turn) * wide, wide), wide)
        copy = pltpu.make_async_copy(streams_ref.at[0, :, lanes], query_ref, sems.at[turn])
        copy.start()
        copies.append(copy)
    for copy in copies:
        copy.wait()


def taps_kernel(taps_ref, skip_ref, *code_refs):
    me = lax.axis_index("seq")
    first = (me == 0).astype(jnp.float32)
    row = lax.broadcasted_iota(jnp.int32, (LANES, LANES), 0)
    lane = lax.broadcasted_iota(jnp.int32, (LANES, LANES), 1)
    for turn, code_ref in enumerate(code_refs):
        block = me ^ turn
        gains = jnp.broadcast_to(skip_ref[pl.ds(block, 1), :], (LANES, LANES))
        gain = jnp.sum(jnp.where(row == lane, gains, 0.0), axis=1, keepdims=True) * first
        start = taps_ref[block, :, :LANES] + jnp.where(lane == 0, gain, 0.0)
        taps = jnp.concatenate([start, taps_ref[block, :, LANES:]], axis=1)
        code_ref[...] = encode(taps, 1)


def combined(waves_ref, k, at):
    re, im = spectrum_rows(waves_ref, k, at)
    re_cos, re_sin, im_cos, im_sin = re[:, :LANES], re[:, LANES:], im[:, :LANES], im[:, LANES:]
    return (
        jnp.concatenate([re_cos + im_sin, re_cos - im_sin], axis=1),
        jnp.concatenate([im_cos - re_sin, im_cos + re_sin], axis=1),
    )


def put_folded(ref, k, at, re, im):
    near_re, far_re, near_im, far_im = re[:, :LANES], re[:, LANES:], im[:, :LANES], im[:, LANES:]
    back_re = jnp.concatenate([near_re + far_re, far_im - near_im], axis=1)
    back_im = jnp.concatenate([near_im + far_im, near_re - far_re], axis=1)
    put_split(ref, row_of(k, 0, at), back_re)
    put_split(ref, row_of(k, 1, at), back_im)


def multiply(source, wave_ref, target):
    target[...] = jnp.dot(source[...], wave_ref[...], preferred_element_type=jnp.float32)


def row_groups():
    return [range(first, first + GROUP, CHUNK) for first in range(0, LANES, GROUP)]


def gated_spectrum_kernel(gated_ref, wave_ref, twist_ref, out_ref, u, *scratch):
    rows, waves = scratch[0:2], scratch[2:4]
    blocks = u.shape[0]
    parts = ROW // gated_ref.shape[1]
    groups = row_groups()

    def unpack(block, _):
        pieces = [decode(gated_ref[block * parts + part], 0) for part in range(parts)]
        u[block] = jnp.transpose(jnp.concatenate(pieces, axis=0))
        return 0

    lax.fori_loop(0, blocks, unpack, 0)
    for step in range(len(groups) + 2):
        if 0 <= step - 1 < len(groups):
            multiply(rows[(step - 1) % 2], wave_ref, waves[(step - 1) % 2])
        if step < len(groups):
            for at in groups[step]:
                taken = [u[n1, at : at + CHUNK, :] for n1 in range(blocks)]
                mix_forward(taken, twist_ref, at % GROUP, rows[step % 2])
        if step >= 2:
            for at in groups[step - 2]:
                for k in range(blocks):
                    re, im = combined(waves[step % 2], k, at % GROUP)
                    out_ref[k, 0, at : at + CHUNK, :] = re
                    out_ref[k, 1, at : at + CHUNK, :] = im


def conv_kernel(gated_ref, *refs):
    blocks = gated_ref.shape[0]
    wave_ref, back_wave_ref, twist_ref, out_ref, codes, out, sems, *scratch = refs[blocks:]
    rows, waves, back_rows, back_waves = (scratch[at : at + 2] for at in (0, 2, 4, 6))
    scale = math.log2(blocks * ROW)
    me = lax.axis_index("seq")
    groups = row_groups()
    for turn, code_ref in zip(turn_order(blocks), refs[:blocks]):
        codes[me ^ turn] = code_ref[...]

    def forward(at, half):
        taken = [decode(codes[n1, at : at + CHUNK, :], 1, scale) for n1 in range(blocks)]
        mix_forward(taken, twist_ref, at % GROUP, rows[half])

    def product(at, half):
        for k in range(blocks):
            re, im = combined(waves[half], k, at % GROUP)
            gated_re = gated_ref[k, 0, at : at + CHUNK, :]
            gated_im = gated_ref[k, 1, at : at + CHUNK, :]
            product_re, product_im = re * gated_re - im * gated_im, re * gated_im + im * gated_re
            put_folded(back_rows[half], k, at % GROUP, product_re, product_im)

    def back(at, half):
        spectra = [spectrum_rows(back_waves[half], k, at % GROUP) for k in range(blocks)]
        totals = mix_back(spectra, twist_ref)
        sizes = [jnp.abs(total) for total in totals]
        peak = jnp.max(functools.reduce(jnp.maximum, sizes), axis=1, keepdims=True)
        for n1, code in enumerate(encode_all(totals, scale_of(peak), 1)):
            out[n1, at : at + CHUNK, :] = code

    copies = []
    for step in range(len(groups) + 4):
        if 0 <= step - 1 < len(groups):
            multiply(rows[(step - 1) % 2], wave_ref, waves[(step - 1) % 2])
        if 0 <= step - 3 < len(groups):
            multiply(back_rows[(step - 3) % 2], back_wave_ref, back_waves[(step - 3) % 2])
        for work, delay in ((forward, 0), (product, 2), (back, 4)):
            if 0 <= step - delay < len(groups):
                for at in groups[step - delay]:
                    work(at, step % 2)
        if step >= 4:
            place = pl.ds((step - 4) * GROUP, GROUP)
            copy = pltpu.make_async_copy(
                out.at[:, place, :], out_ref.at[:, place, :], sems.at[step - 4]
            )
            copy.start()
            copies.append(copy)
    for copy in copies:
        copy.wait()


def turn_kernel(*refs):
    query_refs, out_ref, whole = refs[:-2], refs[-2], refs[-1]
    me = lax.axis_index("ch")
    held = query_refs[0].shape[0]
    for turn, query_ref in enumerate(query_refs):
        at = pl.multiple_of((me ^ turn) * held, held)
        whole[pl.ds(at, held), :] = query_ref[...].astype(jnp.float32)
    out_ref[...] = jnp.transpose(whole[...]).astype(jnp.bfloat16)


def mix_kernel(query_ref, conv_ref, out_ref, mixed, sems):
    copies = []
    for block in range(conv_ref.shape[0]):
        at = pl.ds(block * LANES, LANES)
        queries = query_ref[at, :].astype(jnp.float32)
        mixed[at, :] = (queries * decode(conv_ref[block], 1)).astype(jnp.bfloat16)
        copy = pltpu.make_async_copy(mixed.at[at], out_ref.at[at], sems.at[block])
        copy.start()
        copies.append(copy)
    for copy in copies:
        copy.wait()


def plain_conv(gated, taps):
    blocks = gated.shape[0]
    (cos, sin), twist, mix = tables(blocks)
    cos_twist, sin_twist = twist[:, 0][:, None, :], twist[:, 1][:, None, :]
    dot = functools.partial(jnp.einsum, precision=lax.Precision.HIGHEST)

    def forward(values):
        re = dot("ncm,kn->kcm", values, mix[0])
        im = -dot("ncm,kn->kcm", values, mix[1])
        re, im = re * cos_twist + im * sin_twist, im * cos_twist - re * sin_twist
        return (
            dot("kcm,mq->kcq", re, cos) + dot("kcm,mq->kcq", im, sin),
            dot("kcm,mq->kcq", im, cos) - dot("kcm,mq->kcq", re, sin),
        )

    u_re, u_im = forward(gated)
    h_re, h_im = forward(taps)
    re, im = u_re * h_re - u_im * h_im, u_re * h_im + u_im * h_re
    re, im = (
        dot("kcq,mq->kcm", re, cos) - dot("kcq,mq->kcm", im, sin),
        dot("kcq,mq->kcm", im, cos) + dot("kcq,mq->kcm", re, sin),
    )
    re, im = re * cos_twist - im * sin_twist, im * cos_twist + re * sin_twist
    total = dot("kcm,kn->ncm", re, mix[0]) - dot("kcm,kn->ncm", im, mix[1])
    return total * (1.0 / (blocks * ROW))


def turn_order(count):
    return sorted(range(count), key=lambda turn: (turn > 3, -(turn // 2) if turn > 3 else 0, turn))


def scatter(blocks, axis):
    count = len(blocks)
    return [
        lax.ppermute(block, axis, [(i, i ^ turn) for i in range(count)]) if turn else block
        for turn, block in enumerate(blocks)
    ]


def body(streams, filter_taps, skip_gain):
    groups, parts = lax.axis_size("seq"), lax.axis_size("ch")
    held, _, channels = streams.shape
    wide = channels // parts
    own = wide // groups
    blocks = filter_taps.shape[1] * groups // ROW
    streams = jnp.transpose(streams, (1, 0, 2))
    fits = blocks == 8 and own == LANES and filter_taps.shape[1] == ROW and ROW % held == 0 and groups % 4 == 0
    fits = fits and groups & (groups - 1) == 0 and parts & (parts - 1) == 0
    small = pltpu.CompilerParams(vmem_limit_bytes=SMALL_BYTES)
    if fits:
        far = pl.BlockSpec(memory_space=pl.ANY)
        coded = (groups, parts, held, own)
        stream = pltpu.VMEM((parts, held, wide), jnp.bfloat16)
        gated = pl.pallas_call(
            send_kernel,
            in_specs=[far],
            out_specs=far,
            out_shape=jax.ShapeDtypeStruct(coded, jnp.bfloat16),
            scratch_shapes=[
                stream,
                stream,
                pltpu.VMEM(coded, jnp.bfloat16),
                pltpu.SemaphoreType.DMA((2, 2 * parts)),
                pltpu.SemaphoreType.DMA((2 * parts,)),
            ],
            compiler_params=pltpu.CompilerParams(vmem_limit_bytes=ALL_BYTES),
            cost_estimate=cost(2**25, 2**23),
            name="encode_gated",
        )(streams)
        queries = pl.pallas_call(
            query_kernel,
            in_specs=[far],
            out_specs=[far] * parts,
            out_shape=[jax.ShapeDtypeStruct((held, wide), jnp.bfloat16)] * parts,
            scratch_shapes=[pltpu.SemaphoreType.DMA((parts,))],
            compiler_params=small,
            cost_estimate=cost(2**10, 2**20),
            name="send_queries",
        )(streams)
        taps = pl.pallas_call(
            taps_kernel,
            out_shape=[jax.ShapeDtypeStruct((own, ROW), jnp.bfloat16)] * groups,
            compiler_params=small,
            cost_estimate=cost(2**25, 2**23),
            name="encode_taps",
        )(filter_taps.reshape(groups, own, ROW), skip_gain.reshape(groups, own))
    else:
        gated = encode(streams[1].astype(jnp.float32) * streams[2].astype(jnp.float32), 0)
        gated = jnp.transpose(gated.reshape(held, parts, groups, own), (2, 1, 0, 3))
        queries = jnp.transpose(streams[0].reshape(held, parts, wide), (1, 0, 2))
        first = lax.axis_index("seq") == 0
        taps = filter_taps.at[:, 0].add(jnp.where(first, skip_gain, 0.0))
        taps = encode(taps, 1).reshape(groups, own, -1)
    exchange = functools.partial(lax.all_to_all, split_axis=0, concat_axis=0, tiled=True)
    gated = gated.reshape(groups * parts, held, own)
    if fits:
        taps = scatter(taps, "seq")
        gated = exchange(gated, ("seq", "ch"))
        queries = scatter(queries, "ch")
    else:
        taps = exchange(taps, "seq")
        gated = exchange(gated, ("seq", "ch"))
        queries = exchange(queries, "ch").reshape(parts * held, wide)
    if fits:
        wave, twist, _ = tables(blocks)
        wave, back_wave = folded(wave)
        scratch = [pltpu.VMEM((blocks * 2 * GROUP, 3 * ROW), jnp.bfloat16)] * 2
        scratch += [pltpu.VMEM((blocks * 2 * GROUP, ROW), jnp.float32)] * 2
        large = pltpu.CompilerParams(vmem_limit_bytes=VMEM_BYTES)
        gated = pl.pallas_call(
            gated_spectrum_kernel,
            out_shape=jax.ShapeDtypeStruct((blocks, 2, own, ROW), jnp.float32),
            scratch_shapes=[pltpu.VMEM((blocks, own, ROW), jnp.float32)] + scratch,
            compiler_params=large,
            cost_estimate=cost(2**32, 2**24),
            name="gated_spectrum",
        )(gated, wave, twist)
        convolved = pl.pallas_call(
            conv_kernel,
            out_shape=jax.ShapeDtypeStruct((blocks, own, ROW), jnp.bfloat16),
            in_specs=[pl.BlockSpec(memory_space=pltpu.VMEM)] * (groups + 4),
            out_specs=far,
            scratch_shapes=[
                pltpu.VMEM((blocks, own, ROW), jnp.bfloat16),
                pltpu.VMEM((blocks, own, ROW), jnp.bfloat16),
                pltpu.SemaphoreType.DMA((own // GROUP,)),
            ]
            + scratch * 2,
            compiler_params=large,
            cost_estimate=cost(2**32, 2**24),
            name="convolve",
        )(gated, *[taps[turn] for turn in turn_order(groups)], wave, back_wave, twist)
    else:
        gated = decode(gated, 1).reshape(blocks, ROW, own)
        taps = jnp.transpose(decode(taps, 2), (1, 0, 2)).reshape(own, blocks, ROW)
        convolved = plain_conv(jnp.transpose(gated, (0, 2, 1)), jnp.transpose(taps, (1, 0, 2)))
        convolved = jnp.transpose(convolved, (1, 0, 2)).reshape(own, groups, -1)
        convolved = encode(jnp.transpose(convolved, (1, 0, 2)), 2)
    convolved = exchange(convolved, "seq")
    if fits:
        queries = pl.pallas_call(
            turn_kernel,
            out_shape=jax.ShapeDtypeStruct((wide, ROW), jnp.bfloat16),
            scratch_shapes=[pltpu.VMEM((ROW, wide), jnp.float32)],
            compiler_params=small,
            cost_estimate=cost(2**20, 2**21),
            name="turn_queries",
        )(*queries)
        return pl.pallas_call(
            mix_kernel,
            out_specs=far,
            out_shape=jax.ShapeDtypeStruct((wide, ROW), jnp.bfloat16),
            scratch_shapes=[
                pltpu.VMEM((wide, ROW), jnp.bfloat16),
                pltpu.SemaphoreType.DMA((groups,)),
            ],
            compiler_params=small,
            name="mix_out",
        )(queries, convolved)
    queries = jnp.transpose(queries.astype(jnp.float32))
    return (queries * decode(convolved, 2).reshape(wide, -1)).astype(jnp.bfloat16)


def cost(flops, moved):
    return pl.CostEstimate(flops=int(flops), bytes_accessed=int(moved), transcendentals=0)


def solution(mesh):
    placed = (P(("seq", "ch"), None, None), P("ch", "seq"), P("ch"))
    return jax.shard_map(
        body, mesh=mesh, in_specs=placed, out_specs=P("ch", "seq"), check_vma=False
    )
```

```python
import functools
import math

import jax
import jax.numpy as jnp
import numpy as np
from jax import lax
from jax.experimental import pallas as pl
from jax.experimental.pallas import tpu as pltpu
from jax.sharding import PartitionSpec as P

GRID = 36.0
LOW_POWER = 125.0
EXPONENT_BITS = 8
EXPONENT_BIAS = 127.0
LANES = 128
ROW = 256
CHUNK = 16
GROUP = 16
VMEM_BYTES = 20 * 1024 * 1024
SMALL_BYTES = 12 * 1024 * 1024
ALL_BYTES = 60 * 1024 * 1024


def split_marked(values, axis):
    extent = values.shape[axis]
    if axis == values.ndim - 1:
        cut = max(extent - LANES, 0)
        marked = lax.slice_in_dim(values, cut, extent, axis=axis)
        return marked, lax.slice_in_dim(values, 0, cut, axis=axis) if cut else None
    cut = min(extent, EXPONENT_BITS)
    marked = lax.slice_in_dim(values, 0, cut, axis=axis)
    return marked, lax.slice_in_dim(values, cut, extent, axis=axis) if cut < extent else None


def join_marked(marked, rest, axis):
    if rest is None:
        return marked
    return jnp.concatenate([rest, marked] if axis == rest.ndim - 1 else [marked, rest], axis=axis)


def bit_place(shape, axis):
    place = lax.broadcasted_iota(jnp.int32, shape, axis) - (shape[axis] - EXPONENT_BITS)
    return place.astype(jnp.float32)


def scale_of(peak):
    power = jnp.floor(jnp.log(jnp.maximum(peak, 1e-30)) * (1.0 / math.log(2.0))) + 1.0
    return jnp.clip(power, -100.0, 126.0)


def exponent_bits(power, shape, axis):
    place = bit_place(shape, axis)
    bits = (power + (EXPONENT_BIAS + 0.25)) * jnp.exp2(-1.0 - jnp.maximum(place, 0.0))
    return jnp.where(bits - jnp.floor(bits) >= 0.5, 0.5, 0.0), place >= 0.0


def encode(values, axis):
    peak = jnp.max(jnp.abs(values), axis=axis, keepdims=True)
    return encode_all([values], scale_of(peak), axis)[0]


def encode_all(blocks, power, axis):
    unit_share, codes, bits = jnp.exp2(-power), [], None
    top = 2.0 * LOW_POWER
    for values in blocks:
        share = jnp.abs(values) * unit_share
        place = jnp.minimum(
            jnp.minimum(share * (2.0 * top) - LOW_POWER, share * top - LOW_POWER / 2),
            jnp.minimum(share * LOW_POWER, LOW_POWER + 1.0),
        )
        first, rest = split_marked(place, axis)
        bits = exponent_bits(power, first.shape, axis) if bits is None else bits
        odd, holds = bits
        if axis == values.ndim - 1:
            marked = (jnp.floor(first * GRID - odd + 0.5) + odd) * (1.0 / GRID)
            first = jnp.exp2(jnp.where(holds, marked, first))
        else:
            marked = (jnp.floor(first * 64.0 - odd + 0.5) + odd) * (1.0 / 64.0)
            octave = jnp.floor(marked)
            first = jnp.exp2(octave) * (marked - octave + 1.0)
        size = join_marked(first, None if rest is None else jnp.exp2(rest), axis)
        codes.append(jnp.where(values < 0.0, -size, size).astype(jnp.bfloat16))
    return codes


def decode(code, axis, halvings=0):
    code = code.astype(jnp.float32)
    size = jnp.abs(code)
    place = jnp.log(size) * (1.0 / math.log(2.0))
    first, rest = split_marked(place, axis)
    if axis == code.ndim - 1:
        half = first * GRID + 0.25
    else:
        octave = jnp.floor(first + 0.002)
        first = octave + split_marked(size, axis)[0] * jnp.exp2(-octave) - 1.0
        half = first * 64.0 + 0.25
        place = join_marked(first, rest, axis)
    spot = bit_place(first.shape, axis)
    weight = jnp.where(spot >= 0.0, jnp.exp2(spot), 0.0)
    held = jnp.where(half - jnp.floor(half) >= 0.5, weight, 0.0)
    scale = jnp.exp2(jnp.sum(held, axis=axis, keepdims=True) - (EXPONENT_BIAS + halvings))
    step = 0.25 / LOW_POWER
    share = jnp.maximum(
        place * (4.0 * step), jnp.maximum(place * (2.0 * step) + 0.25, place * step + 0.25)
    )
    return jnp.where(code < 0.0, -scale, scale) * share


def tables(blocks):
    n2 = np.arange(ROW)
    k1 = np.arange(blocks)
    main = 2.0 * np.pi * np.outer(n2, n2 + 0.5) / ROW
    twist = 2.0 * np.pi * np.outer(k1 + 0.25 - blocks / 2, n2) / (blocks * ROW)
    mix = 2.0 * np.pi * np.outer(k1 + 0.25, np.arange(blocks)) / blocks
    wave = np.stack([np.cos(main), np.sin(main)]).astype(np.float32)
    twist = np.stack([np.cos(twist), np.sin(twist)], axis=1).astype(np.float32)
    mix = np.stack([np.cos(mix), np.sin(mix)], axis=0).astype(np.float32)
    return wave, twist, mix


def folded(wave):
    half = np.concatenate([wave[0, :, :LANES], wave[1, :, :LANES]], axis=1)
    parts = []
    for values in (half, half.T):
        high = values.astype(jnp.bfloat16)
        low = (values - high.astype(np.float32)).astype(jnp.bfloat16)
        parts.append(np.concatenate([high, low, high], axis=0))
    return parts


def put_split(ref, at, values):
    high = values.astype(jnp.bfloat16)
    ref[pl.ds(at, values.shape[0]), 0:ROW] = high
    ref[pl.ds(at, values.shape[0]), ROW : 2 * ROW] = high
    ref[pl.ds(at, values.shape[0]), 2 * ROW : 3 * ROW] = (
        values - high.astype(jnp.float32)
    ).astype(jnp.bfloat16)


def eighth(value, sign):
    re, im = value
    side = math.sqrt(0.5)
    return (re - sign * im) * side, (im + sign * re) * side


def four_points(values, sign):
    (a_re, a_im), (b_re, b_im), (c_re, c_im), (d_re, d_im) = values
    sum_re, sum_im, gap_re, gap_im = a_re + c_re, a_im + c_im, a_re - c_re, a_im - c_im
    more_re, more_im = b_re + d_re, b_im + d_im
    side_re, side_im = sign * (d_im - b_im), sign * (b_re - d_re)
    return (
        (sum_re + more_re, sum_im + more_im),
        (gap_re + side_re, gap_im + side_im),
        (sum_re - more_re, sum_im - more_im),
        (gap_re - side_re, gap_im - side_im),
    )


def row_of(k, part, at):
    return (2 * k + part) * GROUP + at


def eight_points(values, sign):
    sums = [(a_re + b_re, a_im + b_im) for (a_re, a_im), (b_re, b_im) in zip(values, values[4:])]
    gaps = [(a_re - b_re, a_im - b_im) for (a_re, a_im), (b_re, b_im) in zip(values, values[4:])]
    (two_re, two_im), three = gaps[2], eighth(gaps[3], sign)
    turned = [gaps[0], eighth(gaps[1], sign), (-sign * two_im, sign * two_re)]
    turned.append((-sign * three[1], sign * three[0]))
    places = [None] * 8
    places[0::2] = four_points(sums, sign)
    places[1::2] = four_points(turned, sign)
    return places


def mix_forward(taken, twist_ref, at, ref):
    angles = [math.pi * n / 16 for n in range(8)]
    turned = [
        (value * math.cos(angle), value * -math.sin(angle)) if angle else (value, 0.0)
        for value, angle in zip(taken, angles)
    ]
    for k, (re, im) in enumerate(eight_points(turned, -1.0)):
        cos_twist, sin_twist = twist_ref[k, 0:1, :], twist_ref[k, 1:2, :]
        put_split(ref, row_of(k, 0, at), re * cos_twist + im * sin_twist)
        put_split(ref, row_of(k, 1, at), im * cos_twist - re * sin_twist)


def mix_back(spectra, twist_ref):
    twisted = []
    for k, (re, im) in enumerate(spectra):
        cos_twist, sin_twist = twist_ref[k, 0:1, :], twist_ref[k, 1:2, :]
        twisted.append((re * cos_twist - im * sin_twist, im * cos_twist + re * sin_twist))
    totals = []
    for n, (re, im) in enumerate(eight_points(twisted, 1.0)):
        angle = math.pi * n / 16
        totals.append(re * math.cos(angle) - im * math.sin(angle) if n else re)
    return totals


def spectrum_rows(waves_ref, k, at):
    re = waves_ref[pl.ds(row_of(k, 0, at), CHUNK), :]
    im = waves_ref[pl.ds(row_of(k, 1, at), CHUNK), :]
    return re, im


def send_kernel(streams_ref, gated_ref, keys, values, codes, in_sems, out_sems):
    groups, parts = gated_ref.shape[:2]
    per = groups
    width = per * LANES
    arrivals = []
    for chunk in range(parts):
        lanes = pl.ds(chunk * width, width)
        for stream, buffer in ((1, keys), (2, values)):
            copy = pltpu.make_async_copy(
                streams_ref.at[stream, :, lanes], buffer.at[chunk], in_sems.at[stream - 1, chunk]
            )
            copy.start()
            arrivals.append(copy)
    copies = []
    for chunk in range(parts):
        for copy in arrivals[2 * chunk : 2 * chunk + 2]:
            copy.wait()
        part, first = chunk, 0
        for block in range(per):
            lanes = slice(block * LANES, (block + 1) * LANES)
            left = keys[chunk, :, lanes].astype(jnp.float32)
            right = values[chunk, :, lanes].astype(jnp.float32)
            codes[first + block, part] = encode(left * right, 0)
        place = (pl.ds(first, per), part)
        copy = pltpu.make_async_copy(codes.at[place], gated_ref.at[place], out_sems.at[chunk])
        copy.start()
        copies.append(copy)
    for copy in copies:
        copy.wait()


def query_kernel(streams_ref, *refs):
    query_refs, sems = refs[:-1], refs[-1]
    me = lax.axis_index("ch")
    wide = query_refs[0].shape[1]
    copies = []
    for turn, query_ref in enumerate(query_refs):
        lanes = pl.ds(pl.multiple_of((me ^ turn) * wide, wide), wide)
        copy = pltpu.make_async_copy(streams_ref.at[0, :, lanes], query_ref, sems.at[turn])
        copy.start()
        copies.append(copy)
    for copy in copies:
        copy.wait()


def taps_kernel(taps_ref, skip_ref, *code_refs):
    me = lax.axis_index("seq")
    first = (me == 0).astype(jnp.float32)
    row = lax.broadcasted_iota(jnp.int32, (LANES, LANES), 0)
    lane = lax.broadcasted_iota(jnp.int32, (LANES, LANES), 1)
    for turn, code_ref in enumerate(code_refs):
        block = me ^ turn
        gains = jnp.broadcast_to(skip_ref[pl.ds(block, 1), :], (LANES, LANES))
        gain = jnp.sum(jnp.where(row == lane, gains, 0.0), axis=1, keepdims=True) * first
        start = taps_ref[block, :, :LANES] + jnp.where(lane == 0, gain, 0.0)
        taps = jnp.concatenate([start, taps_ref[block, :, LANES:]], axis=1)
        code_ref[...] = encode(taps, 1)


def combined(waves_ref, k, at):
    re, im = spectrum_rows(waves_ref, k, at)
    re_cos, re_sin, im_cos, im_sin = re[:, :LANES], re[:, LANES:], im[:, :LANES], im[:, LANES:]
    return (
        jnp.concatenate([re_cos + im_sin, re_cos - im_sin], axis=1),
        jnp.concatenate([im_cos - re_sin, im_cos + re_sin], axis=1),
    )


def put_folded(ref, k, at, re, im):
    near_re, far_re, near_im, far_im = re[:, :LANES], re[:, LANES:], im[:, :LANES], im[:, LANES:]
    back_re = jnp.concatenate([near_re + far_re, far_im - near_im], axis=1)
    back_im = jnp.concatenate([near_im + far_im, near_re - far_re], axis=1)
    put_split(ref, row_of(k, 0, at), back_re)
    put_split(ref, row_of(k, 1, at), back_im)


def multiply(source, wave_ref, target):
    target[...] = jnp.dot(source[...], wave_ref[...], preferred_element_type=jnp.float32)


def row_groups():
    return [range(first, first + GROUP, CHUNK) for first in range(0, LANES, GROUP)]


def gated_spectrum_kernel(gated_ref, wave_ref, twist_ref, out_ref, u, *scratch):
    rows, waves = scratch[0:2], scratch[2:4]
    blocks = u.shape[0]
    parts = ROW // gated_ref.shape[1]
    groups = row_groups()

    def unpack(block, _):
        pieces = [decode(gated_ref[block * parts + part], 0) for part in range(parts)]
        u[block] = jnp.transpose(jnp.concatenate(pieces, axis=0))
        return 0

    lax.fori_loop(0, blocks, unpack, 0)
    for step in range(len(groups) + 2):
        if 0 <= step - 1 < len(groups):
            multiply(rows[(step - 1) % 2], wave_ref, waves[(step - 1) % 2])
        if step < len(groups):
            for at in groups[step]:
                taken = [u[n1, at : at + CHUNK, :] for n1 in range(blocks)]
                mix_forward(taken, twist_ref, at % GROUP, rows[step % 2])
        if step >= 2:
            for at in groups[step - 2]:
                for k in range(blocks):
                    re, im = combined(waves[step % 2], k, at % GROUP)
                    out_ref[k, 0, at : at + CHUNK, :] = re
                    out_ref[k, 1, at : at + CHUNK, :] = im


def conv_kernel(gated_ref, *refs):
    blocks = gated_ref.shape[0]
    wave_ref, back_wave_ref, twist_ref, out_ref, codes, out, sems, *scratch = refs[blocks:]
    rows, waves, back_rows, back_waves = (scratch[at : at + 2] for at in (0, 2, 4, 6))
    scale = math.log2(blocks * ROW)
    me = lax.axis_index("seq")
    groups = row_groups()
    for turn, code_ref in zip(turn_order(blocks), refs[:blocks]):
        codes[me ^ turn] = code_ref[...]

    def forward(at, half):
        taken = [decode(codes[n1, at : at + CHUNK, :], 1, scale) for n1 in range(blocks)]
        mix_forward(taken, twist_ref, at % GROUP, rows[half])

    def product(at, half):
        for k in range(blocks):
            re, im = combined(waves[half], k, at % GROUP)
            gated_re = gated_ref[k, 0, at : at + CHUNK, :]
            gated_im = gated_ref[k, 1, at : at + CHUNK, :]
            product_re, product_im = re * gated_re - im * gated_im, re * gated_im + im * gated_re
            put_folded(back_rows[half], k, at % GROUP, product_re, product_im)

    def back(at, half):
        spectra = [spectrum_rows(back_waves[half], k, at % GROUP) for k in range(blocks)]
        totals = mix_back(spectra, twist_ref)
        sizes = [jnp.abs(total) for total in totals]
        peak = jnp.max(functools.reduce(jnp.maximum, sizes), axis=1, keepdims=True)
        for n1, code in enumerate(encode_all(totals, scale_of(peak), 1)):
            out[n1, at : at + CHUNK, :] = code

    copies = []
    for step in range(len(groups) + 4):
        if 0 <= step - 1 < len(groups):
            multiply(rows[(step - 1) % 2], wave_ref, waves[(step - 1) % 2])
        if 0 <= step - 3 < len(groups):
            multiply(back_rows[(step - 3) % 2], back_wave_ref, back_waves[(step - 3) % 2])
        for work, delay in ((forward, 0), (product, 2), (back, 4)):
            if 0 <= step - delay < len(groups):
                for at in groups[step - delay]:
                    work(at, step % 2)
        if step >= 4:
            place = pl.ds((step - 4) * GROUP, GROUP)
            copy = pltpu.make_async_copy(
                out.at[:, place, :], out_ref.at[:, place, :], sems.at[step - 4]
            )
            copy.start()
            copies.append(copy)
    for copy in copies:
        copy.wait()


def turn_kernel(*refs):
    query_refs, out_ref, whole = refs[:-2], refs[-2], refs[-1]
    me = lax.axis_index("ch")
    held = query_refs[0].shape[0]
    for turn, query_ref in enumerate(query_refs):
        at = pl.multiple_of((me ^ turn) * held, held)
        whole[pl.ds(at, held), :] = query_ref[...].astype(jnp.float32)
    out_ref[...] = jnp.transpose(whole[...]).astype(jnp.bfloat16)


def mix_kernel(query_ref, conv_ref, out_ref, mixed, sems):
    copies = []
    for block in range(conv_ref.shape[0]):
        at = pl.ds(block * LANES, LANES)
        queries = query_ref[at, :].astype(jnp.float32)
        mixed[at, :] = (queries * decode(conv_ref[block], 1)).astype(jnp.bfloat16)
        copy = pltpu.make_async_copy(mixed.at[at], out_ref.at[at], sems.at[block])
        copy.start()
        copies.append(copy)
    for copy in copies:
        copy.wait()


def plain_conv(gated, taps):
    blocks = gated.shape[0]
    (cos, sin), twist, mix = tables(blocks)
    cos_twist, sin_twist = twist[:, 0][:, None, :], twist[:, 1][:, None, :]
    dot = functools.partial(jnp.einsum, precision=lax.Precision.HIGHEST)

    def forward(values):
        re = dot("ncm,kn->kcm", values, mix[0])
        im = -dot("ncm,kn->kcm", values, mix[1])
        re, im = re * cos_twist + im * sin_twist, im * cos_twist - re * sin_twist
        return (
            dot("kcm,mq->kcq", re, cos) + dot("kcm,mq->kcq", im, sin),
            dot("kcm,mq->kcq", im, cos) - dot("kcm,mq->kcq", re, sin),
        )

    u_re, u_im = forward(gated)
    h_re, h_im = forward(taps)
    re, im = u_re * h_re - u_im * h_im, u_re * h_im + u_im * h_re
    re, im = (
        dot("kcq,mq->kcm", re, cos) - dot("kcq,mq->kcm", im, sin),
        dot("kcq,mq->kcm", im, cos) + dot("kcq,mq->kcm", re, sin),
    )
    re, im = re * cos_twist - im * sin_twist, im * cos_twist + re * sin_twist
    total = dot("kcm,kn->ncm", re, mix[0]) - dot("kcm,kn->ncm", im, mix[1])
    return total * (1.0 / (blocks * ROW))


def turn_order(count):
    far = range(4, count, 2)
    return [0, 1, 2, 3, *far, *(turn + 1 for turn in far)]


def scatter(blocks, axis):
    count = len(blocks)
    return [
        lax.ppermute(block, axis, [(i, i ^ turn) for i in range(count)]) if turn else block
        for turn, block in enumerate(blocks)
    ]


def body(streams, filter_taps, skip_gain):
    groups, parts = lax.axis_size("seq"), lax.axis_size("ch")
    held, _, channels = streams.shape
    wide = channels // parts
    own = wide // groups
    blocks = filter_taps.shape[1] * groups // ROW
    streams = jnp.transpose(streams, (1, 0, 2))
    fits = blocks == 8 and own == LANES and filter_taps.shape[1] == ROW and ROW % held == 0 and groups % 4 == 0
    fits = fits and groups & (groups - 1) == 0 and parts & (parts - 1) == 0
    small = pltpu.CompilerParams(vmem_limit_bytes=SMALL_BYTES)
    if fits:
        far = pl.BlockSpec(memory_space=pl.ANY)
        coded = (groups, parts, held, own)
        stream = pltpu.VMEM((parts, held, wide), jnp.bfloat16)
        gated = pl.pallas_call(
            send_kernel,
            in_specs=[far],
            out_specs=far,
            out_shape=jax.ShapeDtypeStruct(coded, jnp.bfloat16),
            scratch_shapes=[
                stream,
                stream,
                pltpu.VMEM(coded, jnp.bfloat16),
                pltpu.SemaphoreType.DMA((2, 2 * parts)),
                pltpu.SemaphoreType.DMA((2 * parts,)),
            ],
            compiler_params=pltpu.CompilerParams(vmem_limit_bytes=ALL_BYTES),
            cost_estimate=cost(2**25, 2**23),
            name="encode_gated",
        )(streams)
        queries = pl.pallas_call(
            query_kernel,
            in_specs=[far],
            out_specs=[far] * parts,
            out_shape=[jax.ShapeDtypeStruct((held, wide), jnp.bfloat16)] * parts,
            scratch_shapes=[pltpu.SemaphoreType.DMA((parts,))],
            compiler_params=small,
            cost_estimate=cost(2**10, 2**20),
            name="send_queries",
        )(streams)
        taps = pl.pallas_call(
            taps_kernel,
            out_shape=[jax.ShapeDtypeStruct((own, ROW), jnp.bfloat16)] * groups,
            compiler_params=small,
            cost_estimate=cost(2**25, 2**23),
            name="encode_taps",
        )(filter_taps.reshape(groups, own, ROW), skip_gain.reshape(groups, own))
    else:
        gated = encode(streams[1].astype(jnp.float32) * streams[2].astype(jnp.float32), 0)
        gated = jnp.transpose(gated.reshape(held, parts, groups, own), (2, 1, 0, 3))
        queries = jnp.transpose(streams[0].reshape(held, parts, wide), (1, 0, 2))
        first = lax.axis_index("seq") == 0
        taps = filter_taps.at[:, 0].add(jnp.where(first, skip_gain, 0.0))
        taps = encode(taps, 1).reshape(groups, own, -1)
    exchange = functools.partial(lax.all_to_all, split_axis=0, concat_axis=0, tiled=True)
    gated = gated.reshape(groups * parts, held, own)
    if fits:
        taps = scatter(taps, "seq")
        gated = exchange(gated, ("seq", "ch"))
        queries = scatter(queries, "ch")
    else:
        taps = exchange(taps, "seq")
        gated = exchange(gated, ("seq", "ch"))
        queries = exchange(queries, "ch").reshape(parts * held, wide)
    if fits:
        wave, twist, _ = tables(blocks)
        wave, back_wave = folded(wave)
        scratch = [pltpu.VMEM((blocks * 2 * GROUP, 3 * ROW), jnp.bfloat16)] * 2
        scratch += [pltpu.VMEM((blocks * 2 * GROUP, ROW), jnp.float32)] * 2
        large = pltpu.CompilerParams(vmem_limit_bytes=VMEM_BYTES)
        gated = pl.pallas_call(
            gated_spectrum_kernel,
            out_shape=jax.ShapeDtypeStruct((blocks, 2, own, ROW), jnp.float32),
            scratch_shapes=[pltpu.VMEM((blocks, own, ROW), jnp.float32)] + scratch,
            compiler_params=large,
            cost_estimate=cost(2**32, 2**24),
            name="gated_spectrum",
        )(gated, wave, twist)
        convolved = pl.pallas_call(
            conv_kernel,
            out_shape=jax.ShapeDtypeStruct((blocks, own, ROW), jnp.bfloat16),
            in_specs=[pl.BlockSpec(memory_space=pltpu.VMEM)] * (groups + 4),
            out_specs=far,
            scratch_shapes=[
                pltpu.VMEM((blocks, own, ROW), jnp.bfloat16),
                pltpu.VMEM((blocks, own, ROW), jnp.bfloat16),
                pltpu.SemaphoreType.DMA((own // GROUP,)),
            ]
            + scratch * 2,
            compiler_params=large,
            cost_estimate=cost(2**32, 2**24),
            name="convolve",
        )(gated, *[taps[turn] for turn in turn_order(groups)], wave, back_wave, twist)
    else:
        gated = decode(gated, 1).reshape(blocks, ROW, own)
        taps = jnp.transpose(decode(taps, 2), (1, 0, 2)).reshape(own, blocks, ROW)
        convolved = plain_conv(jnp.transpose(gated, (0, 2, 1)), jnp.transpose(taps, (1, 0, 2)))
        convolved = jnp.transpose(convolved, (1, 0, 2)).reshape(own, groups, -1)
        convolved = encode(jnp.transpose(convolved, (1, 0, 2)), 2)
    convolved = exchange(convolved, "seq")
    if fits:
        queries = pl.pallas_call(
            turn_kernel,
            out_shape=jax.ShapeDtypeStruct((wide, ROW), jnp.bfloat16),
            scratch_shapes=[pltpu.VMEM((ROW, wide), jnp.float32)],
            compiler_params=small,
            cost_estimate=cost(2**20, 2**21),
            name="turn_queries",
        )(*queries)
        return pl.pallas_call(
            mix_kernel,
            out_specs=far,
            out_shape=jax.ShapeDtypeStruct((wide, ROW), jnp.bfloat16),
            scratch_shapes=[
                pltpu.VMEM((wide, ROW), jnp.bfloat16),
                pltpu.SemaphoreType.DMA((groups,)),
            ],
            compiler_params=small,
            name="mix_out",
        )(queries, convolved)
    queries = jnp.transpose(queries.astype(jnp.float32))
    return (queries * decode(convolved, 2).reshape(wide, -1)).astype(jnp.bfloat16)


def cost(flops, moved):
    return pl.CostEstimate(flops=int(flops), bytes_accessed=int(moved), transcendentals=0)


def solution(mesh):
    placed = (P(("seq", "ch"), None, None), P("ch", "seq"), P("ch"))
    return jax.shard_map(
        body, mesh=mesh, in_specs=placed, out_specs=P("ch", "seq"), check_vma=False
    )
```

```python
import functools
import math

import jax
import jax.numpy as jnp
import numpy as np
from jax import lax
from jax.experimental import pallas as pl
from jax.experimental.pallas import tpu as pltpu
from jax.sharding import PartitionSpec as P

GRID = 36.0
LOW_POWER = 125.0
EXPONENT_BITS = 8
EXPONENT_BIAS = 127.0
LANES = 128
ROW = 256
CHUNK = 16
GROUP = 16
VMEM_BYTES = 20 * 1024 * 1024
SMALL_BYTES = 12 * 1024 * 1024
ALL_BYTES = 60 * 1024 * 1024


def split_marked(values, axis):
    extent = values.shape[axis]
    if axis == values.ndim - 1:
        cut = max(extent - LANES, 0)
        marked = lax.slice_in_dim(values, cut, extent, axis=axis)
        return marked, lax.slice_in_dim(values, 0, cut, axis=axis) if cut else None
    cut = min(extent, EXPONENT_BITS)
    marked = lax.slice_in_dim(values, 0, cut, axis=axis)
    return marked, lax.slice_in_dim(values, cut, extent, axis=axis) if cut < extent else None


def join_marked(marked, rest, axis):
    if rest is None:
        return marked
    return jnp.concatenate([rest, marked] if axis == rest.ndim - 1 else [marked, rest], axis=axis)


def bit_place(shape, axis):
    place = lax.broadcasted_iota(jnp.int32, shape, axis) - (shape[axis] - EXPONENT_BITS)
    return place.astype(jnp.float32)


def scale_of(peak):
    power = jnp.floor(jnp.log(jnp.maximum(peak, 1e-30)) * (1.0 / math.log(2.0))) + 1.0
    return jnp.clip(power, -100.0, 126.0)


def exponent_bits(power, shape, axis):
    place = bit_place(shape, axis)
    bits = (power + (EXPONENT_BIAS + 0.25)) * jnp.exp2(-1.0 - jnp.maximum(place, 0.0))
    return jnp.where(bits - jnp.floor(bits) >= 0.5, 0.5, 0.0), place >= 0.0


def encode(values, axis):
    peak = jnp.max(jnp.abs(values), axis=axis, keepdims=True)
    return encode_all([values], scale_of(peak), axis)[0]


def encode_all(blocks, power, axis):
    unit_share, codes, bits = jnp.exp2(-power), [], None
    top = 2.0 * LOW_POWER
    for values in blocks:
        share = jnp.abs(values) * unit_share
        place = jnp.minimum(
            jnp.minimum(share * (2.0 * top) - LOW_POWER, share * top - LOW_POWER / 2),
            jnp.minimum(share * LOW_POWER, LOW_POWER + 1.0),
        )
        first, rest = split_marked(place, axis)
        bits = exponent_bits(power, first.shape, axis) if bits is None else bits
        odd, holds = bits
        if axis == values.ndim - 1:
            marked = (jnp.floor(first * GRID - odd + 0.5) + odd) * (1.0 / GRID)
            first = jnp.exp2(jnp.where(holds, marked, first))
        else:
            marked = (jnp.floor(first * 64.0 - odd + 0.5) + odd) * (1.0 / 64.0)
            octave = jnp.floor(marked)
            first = jnp.exp2(octave) * (marked - octave + 1.0)
        size = join_marked(first, None if rest is None else jnp.exp2(rest), axis)
        codes.append(jnp.where(values < 0.0, -size, size).astype(jnp.bfloat16))
    return codes


def decode(code, axis, halvings=0):
    code = code.astype(jnp.float32)
    size = jnp.abs(code)
    place = jnp.log(size) * (1.0 / math.log(2.0))
    first, rest = split_marked(place, axis)
    if axis == code.ndim - 1:
        half = first * GRID + 0.25
    else:
        octave = jnp.floor(first + 0.002)
        first = octave + split_marked(size, axis)[0] * jnp.exp2(-octave) - 1.0
        half = first * 64.0 + 0.25
        place = join_marked(first, rest, axis)
    spot = bit_place(first.shape, axis)
    weight = jnp.where(spot >= 0.0, jnp.exp2(spot), 0.0)
    held = jnp.where(half - jnp.floor(half) >= 0.5, weight, 0.0)
    scale = jnp.exp2(jnp.sum(held, axis=axis, keepdims=True) - (EXPONENT_BIAS + halvings))
    step = 0.25 / LOW_POWER
    share = jnp.maximum(
        place * (4.0 * step), jnp.maximum(place * (2.0 * step) + 0.25, place * step + 0.25)
    )
    return jnp.where(code < 0.0, -scale, scale) * share


def tables(blocks):
    n2 = np.arange(ROW)
    k1 = np.arange(blocks)
    main = 2.0 * np.pi * np.outer(n2, n2 + 0.5) / ROW
    twist = 2.0 * np.pi * np.outer(k1 + 0.25 - blocks / 2, n2) / (blocks * ROW)
    mix = 2.0 * np.pi * np.outer(k1 + 0.25, np.arange(blocks)) / blocks
    wave = np.stack([np.cos(main), np.sin(main)]).astype(np.float32)
    twist = np.stack([np.cos(twist), np.sin(twist)], axis=1).astype(np.float32)
    mix = np.stack([np.cos(mix), np.sin(mix)], axis=0).astype(np.float32)
    return wave, twist, mix


def folded(wave):
    half = np.concatenate([wave[0, :, :LANES], wave[1, :, :LANES]], axis=1)
    parts = []
    for values in (half, half.T):
        high = values.astype(jnp.bfloat16)
        low = (values - high.astype(np.float32)).astype(jnp.bfloat16)
        parts.append(np.concatenate([high, low, high], axis=0))
    return parts


def put_split(ref, at, values):
    high = values.astype(jnp.bfloat16)
    ref[pl.ds(at, values.shape[0]), 0:ROW] = high
    ref[pl.ds(at, values.shape[0]), ROW : 2 * ROW] = high
    ref[pl.ds(at, values.shape[0]), 2 * ROW : 3 * ROW] = (
        values - high.astype(jnp.float32)
    ).astype(jnp.bfloat16)


def eighth(value, sign):
    re, im = value
    side = math.sqrt(0.5)
    return (re - sign * im) * side, (im + sign * re) * side


def four_points(values, sign):
    (a_re, a_im), (b_re, b_im), (c_re, c_im), (d_re, d_im) = values
    sum_re, sum_im, gap_re, gap_im = a_re + c_re, a_im + c_im, a_re - c_re, a_im - c_im
    more_re, more_im = b_re + d_re, b_im + d_im
    side_re, side_im = sign * (d_im - b_im), sign * (b_re - d_re)
    return (
        (sum_re + more_re, sum_im + more_im),
        (gap_re + side_re, gap_im + side_im),
        (sum_re - more_re, sum_im - more_im),
        (gap_re - side_re, gap_im - side_im),
    )


def row_of(k, part, at):
    return (2 * k + part) * GROUP + at


def eight_points(values, sign):
    sums = [(a_re + b_re, a_im + b_im) for (a_re, a_im), (b_re, b_im) in zip(values, values[4:])]
    gaps = [(a_re - b_re, a_im - b_im) for (a_re, a_im), (b_re, b_im) in zip(values, values[4:])]
    (two_re, two_im), three = gaps[2], eighth(gaps[3], sign)
    turned = [gaps[0], eighth(gaps[1], sign), (-sign * two_im, sign * two_re)]
    turned.append((-sign * three[1], sign * three[0]))
    places = [None] * 8
    places[0::2] = four_points(sums, sign)
    places[1::2] = four_points(turned, sign)
    return places


def mix_forward(taken, twist_ref, at, ref):
    angles = [math.pi * n / 16 for n in range(8)]
    turned = [
        (value * math.cos(angle), value * -math.sin(angle)) if angle else (value, 0.0)
        for value, angle in zip(taken, angles)
    ]
    for k, (re, im) in enumerate(eight_points(turned, -1.0)):
        cos_twist, sin_twist = twist_ref[k, 0:1, :], twist_ref[k, 1:2, :]
        put_split(ref, row_of(k, 0, at), re * cos_twist + im * sin_twist)
        put_split(ref, row_of(k, 1, at), im * cos_twist - re * sin_twist)


def mix_back(spectra, twist_ref):
    twisted = []
    for k, (re, im) in enumerate(spectra):
        cos_twist, sin_twist = twist_ref[k, 0:1, :], twist_ref[k, 1:2, :]
        twisted.append((re * cos_twist - im * sin_twist, im * cos_twist + re * sin_twist))
    totals = []
    for n, (re, im) in enumerate(eight_points(twisted, 1.0)):
        angle = math.pi * n / 16
        totals.append(re * math.cos(angle) - im * math.sin(angle) if n else re)
    return totals


def spectrum_rows(waves_ref, k, at):
    re = waves_ref[pl.ds(row_of(k, 0, at), CHUNK), :]
    im = waves_ref[pl.ds(row_of(k, 1, at), CHUNK), :]
    return re, im


def send_kernel(streams_ref, gated_ref, keys, values, codes, in_sems, out_sems):
    parts, groups = gated_ref.shape[:2]
    per = groups
    width = per * LANES
    arrivals = []
    for chunk in range(parts):
        lanes = pl.ds(chunk * width, width)
        for stream, buffer in ((1, keys), (2, values)):
            copy = pltpu.make_async_copy(
                streams_ref.at[stream, :, lanes], buffer.at[chunk], in_sems.at[stream - 1, chunk]
            )
            copy.start()
            arrivals.append(copy)
    copies = []
    for chunk in range(parts):
        for copy in arrivals[2 * chunk : 2 * chunk + 2]:
            copy.wait()
        for block in range(per):
            lanes = slice(block * LANES, (block + 1) * LANES)
            left = keys[chunk, :, lanes].astype(jnp.float32)
            right = values[chunk, :, lanes].astype(jnp.float32)
            codes[chunk, block] = encode(left * right, 0)
        copy = pltpu.make_async_copy(codes.at[chunk], gated_ref.at[chunk], out_sems.at[chunk])
        copy.start()
        copies.append(copy)
    for copy in copies:
        copy.wait()


def query_kernel(streams_ref, *refs):
    query_refs, sems = refs[:-1], refs[-1]
    me = lax.axis_index("ch")
    wide = query_refs[0].shape[1]
    copies = []
    for turn, query_ref in enumerate(query_refs):
        lanes = pl.ds(pl.multiple_of((me ^ turn) * wide, wide), wide)
        copy = pltpu.make_async_copy(streams_ref.at[0, :, lanes], query_ref, sems.at[turn])
        copy.start()
        copies.append(copy)
    for copy in copies:
        copy.wait()


def taps_kernel(taps_ref, skip_ref, *code_refs):
    me = lax.axis_index("seq")
    first = (me == 0).astype(jnp.float32)
    row = lax.broadcasted_iota(jnp.int32, (LANES, LANES), 0)
    lane = lax.broadcasted_iota(jnp.int32, (LANES, LANES), 1)
    for turn, code_ref in enumerate(code_refs):
        block = me ^ turn
        gains = jnp.broadcast_to(skip_ref[pl.ds(block, 1), :], (LANES, LANES))
        gain = jnp.sum(jnp.where(row == lane, gains, 0.0), axis=1, keepdims=True) * first
        start = taps_ref[block, :, :LANES] + jnp.where(lane == 0, gain, 0.0)
        taps = jnp.concatenate([start, taps_ref[block, :, LANES:]], axis=1)
        code_ref[...] = encode(taps, 1)


def combined(waves_ref, k, at):
    re, im = spectrum_rows(waves_ref, k, at)
    re_cos, re_sin, im_cos, im_sin = re[:, :LANES], re[:, LANES:], im[:, :LANES], im[:, LANES:]
    return (
        jnp.concatenate([re_cos + im_sin, re_cos - im_sin], axis=1),
        jnp.concatenate([im_cos - re_sin, im_cos + re_sin], axis=1),
    )


def put_folded(ref, k, at, re, im):
    near_re, far_re, near_im, far_im = re[:, :LANES], re[:, LANES:], im[:, :LANES], im[:, LANES:]
    back_re = jnp.concatenate([near_re + far_re, far_im - near_im], axis=1)
    back_im = jnp.concatenate([near_im + far_im, near_re - far_re], axis=1)
    put_split(ref, row_of(k, 0, at), back_re)
    put_split(ref, row_of(k, 1, at), back_im)


def multiply(source, wave_ref, target):
    target[...] = jnp.dot(source[...], wave_ref[...], preferred_element_type=jnp.float32)


def row_groups():
    return [range(first, first + GROUP, CHUNK) for first in range(0, LANES, GROUP)]


def gated_spectrum_kernel(gated_ref, wave_ref, twist_ref, out_ref, u, *scratch):
    rows, waves = scratch[0:2], scratch[2:4]
    blocks = u.shape[0]
    parts = ROW // gated_ref.shape[1]
    groups = row_groups()

    def unpack(block, _):
        pieces = [decode(gated_ref[part * blocks + block], 0) for part in range(parts)]
        u[block] = jnp.transpose(jnp.concatenate(pieces, axis=0))
        return 0

    lax.fori_loop(0, blocks, unpack, 0)
    for step in range(len(groups) + 2):
        if 0 <= step - 1 < len(groups):
            multiply(rows[(step - 1) % 2], wave_ref, waves[(step - 1) % 2])
        if step < len(groups):
            for at in groups[step]:
                taken = [u[n1, at : at + CHUNK, :] for n1 in range(blocks)]
                mix_forward(taken, twist_ref, at % GROUP, rows[step % 2])
        if step >= 2:
            for at in groups[step - 2]:
                for k in range(blocks):
                    re, im = combined(waves[step % 2], k, at % GROUP)
                    out_ref[k, 0, at : at + CHUNK, :] = re
                    out_ref[k, 1, at : at + CHUNK, :] = im


def conv_kernel(gated_ref, *refs):
    blocks = gated_ref.shape[0]
    wave_ref, back_wave_ref, twist_ref, out_ref, codes, out, sems, *scratch = refs[blocks:]
    rows, waves, back_rows, back_waves = (scratch[at : at + 2] for at in (0, 2, 4, 6))
    scale = math.log2(blocks * ROW)
    me = lax.axis_index("seq")
    groups = row_groups()
    for turn, code_ref in zip(turn_order(blocks), refs[:blocks]):
        codes[me ^ turn] = code_ref[...]

    def forward(at, half):
        taken = [decode(codes[n1, at : at + CHUNK, :], 1, scale) for n1 in range(blocks)]
        mix_forward(taken, twist_ref, at % GROUP, rows[half])

    def product(at, half):
        for k in range(blocks):
            re, im = combined(waves[half], k, at % GROUP)
            gated_re = gated_ref[k, 0, at : at + CHUNK, :]
            gated_im = gated_ref[k, 1, at : at + CHUNK, :]
            product_re, product_im = re * gated_re - im * gated_im, re * gated_im + im * gated_re
            put_folded(back_rows[half], k, at % GROUP, product_re, product_im)

    def back(at, half):
        spectra = [spectrum_rows(back_waves[half], k, at % GROUP) for k in range(blocks)]
        totals = mix_back(spectra, twist_ref)
        sizes = [jnp.abs(total) for total in totals]
        peak = jnp.max(functools.reduce(jnp.maximum, sizes), axis=1, keepdims=True)
        for n1, code in enumerate(encode_all(totals, scale_of(peak), 1)):
            out[n1, at : at + CHUNK, :] = code

    copies = []
    for step in range(len(groups) + 4):
        if 0 <= step - 1 < len(groups):
            multiply(rows[(step - 1) % 2], wave_ref, waves[(step - 1) % 2])
        if 0 <= step - 3 < len(groups):
            multiply(back_rows[(step - 3) % 2], back_wave_ref, back_waves[(step - 3) % 2])
        for work, delay in ((forward, 0), (product, 2), (back, 4)):
            if 0 <= step - delay < len(groups):
                for at in groups[step - delay]:
                    work(at, step % 2)
        if step >= 4:
            place = pl.ds((step - 4) * GROUP, GROUP)
            copy = pltpu.make_async_copy(
                out.at[:, place, :], out_ref.at[:, place, :], sems.at[step - 4]
            )
            copy.start()
            copies.append(copy)
    for copy in copies:
        copy.wait()


def turn_kernel(*refs):
    query_refs, out_ref, whole = refs[:-2], refs[-2], refs[-1]
    me = lax.axis_index("ch")
    held = query_refs[0].shape[0]
    for turn, query_ref in enumerate(query_refs):
        at = pl.multiple_of((me ^ turn) * held, held)
        whole[pl.ds(at, held), :] = query_ref[...].astype(jnp.float32)
    out_ref[...] = jnp.transpose(whole[...]).astype(jnp.bfloat16)


def mix_kernel(query_ref, conv_ref, out_ref, mixed, sems):
    copies = []
    for block in range(conv_ref.shape[0]):
        at = pl.ds(block * LANES, LANES)
        queries = query_ref[at, :].astype(jnp.float32)
        mixed[at, :] = (queries * decode(conv_ref[block], 1)).astype(jnp.bfloat16)
        copy = pltpu.make_async_copy(mixed.at[at], out_ref.at[at], sems.at[block])
        copy.start()
        copies.append(copy)
    for copy in copies:
        copy.wait()


def plain_conv(gated, taps):
    blocks = gated.shape[0]
    (cos, sin), twist, mix = tables(blocks)
    cos_twist, sin_twist = twist[:, 0][:, None, :], twist[:, 1][:, None, :]
    dot = functools.partial(jnp.einsum, precision=lax.Precision.HIGHEST)

    def forward(values):
        re = dot("ncm,kn->kcm", values, mix[0])
        im = -dot("ncm,kn->kcm", values, mix[1])
        re, im = re * cos_twist + im * sin_twist, im * cos_twist - re * sin_twist
        return (
            dot("kcm,mq->kcq", re, cos) + dot("kcm,mq->kcq", im, sin),
            dot("kcm,mq->kcq", im, cos) - dot("kcm,mq->kcq", re, sin),
        )

    u_re, u_im = forward(gated)
    h_re, h_im = forward(taps)
    re, im = u_re * h_re - u_im * h_im, u_re * h_im + u_im * h_re
    re, im = (
        dot("kcq,mq->kcm", re, cos) - dot("kcq,mq->kcm", im, sin),
        dot("kcq,mq->kcm", im, cos) + dot("kcq,mq->kcm", re, sin),
    )
    re, im = re * cos_twist - im * sin_twist, im * cos_twist + re * sin_twist
    total = dot("kcm,kn->ncm", re, mix[0]) - dot("kcm,kn->ncm", im, mix[1])
    return total * (1.0 / (blocks * ROW))


def turn_order(count):
    far = range(4, count, 2)
    return [0, 1, 2, 3, *far, *(turn + 1 for turn in far)]


def scatter(blocks, axis):
    count = len(blocks)
    return [
        lax.ppermute(block, axis, [(i, i ^ turn) for i in range(count)]) if turn else block
        for turn, block in enumerate(blocks)
    ]


def body(streams, filter_taps, skip_gain):
    groups, parts = lax.axis_size("seq"), lax.axis_size("ch")
    held, _, channels = streams.shape
    wide = channels // parts
    own = wide // groups
    blocks = filter_taps.shape[1] * groups // ROW
    streams = jnp.transpose(streams, (1, 0, 2))
    fits = blocks == 8 and own == LANES and filter_taps.shape[1] == ROW and ROW % held == 0 and groups % 4 == 0
    fits = fits and groups & (groups - 1) == 0 and parts & (parts - 1) == 0
    small = pltpu.CompilerParams(vmem_limit_bytes=SMALL_BYTES)
    if fits:
        far = pl.BlockSpec(memory_space=pl.ANY)
        coded = (parts, groups, held, own)
        stream = pltpu.VMEM((parts, held, wide), jnp.bfloat16)
        gated = pl.pallas_call(
            send_kernel,
            in_specs=[far],
            out_specs=far,
            out_shape=jax.ShapeDtypeStruct(coded, jnp.bfloat16),
            scratch_shapes=[
                stream,
                stream,
                pltpu.VMEM(coded, jnp.bfloat16),
                pltpu.SemaphoreType.DMA((2, 2 * parts)),
                pltpu.SemaphoreType.DMA((2 * parts,)),
            ],
            compiler_params=pltpu.CompilerParams(vmem_limit_bytes=ALL_BYTES),
            cost_estimate=cost(2**25, 2**23),
            name="encode_gated",
        )(streams)
        queries = pl.pallas_call(
            query_kernel,
            in_specs=[far],
            out_specs=[far] * parts,
            out_shape=[jax.ShapeDtypeStruct((held, wide), jnp.bfloat16)] * parts,
            scratch_shapes=[pltpu.SemaphoreType.DMA((parts,))],
            compiler_params=small,
            cost_estimate=cost(2**10, 2**20),
            name="send_queries",
        )(streams)
        taps = pl.pallas_call(
            taps_kernel,
            out_shape=[jax.ShapeDtypeStruct((own, ROW), jnp.bfloat16)] * groups,
            compiler_params=small,
            cost_estimate=cost(2**25, 2**23),
            name="encode_taps",
        )(filter_taps.reshape(groups, own, ROW), skip_gain.reshape(groups, own))
    else:
        gated = encode(streams[1].astype(jnp.float32) * streams[2].astype(jnp.float32), 0)
        gated = jnp.transpose(gated.reshape(held, parts, groups, own), (2, 1, 0, 3))
        queries = jnp.transpose(streams[0].reshape(held, parts, wide), (1, 0, 2))
        first = lax.axis_index("seq") == 0
        taps = filter_taps.at[:, 0].add(jnp.where(first, skip_gain, 0.0))
        taps = encode(taps, 1).reshape(groups, own, -1)
    exchange = functools.partial(lax.all_to_all, split_axis=0, concat_axis=0, tiled=True)
    gated = gated.reshape(groups * parts, held, own)
    if fits:
        taps = scatter(taps, "seq")
        gated = exchange(gated, ("ch", "seq"))
        queries = scatter(queries, "ch")
    else:
        taps = exchange(taps, "seq")
        gated = exchange(gated, ("seq", "ch"))
        queries = exchange(queries, "ch").reshape(parts * held, wide)
    if fits:
        wave, twist, _ = tables(blocks)
        wave, back_wave = folded(wave)
        scratch = [pltpu.VMEM((blocks * 2 * GROUP, 3 * ROW), jnp.bfloat16)] * 2
        scratch += [pltpu.VMEM((blocks * 2 * GROUP, ROW), jnp.float32)] * 2
        large = pltpu.CompilerParams(vmem_limit_bytes=VMEM_BYTES)
        gated = pl.pallas_call(
            gated_spectrum_kernel,
            out_shape=jax.ShapeDtypeStruct((blocks, 2, own, ROW), jnp.float32),
            scratch_shapes=[pltpu.VMEM((blocks, own, ROW), jnp.float32)] + scratch,
            compiler_params=large,
            cost_estimate=cost(2**32, 2**24),
            name="gated_spectrum",
        )(gated, wave, twist)
        convolved = pl.pallas_call(
            conv_kernel,
            out_shape=jax.ShapeDtypeStruct((blocks, own, ROW), jnp.bfloat16),
            in_specs=[pl.BlockSpec(memory_space=pltpu.VMEM)] * (groups + 4),
            out_specs=far,
            scratch_shapes=[
                pltpu.VMEM((blocks, own, ROW), jnp.bfloat16),
                pltpu.VMEM((blocks, own, ROW), jnp.bfloat16),
                pltpu.SemaphoreType.DMA((own // GROUP,)),
            ]
            + scratch * 2,
            compiler_params=large,
            cost_estimate=cost(2**32, 2**24),
            name="convolve",
        )(gated, *[taps[turn] for turn in turn_order(groups)], wave, back_wave, twist)
    else:
        gated = decode(gated, 1).reshape(blocks, ROW, own)
        taps = jnp.transpose(decode(taps, 2), (1, 0, 2)).reshape(own, blocks, ROW)
        convolved = plain_conv(jnp.transpose(gated, (0, 2, 1)), jnp.transpose(taps, (1, 0, 2)))
        convolved = jnp.transpose(convolved, (1, 0, 2)).reshape(own, groups, -1)
        convolved = encode(jnp.transpose(convolved, (1, 0, 2)), 2)
    convolved = exchange(convolved, "seq")
    if fits:
        queries = pl.pallas_call(
            turn_kernel,
            out_shape=jax.ShapeDtypeStruct((wide, ROW), jnp.bfloat16),
            scratch_shapes=[pltpu.VMEM((ROW, wide), jnp.float32)],
            compiler_params=small,
            cost_estimate=cost(2**20, 2**21),
            name="turn_queries",
        )(*queries)
        return pl.pallas_call(
            mix_kernel,
            out_specs=far,
            out_shape=jax.ShapeDtypeStruct((wide, ROW), jnp.bfloat16),
            scratch_shapes=[
                pltpu.VMEM((wide, ROW), jnp.bfloat16),
                pltpu.SemaphoreType.DMA((groups,)),
            ],
            compiler_params=small,
            name="mix_out",
        )(queries, convolved)
    queries = jnp.transpose(queries.astype(jnp.float32))
    return (queries * decode(convolved, 2).reshape(wide, -1)).astype(jnp.bfloat16)


def cost(flops, moved):
    return pl.CostEstimate(flops=int(flops), bytes_accessed=int(moved), transcendentals=0)


def solution(mesh):
    placed = (P(("seq", "ch"), None, None), P("ch", "seq"), P("ch"))
    return jax.shard_map(
        body, mesh=mesh, in_specs=placed, out_specs=P("ch", "seq"), check_vma=False
    )
```

```python
import functools
import math

import jax
import jax.numpy as jnp
import numpy as np
from jax import lax
from jax.experimental import pallas as pl
from jax.experimental.pallas import tpu as pltpu
from jax.sharding import PartitionSpec as P

GRID = 36.0
LOW_POWER = 125.0
EXPONENT_BITS = 8
EXPONENT_BIAS = 127.0
LANES = 128
ROW = 256
CHUNK = 16
GROUP = 16
VMEM_BYTES = 20 * 1024 * 1024
SMALL_BYTES = 12 * 1024 * 1024
ALL_BYTES = 60 * 1024 * 1024


def split_marked(values, axis):
    extent = values.shape[axis]
    if axis == values.ndim - 1:
        cut = max(extent - LANES, 0)
        marked = lax.slice_in_dim(values, cut, extent, axis=axis)
        return marked, lax.slice_in_dim(values, 0, cut, axis=axis) if cut else None
    cut = min(extent, EXPONENT_BITS)
    marked = lax.slice_in_dim(values, 0, cut, axis=axis)
    return marked, lax.slice_in_dim(values, cut, extent, axis=axis) if cut < extent else None


def join_marked(marked, rest, axis):
    if rest is None:
        return marked
    return jnp.concatenate([rest, marked] if axis == rest.ndim - 1 else [marked, rest], axis=axis)


def bit_place(shape, axis):
    place = lax.broadcasted_iota(jnp.int32, shape, axis) - (shape[axis] - EXPONENT_BITS)
    return place.astype(jnp.float32)


def scale_of(peak):
    power = jnp.floor(jnp.log(jnp.maximum(peak, 1e-30)) * (1.0 / math.log(2.0))) + 1.0
    return jnp.clip(power, -100.0, 126.0)


def exponent_bits(power, shape, axis):
    place = bit_place(shape, axis)
    bits = (power + (EXPONENT_BIAS + 0.25)) * jnp.exp2(-1.0 - jnp.maximum(place, 0.0))
    return jnp.where(bits - jnp.floor(bits) >= 0.5, 0.5, 0.0), place >= 0.0


def encode(values, axis):
    peak = jnp.max(jnp.abs(values), axis=axis, keepdims=True)
    return encode_all([values], scale_of(peak), axis)[0]


def encode_all(blocks, power, axis):
    unit_share, codes, bits = jnp.exp2(-power), [], None
    top = 2.0 * LOW_POWER
    for values in blocks:
        share = jnp.abs(values) * unit_share
        place = jnp.minimum(
            jnp.minimum(share * (2.0 * top) - LOW_POWER, share * top - LOW_POWER / 2),
            jnp.minimum(share * LOW_POWER, LOW_POWER + 1.0),
        )
        first, rest = split_marked(place, axis)
        bits = exponent_bits(power, first.shape, axis) if bits is None else bits
        odd, holds = bits
        if axis == values.ndim - 1:
            marked = (jnp.floor(first * GRID - odd + 0.5) + odd) * (1.0 / GRID)
            first = jnp.exp2(jnp.where(holds, marked, first))
        else:
            marked = (jnp.floor(first * 64.0 - odd + 0.5) + odd) * (1.0 / 64.0)
            octave = jnp.floor(marked)
            first = jnp.exp2(octave) * (marked - octave + 1.0)
        size = join_marked(first, None if rest is None else jnp.exp2(rest), axis)
        codes.append(jnp.where(values < 0.0, -size, size).astype(jnp.bfloat16))
    return codes


def decode(code, axis, halvings=0):
    code = code.astype(jnp.float32)
    size = jnp.abs(code)
    place = jnp.log(size) * (1.0 / math.log(2.0))
    first, rest = split_marked(place, axis)
    if axis == code.ndim - 1:
        half = first * GRID + 0.25
    else:
        octave = jnp.floor(first + 0.002)
        first = octave + split_marked(size, axis)[0] * jnp.exp2(-octave) - 1.0
        half = first * 64.0 + 0.25
        place = join_marked(first, rest, axis)
    spot = bit_place(first.shape, axis)
    weight = jnp.where(spot >= 0.0, jnp.exp2(spot), 0.0)
    held = jnp.where(half - jnp.floor(half) >= 0.5, weight, 0.0)
    scale = jnp.exp2(jnp.sum(held, axis=axis, keepdims=True) - (EXPONENT_BIAS + halvings))
    step = 0.25 / LOW_POWER
    share = jnp.maximum(
        place * (4.0 * step), jnp.maximum(place * (2.0 * step) + 0.25, place * step + 0.25)
    )
    return jnp.where(code < 0.0, -scale, scale) * share


def tables(blocks):
    n2 = np.arange(ROW)
    k1 = np.arange(blocks)
    main = 2.0 * np.pi * np.outer(n2, n2 + 0.5) / ROW
    twist = 2.0 * np.pi * np.outer(k1 + 0.25 - blocks / 2, n2) / (blocks * ROW)
    mix = 2.0 * np.pi * np.outer(k1 + 0.25, np.arange(blocks)) / blocks
    wave = np.stack([np.cos(main), np.sin(main)]).astype(np.float32)
    twist = np.stack([np.cos(twist), np.sin(twist)], axis=1).astype(np.float32)
    mix = np.stack([np.cos(mix), np.sin(mix)], axis=0).astype(np.float32)
    return wave, twist, mix


def folded(wave):
    half = np.concatenate([wave[0, :, :LANES], wave[1, :, :LANES]], axis=1)
    parts = []
    for values in (half, half.T):
        high = values.astype(jnp.bfloat16)
        low = (values - high.astype(np.float32)).astype(jnp.bfloat16)
        parts.append(np.concatenate([high, low, high], axis=0))
    return parts


def put_split(ref, at, values):
    high = values.astype(jnp.bfloat16)
    ref[pl.ds(at, values.shape[0]), 0:ROW] = high
    ref[pl.ds(at, values.shape[0]), ROW : 2 * ROW] = high
    ref[pl.ds(at, values.shape[0]), 2 * ROW : 3 * ROW] = (
        values - high.astype(jnp.float32)
    ).astype(jnp.bfloat16)


def eighth(value, sign):
    re, im = value
    side = math.sqrt(0.5)
    return (re - sign * im) * side, (im + sign * re) * side


def four_points(values, sign):
    (a_re, a_im), (b_re, b_im), (c_re, c_im), (d_re, d_im) = values
    sum_re, sum_im, gap_re, gap_im = a_re + c_re, a_im + c_im, a_re - c_re, a_im - c_im
    more_re, more_im = b_re + d_re, b_im + d_im
    side_re, side_im = sign * (d_im - b_im), sign * (b_re - d_re)
    return (
        (sum_re + more_re, sum_im + more_im),
        (gap_re + side_re, gap_im + side_im),
        (sum_re - more_re, sum_im - more_im),
        (gap_re - side_re, gap_im - side_im),
    )


def row_of(k, part, at):
    return (2 * k + part) * GROUP + at


def eight_points(values, sign):
    sums = [(a_re + b_re, a_im + b_im) for (a_re, a_im), (b_re, b_im) in zip(values, values[4:])]
    gaps = [(a_re - b_re, a_im - b_im) for (a_re, a_im), (b_re, b_im) in zip(values, values[4:])]
    (two_re, two_im), three = gaps[2], eighth(gaps[3], sign)
    turned = [gaps[0], eighth(gaps[1], sign), (-sign * two_im, sign * two_re)]
    turned.append((-sign * three[1], sign * three[0]))
    places = [None] * 8
    places[0::2] = four_points(sums, sign)
    places[1::2] = four_points(turned, sign)
    return places


def mix_forward(taken, twist_ref, at, ref):
    angles = [math.pi * n / 16 for n in range(8)]
    turned = [
        (value * math.cos(angle), value * -math.sin(angle)) if angle else (value, 0.0)
        for value, angle in zip(taken, angles)
    ]
    for k, (re, im) in enumerate(eight_points(turned, -1.0)):
        cos_twist, sin_twist = twist_ref[k, 0:1, :], twist_ref[k, 1:2, :]
        put_split(ref, row_of(k, 0, at), re * cos_twist + im * sin_twist)
        put_split(ref, row_of(k, 1, at), im * cos_twist - re * sin_twist)


def mix_back(spectra, twist_ref):
    twisted = []
    for k, (re, im) in enumerate(spectra):
        cos_twist, sin_twist = twist_ref[k, 0:1, :], twist_ref[k, 1:2, :]
        twisted.append((re * cos_twist - im * sin_twist, im * cos_twist + re * sin_twist))
    totals = []
    for n, (re, im) in enumerate(eight_points(twisted, 1.0)):
        angle = math.pi * n / 16
        totals.append(re * math.cos(angle) - im * math.sin(angle) if n else re)
    return totals


def spectrum_rows(waves_ref, k, at):
    re = waves_ref[pl.ds(row_of(k, 0, at), CHUNK), :]
    im = waves_ref[pl.ds(row_of(k, 1, at), CHUNK), :]
    return re, im


def send_kernel(streams_ref, gated_ref, keys, values, codes, in_sems, out_sems):
    groups, parts = gated_ref.shape[:2]
    per = groups
    width = per * LANES
    arrivals = []
    for chunk in range(parts):
        lanes = pl.ds(chunk * width, width)
        for stream, buffer in ((1, keys), (2, values)):
            copy = pltpu.make_async_copy(
                streams_ref.at[stream, :, lanes], buffer.at[chunk], in_sems.at[stream - 1, chunk]
            )
            copy.start()
            arrivals.append(copy)
    copies = []
    for chunk in range(parts):
        for copy in arrivals[2 * chunk : 2 * chunk + 2]:
            copy.wait()
        part, first = chunk, 0
        for block in range(per):
            lanes = slice(block * LANES, (block + 1) * LANES)
            left = keys[chunk, :, lanes].astype(jnp.float32)
            right = values[chunk, :, lanes].astype(jnp.float32)
            codes[first + block, part] = encode(left * right, 0)
        place = (pl.ds(first, per), part)
        copy = pltpu.make_async_copy(codes.at[place], gated_ref.at[place], out_sems.at[chunk])
        copy.start()
        copies.append(copy)
    for copy in copies:
        copy.wait()


def query_kernel(streams_ref, *refs):
    query_refs, sems = refs[:-1], refs[-1]
    me = lax.axis_index("ch")
    wide = query_refs[0].shape[1]
    copies = []
    for turn, query_ref in enumerate(query_refs):
        lanes = pl.ds(pl.multiple_of((me ^ turn) * wide, wide), wide)
        copy = pltpu.make_async_copy(streams_ref.at[0, :, lanes], query_ref, sems.at[turn])
        copy.start()
        copies.append(copy)
    for copy in copies:
        copy.wait()


def taps_kernel(taps_ref, skip_ref, *code_refs):
    me = lax.axis_index("seq")
    first = (me == 0).astype(jnp.float32)
    row = lax.broadcasted_iota(jnp.int32, (LANES, LANES), 0)
    lane = lax.broadcasted_iota(jnp.int32, (LANES, LANES), 1)
    for turn, code_ref in enumerate(code_refs):
        block = me ^ turn
        gains = jnp.broadcast_to(skip_ref[pl.ds(block, 1), :], (LANES, LANES))
        gain = jnp.sum(jnp.where(row == lane, gains, 0.0), axis=1, keepdims=True) * first
        start = taps_ref[block, :, :LANES] + jnp.where(lane == 0, gain, 0.0)
        taps = jnp.concatenate([start, taps_ref[block, :, LANES:]], axis=1)
        code_ref[...] = encode(taps, 1)


def combined(waves_ref, k, at):
    re, im = spectrum_rows(waves_ref, k, at)
    re_cos, re_sin, im_cos, im_sin = re[:, :LANES], re[:, LANES:], im[:, :LANES], im[:, LANES:]
    return (
        jnp.concatenate([re_cos + im_sin, re_cos - im_sin], axis=1),
        jnp.concatenate([im_cos - re_sin, im_cos + re_sin], axis=1),
    )


def put_folded(ref, k, at, re, im):
    near_re, far_re, near_im, far_im = re[:, :LANES], re[:, LANES:], im[:, :LANES], im[:, LANES:]
    back_re = jnp.concatenate([near_re + far_re, far_im - near_im], axis=1)
    back_im = jnp.concatenate([near_im + far_im, near_re - far_re], axis=1)
    put_split(ref, row_of(k, 0, at), back_re)
    put_split(ref, row_of(k, 1, at), back_im)


def multiply(source, wave_ref, target):
    target[...] = jnp.dot(source[...], wave_ref[...], preferred_element_type=jnp.float32)


def row_groups():
    return [range(first, first + GROUP, CHUNK) for first in range(0, LANES, GROUP)]


def gated_spectrum_kernel(gated_ref, wave_ref, twist_ref, *refs):
    early = (len(refs) - 6) // 2
    out_ref, u, rows, waves = refs[early], refs[-5], refs[-4:-2], refs[-2:]
    blocks = u.shape[0]
    for code_ref, taps_ref in zip(refs[:early], refs[early + 1 :]):
        taps_ref[...] = decode(code_ref[...], 1, math.log2(blocks * ROW))
    parts = ROW // gated_ref.shape[1]
    groups = row_groups()

    def unpack(block, _):
        pieces = [decode(gated_ref[block * parts + part], 0) for part in range(parts)]
        u[block] = jnp.transpose(jnp.concatenate(pieces, axis=0))
        return 0

    lax.fori_loop(0, blocks, unpack, 0)
    for step in range(len(groups) + 2):
        if 0 <= step - 1 < len(groups):
            multiply(rows[(step - 1) % 2], wave_ref, waves[(step - 1) % 2])
        if step < len(groups):
            for at in groups[step]:
                taken = [u[n1, at : at + CHUNK, :] for n1 in range(blocks)]
                mix_forward(taken, twist_ref, at % GROUP, rows[step % 2])
        if step >= 2:
            for at in groups[step - 2]:
                for k in range(blocks):
                    re, im = combined(waves[step % 2], k, at % GROUP)
                    out_ref[k, 0, at : at + CHUNK, :] = re
                    out_ref[k, 1, at : at + CHUNK, :] = im


def conv_kernel(gated_ref, *refs):
    blocks = gated_ref.shape[0]
    wave_ref, back_wave_ref, twist_ref, out_ref, taps, out, sems, *scratch = refs[blocks:]
    rows, waves, back_rows, back_waves = (scratch[at : at + 2] for at in (0, 2, 4, 6))
    scale = math.log2(blocks * ROW)
    me = lax.axis_index("seq")
    groups = row_groups()
    for turn, taps_ref in enumerate(refs[:blocks]):
        early = taps_ref.dtype == jnp.float32
        taps[me ^ turn] = taps_ref[...] if early else decode(taps_ref[...], 1, scale)

    def forward(at, half):
        taken = [taps[n1, at : at + CHUNK, :] for n1 in range(blocks)]
        mix_forward(taken, twist_ref, at % GROUP, rows[half])

    def product(at, half):
        for k in range(blocks):
            re, im = combined(waves[half], k, at % GROUP)
            gated_re = gated_ref[k, 0, at : at + CHUNK, :]
            gated_im = gated_ref[k, 1, at : at + CHUNK, :]
            product_re, product_im = re * gated_re - im * gated_im, re * gated_im + im * gated_re
            put_folded(back_rows[half], k, at % GROUP, product_re, product_im)

    def back(at, half):
        spectra = [spectrum_rows(back_waves[half], k, at % GROUP) for k in range(blocks)]
        totals = mix_back(spectra, twist_ref)
        sizes = [jnp.abs(total) for total in totals]
        peak = jnp.max(functools.reduce(jnp.maximum, sizes), axis=1, keepdims=True)
        for n1, code in enumerate(encode_all(totals, scale_of(peak), 1)):
            out[n1, at : at + CHUNK, :] = code

    copies = []
    for step in range(len(groups) + 4):
        if 0 <= step - 1 < len(groups):
            multiply(rows[(step - 1) % 2], wave_ref, waves[(step - 1) % 2])
        if 0 <= step - 3 < len(groups):
            multiply(back_rows[(step - 3) % 2], back_wave_ref, back_waves[(step - 3) % 2])
        for work, delay in ((forward, 0), (product, 2), (back, 4)):
            if 0 <= step - delay < len(groups):
                for at in groups[step - delay]:
                    work(at, step % 2)
        if step >= 4:
            place = pl.ds((step - 4) * GROUP, GROUP)
            copy = pltpu.make_async_copy(
                out.at[:, place, :], out_ref.at[:, place, :], sems.at[step - 4]
            )
            copy.start()
            copies.append(copy)
    for copy in copies:
        copy.wait()


def turn_kernel(*refs):
    query_refs, out_ref, whole = refs[:-2], refs[-2], refs[-1]
    me = lax.axis_index("ch")
    held = query_refs[0].shape[0]
    for turn, query_ref in enumerate(query_refs):
        at = pl.multiple_of((me ^ turn) * held, held)
        whole[pl.ds(at, held), :] = query_ref[...].astype(jnp.float32)
    out_ref[...] = jnp.transpose(whole[...]).astype(jnp.bfloat16)


def mix_kernel(query_ref, conv_ref, out_ref, mixed, sems):
    copies = []
    for block in range(conv_ref.shape[0]):
        at = pl.ds(block * LANES, LANES)
        queries = query_ref[at, :].astype(jnp.float32)
        mixed[at, :] = (queries * decode(conv_ref[block], 1)).astype(jnp.bfloat16)
        copy = pltpu.make_async_copy(mixed.at[at], out_ref.at[at], sems.at[block])
        copy.start()
        copies.append(copy)
    for copy in copies:
        copy.wait()


def plain_conv(gated, taps):
    blocks = gated.shape[0]
    (cos, sin), twist, mix = tables(blocks)
    cos_twist, sin_twist = twist[:, 0][:, None, :], twist[:, 1][:, None, :]
    dot = functools.partial(jnp.einsum, precision=lax.Precision.HIGHEST)

    def forward(values):
        re = dot("ncm,kn->kcm", values, mix[0])
        im = -dot("ncm,kn->kcm", values, mix[1])
        re, im = re * cos_twist + im * sin_twist, im * cos_twist - re * sin_twist
        return (
            dot("kcm,mq->kcq", re, cos) + dot("kcm,mq->kcq", im, sin),
            dot("kcm,mq->kcq", im, cos) - dot("kcm,mq->kcq", re, sin),
        )

    u_re, u_im = forward(gated)
    h_re, h_im = forward(taps)
    re, im = u_re * h_re - u_im * h_im, u_re * h_im + u_im * h_re
    re, im = (
        dot("kcq,mq->kcm", re, cos) - dot("kcq,mq->kcm", im, sin),
        dot("kcq,mq->kcm", im, cos) + dot("kcq,mq->kcm", re, sin),
    )
    re, im = re * cos_twist - im * sin_twist, im * cos_twist + re * sin_twist
    total = dot("kcm,kn->ncm", re, mix[0]) - dot("kcm,kn->ncm", im, mix[1])
    return total * (1.0 / (blocks * ROW))


def scatter(blocks, axis):
    count = len(blocks)
    return [
        lax.ppermute(block, axis, [(i, i ^ turn) for i in range(count)]) if turn else block
        for turn, block in enumerate(blocks)
    ]


def body(streams, filter_taps, skip_gain):
    groups, parts = lax.axis_size("seq"), lax.axis_size("ch")
    held, _, channels = streams.shape
    wide = channels // parts
    own = wide // groups
    blocks = filter_taps.shape[1] * groups // ROW
    streams = jnp.transpose(streams, (1, 0, 2))
    fits = blocks == 8 and own == LANES and filter_taps.shape[1] == ROW and ROW % held == 0 and groups % 4 == 0
    fits = fits and groups & (groups - 1) == 0 and parts & (parts - 1) == 0
    small = pltpu.CompilerParams(vmem_limit_bytes=SMALL_BYTES)
    if fits:
        far = pl.BlockSpec(memory_space=pl.ANY)
        coded = (groups, parts, held, own)
        stream = pltpu.VMEM((parts, held, wide), jnp.bfloat16)
        gated = pl.pallas_call(
            send_kernel,
            in_specs=[far],
            out_specs=far,
            out_shape=jax.ShapeDtypeStruct(coded, jnp.bfloat16),
            scratch_shapes=[
                stream,
                stream,
                pltpu.VMEM(coded, jnp.bfloat16),
                pltpu.SemaphoreType.DMA((2, 2 * parts)),
                pltpu.SemaphoreType.DMA((2 * parts,)),
            ],
            compiler_params=pltpu.CompilerParams(vmem_limit_bytes=ALL_BYTES),
            cost_estimate=cost(2**25, 2**23),
            name="encode_gated",
        )(streams)
        queries = pl.pallas_call(
            query_kernel,
            in_specs=[far],
            out_specs=[far] * parts,
            out_shape=[jax.ShapeDtypeStruct((held, wide), jnp.bfloat16)] * parts,
            scratch_shapes=[pltpu.SemaphoreType.DMA((parts,))],
            compiler_params=small,
            cost_estimate=cost(2**10, 2**20),
            name="send_queries",
        )(streams)
        taps = pl.pallas_call(
            taps_kernel,
            out_shape=[jax.ShapeDtypeStruct((own, ROW), jnp.bfloat16)] * groups,
            compiler_params=small,
            cost_estimate=cost(2**25, 2**23),
            name="encode_taps",
        )(filter_taps.reshape(groups, own, ROW), skip_gain.reshape(groups, own))
    else:
        gated = encode(streams[1].astype(jnp.float32) * streams[2].astype(jnp.float32), 0)
        gated = jnp.transpose(gated.reshape(held, parts, groups, own), (2, 1, 0, 3))
        queries = jnp.transpose(streams[0].reshape(held, parts, wide), (1, 0, 2))
        first = lax.axis_index("seq") == 0
        taps = filter_taps.at[:, 0].add(jnp.where(first, skip_gain, 0.0))
        taps = encode(taps, 1).reshape(groups, own, -1)
    exchange = functools.partial(lax.all_to_all, split_axis=0, concat_axis=0, tiled=True)
    gated = gated.reshape(groups * parts, held, own)
    if fits:
        taps = scatter(taps, "seq")
        gated = exchange(gated, ("seq", "ch"))
        queries = scatter(queries, "ch")
    else:
        taps = exchange(taps, "seq")
        gated = exchange(gated, ("seq", "ch"))
        queries = exchange(queries, "ch").reshape(parts * held, wide)
    if fits:
        wave, twist, _ = tables(blocks)
        wave, back_wave = folded(wave)
        scratch = [pltpu.VMEM((blocks * 2 * GROUP, 3 * ROW), jnp.bfloat16)] * 2
        scratch += [pltpu.VMEM((blocks * 2 * GROUP, ROW), jnp.float32)] * 2
        large = pltpu.CompilerParams(vmem_limit_bytes=VMEM_BYTES)
        early = groups // 2
        gated, *known = pl.pallas_call(
            gated_spectrum_kernel,
            out_shape=[jax.ShapeDtypeStruct((blocks, 2, own, ROW), jnp.float32)]
            + [jax.ShapeDtypeStruct((own, ROW), jnp.float32)] * early,
            scratch_shapes=[pltpu.VMEM((blocks, own, ROW), jnp.float32)] + scratch,
            compiler_params=large,
            cost_estimate=cost(2**32, 2**24),
            name="gated_spectrum",
        )(gated, wave, twist, *taps[:early])
        convolved = pl.pallas_call(
            conv_kernel,
            out_shape=jax.ShapeDtypeStruct((blocks, own, ROW), jnp.bfloat16),
            in_specs=[pl.BlockSpec(memory_space=pltpu.VMEM)] * (groups + 4),
            out_specs=far,
            scratch_shapes=[
                pltpu.VMEM((blocks, own, ROW), jnp.float32),
                pltpu.VMEM((blocks, own, ROW), jnp.bfloat16),
                pltpu.SemaphoreType.DMA((own // GROUP,)),
            ]
            + scratch * 2,
            compiler_params=large,
            cost_estimate=cost(2**32, 2**24),
            name="convolve",
        )(gated, *known, *taps[early:], wave, back_wave, twist)
    else:
        gated = decode(gated, 1).reshape(blocks, ROW, own)
        taps = jnp.transpose(decode(taps, 2), (1, 0, 2)).reshape(own, blocks, ROW)
        convolved = plain_conv(jnp.transpose(gated, (0, 2, 1)), jnp.transpose(taps, (1, 0, 2)))
        convolved = jnp.transpose(convolved, (1, 0, 2)).reshape(own, groups, -1)
        convolved = encode(jnp.transpose(convolved, (1, 0, 2)), 2)
    convolved = exchange(convolved, "seq")
    if fits:
        queries = pl.pallas_call(
            turn_kernel,
            out_shape=jax.ShapeDtypeStruct((wide, ROW), jnp.bfloat16),
            scratch_shapes=[pltpu.VMEM((ROW, wide), jnp.float32)],
            compiler_params=small,
            cost_estimate=cost(2**20, 2**21),
            name="turn_queries",
        )(*queries)
        return pl.pallas_call(
            mix_kernel,
            out_specs=far,
            out_shape=jax.ShapeDtypeStruct((wide, ROW), jnp.bfloat16),
            scratch_shapes=[
                pltpu.VMEM((wide, ROW), jnp.bfloat16),
                pltpu.SemaphoreType.DMA((groups,)),
            ],
            compiler_params=small,
            name="mix_out",
        )(queries, convolved)
    queries = jnp.transpose(queries.astype(jnp.float32))
    return (queries * decode(convolved, 2).reshape(wide, -1)).astype(jnp.bfloat16)


def cost(flops, moved):
    return pl.CostEstimate(flops=int(flops), bytes_accessed=int(moved), transcendentals=0)


def solution(mesh):
    placed = (P(("seq", "ch"), None, None), P("ch", "seq"), P("ch"))
    return jax.shard_map(
        body, mesh=mesh, in_specs=placed, out_specs=P("ch", "seq"), check_vma=False
    )
```

```python
import functools
import math

import jax
import jax.numpy as jnp
import numpy as np
from jax import lax
from jax.experimental import pallas as pl
from jax.experimental.pallas import tpu as pltpu
from jax.sharding import PartitionSpec as P

GRID = 36.0
LOW_POWER = 125.0
EXPONENT_BITS = 8
EXPONENT_BIAS = 127.0
LANES = 128
ROW = 256
CHUNK = 16
GROUP = 16
VMEM_BYTES = 20 * 1024 * 1024
SMALL_BYTES = 12 * 1024 * 1024
ALL_BYTES = 60 * 1024 * 1024


def split_marked(values, axis):
    extent = values.shape[axis]
    if axis == values.ndim - 1:
        cut = max(extent - LANES, 0)
        marked = lax.slice_in_dim(values, cut, extent, axis=axis)
        return marked, lax.slice_in_dim(values, 0, cut, axis=axis) if cut else None
    cut = min(extent, EXPONENT_BITS)
    marked = lax.slice_in_dim(values, 0, cut, axis=axis)
    return marked, lax.slice_in_dim(values, cut, extent, axis=axis) if cut < extent else None


def join_marked(marked, rest, axis):
    if rest is None:
        return marked
    return jnp.concatenate([rest, marked] if axis == rest.ndim - 1 else [marked, rest], axis=axis)


def bit_place(shape, axis):
    place = lax.broadcasted_iota(jnp.int32, shape, axis) - (shape[axis] - EXPONENT_BITS)
    return place.astype(jnp.float32)


def scale_of(peak):
    power = jnp.floor(jnp.log(jnp.maximum(peak, 1e-30)) * (1.0 / math.log(2.0))) + 1.0
    return jnp.clip(power, -100.0, 126.0)


def exponent_bits(power, shape, axis):
    place = bit_place(shape, axis)
    bits = (power + (EXPONENT_BIAS + 0.25)) * jnp.exp2(-1.0 - jnp.maximum(place, 0.0))
    return jnp.where(bits - jnp.floor(bits) >= 0.5, 0.5, 0.0), place >= 0.0


def encode(values, axis):
    peak = jnp.max(jnp.abs(values), axis=axis, keepdims=True)
    return encode_all([values], scale_of(peak), axis)[0]


def encode_all(blocks, power, axis):
    unit_share, codes, bits = jnp.exp2(-power), [], None
    top = 2.0 * LOW_POWER
    for values in blocks:
        share = jnp.abs(values) * unit_share
        place = jnp.minimum(
            jnp.minimum(share * (2.0 * top) - LOW_POWER, share * top - LOW_POWER / 2),
            jnp.minimum(share * LOW_POWER, LOW_POWER + 1.0),
        )
        first, rest = split_marked(place, axis)
        bits = exponent_bits(power, first.shape, axis) if bits is None else bits
        odd, holds = bits
        if axis == values.ndim - 1:
            marked = (jnp.floor(first * GRID - odd + 0.5) + odd) * (1.0 / GRID)
            first = jnp.exp2(jnp.where(holds, marked, first))
        else:
            marked = (jnp.floor(first * 64.0 - odd + 0.5) + odd) * (1.0 / 64.0)
            octave = jnp.floor(marked)
            first = jnp.exp2(octave) * (marked - octave + 1.0)
        size = join_marked(first, None if rest is None else jnp.exp2(rest), axis)
        codes.append(jnp.where(values < 0.0, -size, size).astype(jnp.bfloat16))
    return codes


def decode(code, axis, halvings=0):
    code = code.astype(jnp.float32)
    size = jnp.abs(code)
    place = jnp.log(size) * (1.0 / math.log(2.0))
    first, rest = split_marked(place, axis)
    if axis == code.ndim - 1:
        half = first * GRID + 0.25
    else:
        octave = jnp.floor(first + 0.002)
        first = octave + split_marked(size, axis)[0] * jnp.exp2(-octave) - 1.0
        half = first * 64.0 + 0.25
        place = join_marked(first, rest, axis)
    spot = bit_place(first.shape, axis)
    weight = jnp.where(spot >= 0.0, jnp.exp2(spot), 0.0)
    held = jnp.where(half - jnp.floor(half) >= 0.5, weight, 0.0)
    scale = jnp.exp2(jnp.sum(held, axis=axis, keepdims=True) - (EXPONENT_BIAS + halvings))
    step = 0.25 / LOW_POWER
    share = jnp.maximum(
        place * (4.0 * step), jnp.maximum(place * (2.0 * step) + 0.25, place * step + 0.25)
    )
    return jnp.where(code < 0.0, -scale, scale) * share


def tables(blocks):
    n2 = np.arange(ROW)
    k1 = np.arange(blocks)
    main = 2.0 * np.pi * np.outer(n2, n2 + 0.5) / ROW
    twist = 2.0 * np.pi * np.outer(k1 + 0.25 - blocks / 2, n2) / (blocks * ROW)
    mix = 2.0 * np.pi * np.outer(k1 + 0.25, np.arange(blocks)) / blocks
    wave = np.stack([np.cos(main), np.sin(main)]).astype(np.float32)
    twist = np.stack([np.cos(twist), np.sin(twist)], axis=1).astype(np.float32)
    mix = np.stack([np.cos(mix), np.sin(mix)], axis=0).astype(np.float32)
    return wave, twist, mix


def folded(wave):
    half = np.concatenate([wave[0, :, :LANES], wave[1, :, :LANES]], axis=1)
    parts = []
    for values in (half, half.T):
        high = values.astype(jnp.bfloat16)
        low = (values - high.astype(np.float32)).astype(jnp.bfloat16)
        parts.append(np.concatenate([high, low, high], axis=0))
    return parts


def put_split(ref, at, values):
    high = values.astype(jnp.bfloat16)
    ref[pl.ds(at, values.shape[0]), 0:ROW] = high
    ref[pl.ds(at, values.shape[0]), ROW : 2 * ROW] = high
    ref[pl.ds(at, values.shape[0]), 2 * ROW : 3 * ROW] = (
        values - high.astype(jnp.float32)
    ).astype(jnp.bfloat16)


def eighth(value, sign):
    re, im = value
    side = math.sqrt(0.5)
    return (re - sign * im) * side, (im + sign * re) * side


def four_points(values, sign):
    (a_re, a_im), (b_re, b_im), (c_re, c_im), (d_re, d_im) = values
    sum_re, sum_im, gap_re, gap_im = a_re + c_re, a_im + c_im, a_re - c_re, a_im - c_im
    more_re, more_im = b_re + d_re, b_im + d_im
    side_re, side_im = sign * (d_im - b_im), sign * (b_re - d_re)
    return (
        (sum_re + more_re, sum_im + more_im),
        (gap_re + side_re, gap_im + side_im),
        (sum_re - more_re, sum_im - more_im),
        (gap_re - side_re, gap_im - side_im),
    )


def row_of(k, part, at):
    return (2 * k + part) * GROUP + at


def eight_points(values, sign):
    sums = [(a_re + b_re, a_im + b_im) for (a_re, a_im), (b_re, b_im) in zip(values, values[4:])]
    gaps = [(a_re - b_re, a_im - b_im) for (a_re, a_im), (b_re, b_im) in zip(values, values[4:])]
    (two_re, two_im), three = gaps[2], eighth(gaps[3], sign)
    turned = [gaps[0], eighth(gaps[1], sign), (-sign * two_im, sign * two_re)]
    turned.append((-sign * three[1], sign * three[0]))
    places = [None] * 8
    places[0::2] = four_points(sums, sign)
    places[1::2] = four_points(turned, sign)
    return places


def mix_forward(taken, twist_ref, at, ref):
    angles = [math.pi * n / 16 for n in range(8)]
    turned = [
        (value * math.cos(angle), value * -math.sin(angle)) if angle else (value, 0.0)
        for value, angle in zip(taken, angles)
    ]
    for k, (re, im) in enumerate(eight_points(turned, -1.0)):
        cos_twist, sin_twist = twist_ref[k, 0:1, :], twist_ref[k, 1:2, :]
        put_split(ref, row_of(k, 0, at), re * cos_twist + im * sin_twist)
        put_split(ref, row_of(k, 1, at), im * cos_twist - re * sin_twist)


def mix_back(spectra, twist_ref):
    twisted = []
    for k, (re, im) in enumerate(spectra):
        cos_twist, sin_twist = twist_ref[k, 0:1, :], twist_ref[k, 1:2, :]
        twisted.append((re * cos_twist - im * sin_twist, im * cos_twist + re * sin_twist))
    totals = []
    for n, (re, im) in enumerate(eight_points(twisted, 1.0)):
        angle = math.pi * n / 16
        totals.append(re * math.cos(angle) - im * math.sin(angle) if n else re)
    return totals


def spectrum_rows(waves_ref, k, at):
    re = waves_ref[pl.ds(row_of(k, 0, at), CHUNK), :]
    im = waves_ref[pl.ds(row_of(k, 1, at), CHUNK), :]
    return re, im


def send_kernel(streams_ref, gated_ref, keys, values, codes, in_sems, out_sems):
    groups, parts = gated_ref.shape[:2]
    per = groups
    width = per * LANES
    arrivals = []
    for chunk in range(parts):
        lanes = pl.ds(chunk * width, width)
        for stream, buffer in ((1, keys), (2, values)):
            copy = pltpu.make_async_copy(
                streams_ref.at[stream, :, lanes], buffer.at[chunk], in_sems.at[stream - 1, chunk]
            )
            copy.start()
            arrivals.append(copy)
    copies = []
    for chunk in range(parts):
        for copy in arrivals[2 * chunk : 2 * chunk + 2]:
            copy.wait()
        part, first = chunk, 0
        for block in range(per):
            lanes = slice(block * LANES, (block + 1) * LANES)
            left = keys[chunk, :, lanes].astype(jnp.float32)
            right = values[chunk, :, lanes].astype(jnp.float32)
            codes[first + block, part] = encode(left * right, 0)
        place = (pl.ds(first, per), part)
        copy = pltpu.make_async_copy(codes.at[place], gated_ref.at[place], out_sems.at[chunk])
        copy.start()
        copies.append(copy)
    for copy in copies:
        copy.wait()


def query_kernel(streams_ref, *refs):
    query_refs, sems = refs[:-1], refs[-1]
    me = lax.axis_index("ch")
    wide = query_refs[0].shape[1]
    copies = []
    for turn, query_ref in enumerate(query_refs):
        lanes = pl.ds(pl.multiple_of((me ^ turn) * wide, wide), wide)
        copy = pltpu.make_async_copy(streams_ref.at[0, :, lanes], query_ref, sems.at[turn])
        copy.start()
        copies.append(copy)
    for copy in copies:
        copy.wait()


def taps_kernel(taps_ref, skip_ref, *code_refs):
    me = lax.axis_index("seq")
    first = (me == 0).astype(jnp.float32)
    row = lax.broadcasted_iota(jnp.int32, (LANES, LANES), 0)
    lane = lax.broadcasted_iota(jnp.int32, (LANES, LANES), 1)
    for turn, code_ref in enumerate(code_refs):
        block = me ^ turn
        gains = jnp.broadcast_to(skip_ref[pl.ds(block, 1), :], (LANES, LANES))
        gain = jnp.sum(jnp.where(row == lane, gains, 0.0), axis=1, keepdims=True) * first
        start = taps_ref[block, :, :LANES] + jnp.where(lane == 0, gain, 0.0)
        taps = jnp.concatenate([start, taps_ref[block, :, LANES:]], axis=1)
        code_ref[...] = encode(taps, 1)


def combined(waves_ref, k, at):
    re, im = spectrum_rows(waves_ref, k, at)
    re_cos, re_sin, im_cos, im_sin = re[:, :LANES], re[:, LANES:], im[:, :LANES], im[:, LANES:]
    return (
        jnp.concatenate([re_cos + im_sin, re_cos - im_sin], axis=1),
        jnp.concatenate([im_cos - re_sin, im_cos + re_sin], axis=1),
    )


def put_folded(ref, k, at, re, im):
    near_re, far_re, near_im, far_im = re[:, :LANES], re[:, LANES:], im[:, :LANES], im[:, LANES:]
    back_re = jnp.concatenate([near_re + far_re, far_im - near_im], axis=1)
    back_im = jnp.concatenate([near_im + far_im, near_re - far_re], axis=1)
    put_split(ref, row_of(k, 0, at), back_re)
    put_split(ref, row_of(k, 1, at), back_im)


def multiply(source, wave_ref, target):
    target[...] = jnp.dot(source[...], wave_ref[...], preferred_element_type=jnp.float32)


def row_groups():
    return [range(first, first + GROUP, CHUNK) for first in range(0, LANES, GROUP)]


def gated_spectrum_kernel(gated_ref, wave_ref, twist_ref, *refs):
    early = (len(refs) - 6) // 2
    out_ref, u, rows, waves = refs[early], refs[-5], refs[-4:-2], refs[-2:]
    blocks = u.shape[0]
    for code_ref, taps_ref in zip(refs[:early], refs[early + 1 :]):
        taps_ref[...] = decode(code_ref[...], 1, math.log2(blocks * ROW))
    parts = ROW // gated_ref.shape[1]
    groups = row_groups()

    def unpack(block, _):
        pieces = [decode(gated_ref[block * parts + part], 0) for part in range(parts)]
        u[block] = jnp.transpose(jnp.concatenate(pieces, axis=0))
        return 0

    lax.fori_loop(0, blocks, unpack, 0)
    for step in range(len(groups) + 2):
        if 0 <= step - 1 < len(groups):
            multiply(rows[(step - 1) % 2], wave_ref, waves[(step - 1) % 2])
        if step < len(groups):
            for at in groups[step]:
                taken = [u[n1, at : at + CHUNK, :] for n1 in range(blocks)]
                mix_forward(taken, twist_ref, at % GROUP, rows[step % 2])
        if step >= 2:
            for at in groups[step - 2]:
                for k in range(blocks):
                    re, im = combined(waves[step % 2], k, at % GROUP)
                    out_ref[k, 0, at : at + CHUNK, :] = re
                    out_ref[k, 1, at : at + CHUNK, :] = im


def conv_kernel(gated_ref, *refs):
    blocks = gated_ref.shape[0]
    wave_ref, back_wave_ref, twist_ref, out_ref, taps, out, sems, *scratch = refs[blocks:]
    rows, waves, back_rows, back_waves = (scratch[at : at + 2] for at in (0, 2, 4, 6))
    scale = math.log2(blocks * ROW)
    me = lax.axis_index("seq")
    groups = row_groups()
    for turn, taps_ref in zip(turn_order(blocks), refs[:blocks]):
        early = taps_ref.dtype == jnp.float32
        taps[me ^ turn] = taps_ref[...] if early else decode(taps_ref[...], 1, scale)

    def forward(at, half):
        taken = [taps[n1, at : at + CHUNK, :] for n1 in range(blocks)]
        mix_forward(taken, twist_ref, at % GROUP, rows[half])

    def product(at, half):
        for k in range(blocks):
            re, im = combined(waves[half], k, at % GROUP)
            gated_re = gated_ref[k, 0, at : at + CHUNK, :]
            gated_im = gated_ref[k, 1, at : at + CHUNK, :]
            product_re, product_im = re * gated_re - im * gated_im, re * gated_im + im * gated_re
            put_folded(back_rows[half], k, at % GROUP, product_re, product_im)

    def back(at, half):
        spectra = [spectrum_rows(back_waves[half], k, at % GROUP) for k in range(blocks)]
        totals = mix_back(spectra, twist_ref)
        sizes = [jnp.abs(total) for total in totals]
        peak = jnp.max(functools.reduce(jnp.maximum, sizes), axis=1, keepdims=True)
        for n1, code in enumerate(encode_all(totals, scale_of(peak), 1)):
            out[n1, at : at + CHUNK, :] = code

    copies = []
    for step in range(len(groups) + 4):
        if 0 <= step - 1 < len(groups):
            multiply(rows[(step - 1) % 2], wave_ref, waves[(step - 1) % 2])
        if 0 <= step - 3 < len(groups):
            multiply(back_rows[(step - 3) % 2], back_wave_ref, back_waves[(step - 3) % 2])
        for work, delay in ((forward, 0), (product, 2), (back, 4)):
            if 0 <= step - delay < len(groups):
                for at in groups[step - delay]:
                    work(at, step % 2)
        if step >= 4:
            place = pl.ds((step - 4) * GROUP, GROUP)
            copy = pltpu.make_async_copy(
                out.at[:, place, :], out_ref.at[:, place, :], sems.at[step - 4]
            )
            copy.start()
            copies.append(copy)
    for copy in copies:
        copy.wait()


def turn_kernel(*refs):
    query_refs, out_ref, whole = refs[:-2], refs[-2], refs[-1]
    me = lax.axis_index("ch")
    held = query_refs[0].shape[0]
    for turn, query_ref in enumerate(query_refs):
        at = pl.multiple_of((me ^ turn) * held, held)
        whole[pl.ds(at, held), :] = query_ref[...].astype(jnp.float32)
    out_ref[...] = jnp.transpose(whole[...]).astype(jnp.bfloat16)


def mix_kernel(query_ref, conv_ref, out_ref, mixed, sems):
    copies = []
    for block in range(conv_ref.shape[0]):
        at = pl.ds(block * LANES, LANES)
        queries = query_ref[at, :].astype(jnp.float32)
        mixed[at, :] = (queries * decode(conv_ref[block], 1)).astype(jnp.bfloat16)
        copy = pltpu.make_async_copy(mixed.at[at], out_ref.at[at], sems.at[block])
        copy.start()
        copies.append(copy)
    for copy in copies:
        copy.wait()


def plain_conv(gated, taps):
    blocks = gated.shape[0]
    (cos, sin), twist, mix = tables(blocks)
    cos_twist, sin_twist = twist[:, 0][:, None, :], twist[:, 1][:, None, :]
    dot = functools.partial(jnp.einsum, precision=lax.Precision.HIGHEST)

    def forward(values):
        re = dot("ncm,kn->kcm", values, mix[0])
        im = -dot("ncm,kn->kcm", values, mix[1])
        re, im = re * cos_twist + im * sin_twist, im * cos_twist - re * sin_twist
        return (
            dot("kcm,mq->kcq", re, cos) + dot("kcm,mq->kcq", im, sin),
            dot("kcm,mq->kcq", im, cos) - dot("kcm,mq->kcq", re, sin),
        )

    u_re, u_im = forward(gated)
    h_re, h_im = forward(taps)
    re, im = u_re * h_re - u_im * h_im, u_re * h_im + u_im * h_re
    re, im = (
        dot("kcq,mq->kcm", re, cos) - dot("kcq,mq->kcm", im, sin),
        dot("kcq,mq->kcm", im, cos) + dot("kcq,mq->kcm", re, sin),
    )
    re, im = re * cos_twist - im * sin_twist, im * cos_twist + re * sin_twist
    total = dot("kcm,kn->ncm", re, mix[0]) - dot("kcm,kn->ncm", im, mix[1])
    return total * (1.0 / (blocks * ROW))


def turn_order(count):
    far = range(4, count, 2)
    return [0, 1, 2, 3, *far, *(turn + 1 for turn in far)]


def scatter(blocks, axis):
    count = len(blocks)
    return [
        lax.ppermute(block, axis, [(i, i ^ turn) for i in range(count)]) if turn else block
        for turn, block in enumerate(blocks)
    ]


def body(streams, filter_taps, skip_gain):
    groups, parts = lax.axis_size("seq"), lax.axis_size("ch")
    held, _, channels = streams.shape
    wide = channels // parts
    own = wide // groups
    blocks = filter_taps.shape[1] * groups // ROW
    streams = jnp.transpose(streams, (1, 0, 2))
    fits = blocks == 8 and own == LANES and filter_taps.shape[1] == ROW and ROW % held == 0 and groups % 4 == 0
    fits = fits and groups & (groups - 1) == 0 and parts & (parts - 1) == 0
    small = pltpu.CompilerParams(vmem_limit_bytes=SMALL_BYTES)
    if fits:
        far = pl.BlockSpec(memory_space=pl.ANY)
        coded = (groups, parts, held, own)
        stream = pltpu.VMEM((parts, held, wide), jnp.bfloat16)
        gated = pl.pallas_call(
            send_kernel,
            in_specs=[far],
            out_specs=far,
            out_shape=jax.ShapeDtypeStruct(coded, jnp.bfloat16),
            scratch_shapes=[
                stream,
                stream,
                pltpu.VMEM(coded, jnp.bfloat16),
                pltpu.SemaphoreType.DMA((2, 2 * parts)),
                pltpu.SemaphoreType.DMA((2 * parts,)),
            ],
            compiler_params=pltpu.CompilerParams(vmem_limit_bytes=ALL_BYTES),
            cost_estimate=cost(2**25, 2**23),
            name="encode_gated",
        )(streams)
        queries = pl.pallas_call(
            query_kernel,
            in_specs=[far],
            out_specs=[far] * parts,
            out_shape=[jax.ShapeDtypeStruct((held, wide), jnp.bfloat16)] * parts,
            scratch_shapes=[pltpu.SemaphoreType.DMA((parts,))],
            compiler_params=small,
            cost_estimate=cost(2**10, 2**20),
            name="send_queries",
        )(streams)
        taps = pl.pallas_call(
            taps_kernel,
            out_shape=[jax.ShapeDtypeStruct((own, ROW), jnp.bfloat16)] * groups,
            compiler_params=small,
            cost_estimate=cost(2**25, 2**23),
            name="encode_taps",
        )(filter_taps.reshape(groups, own, ROW), skip_gain.reshape(groups, own))
    else:
        gated = encode(streams[1].astype(jnp.float32) * streams[2].astype(jnp.float32), 0)
        gated = jnp.transpose(gated.reshape(held, parts, groups, own), (2, 1, 0, 3))
        queries = jnp.transpose(streams[0].reshape(held, parts, wide), (1, 0, 2))
        first = lax.axis_index("seq") == 0
        taps = filter_taps.at[:, 0].add(jnp.where(first, skip_gain, 0.0))
        taps = encode(taps, 1).reshape(groups, own, -1)
    exchange = functools.partial(lax.all_to_all, split_axis=0, concat_axis=0, tiled=True)
    gated = gated.reshape(groups * parts, held, own)
    if fits:
        taps = scatter(taps, "seq")
        gated = exchange(gated, ("seq", "ch"))
        queries = scatter(queries, "ch")
    else:
        taps = exchange(taps, "seq")
        gated = exchange(gated, ("seq", "ch"))
        queries = exchange(queries, "ch").reshape(parts * held, wide)
    if fits:
        wave, twist, _ = tables(blocks)
        wave, back_wave = folded(wave)
        scratch = [pltpu.VMEM((blocks * 2 * GROUP, 3 * ROW), jnp.bfloat16)] * 2
        scratch += [pltpu.VMEM((blocks * 2 * GROUP, ROW), jnp.float32)] * 2
        large = pltpu.CompilerParams(vmem_limit_bytes=VMEM_BYTES)
        early = groups // 2
        gated, *known = pl.pallas_call(
            gated_spectrum_kernel,
            out_shape=[jax.ShapeDtypeStruct((blocks, 2, own, ROW), jnp.float32)]
            + [jax.ShapeDtypeStruct((own, ROW), jnp.float32)] * early,
            scratch_shapes=[pltpu.VMEM((blocks, own, ROW), jnp.float32)] + scratch,
            compiler_params=large,
            cost_estimate=cost(2**32, 2**24),
            name="gated_spectrum",
        )(gated, wave, twist, *taps[:early])
        convolved = pl.pallas_call(
            conv_kernel,
            out_shape=jax.ShapeDtypeStruct((blocks, own, ROW), jnp.bfloat16),
            in_specs=[pl.BlockSpec(memory_space=pltpu.VMEM)] * (groups + 4),
            out_specs=far,
            scratch_shapes=[
                pltpu.VMEM((blocks, own, ROW), jnp.float32),
                pltpu.VMEM((blocks, own, ROW), jnp.bfloat16),
                pltpu.SemaphoreType.DMA((own // GROUP,)),
            ]
            + scratch * 2,
            compiler_params=large,
            cost_estimate=cost(2**32, 2**24),
            name="convolve",
        )(gated, *known, *[taps[turn] for turn in turn_order(groups)[early:]], wave, back_wave, twist)
    else:
        gated = decode(gated, 1).reshape(blocks, ROW, own)
        taps = jnp.transpose(decode(taps, 2), (1, 0, 2)).reshape(own, blocks, ROW)
        convolved = plain_conv(jnp.transpose(gated, (0, 2, 1)), jnp.transpose(taps, (1, 0, 2)))
        convolved = jnp.transpose(convolved, (1, 0, 2)).reshape(own, groups, -1)
        convolved = encode(jnp.transpose(convolved, (1, 0, 2)), 2)
    convolved = exchange(convolved, "seq")
    if fits:
        queries = pl.pallas_call(
            turn_kernel,
            out_shape=jax.ShapeDtypeStruct((wide, ROW), jnp.bfloat16),
            scratch_shapes=[pltpu.VMEM((ROW, wide), jnp.float32)],
            compiler_params=small,
            cost_estimate=cost(2**20, 2**21),
            name="turn_queries",
        )(*queries)
        return pl.pallas_call(
            mix_kernel,
            out_specs=far,
            out_shape=jax.ShapeDtypeStruct((wide, ROW), jnp.bfloat16),
            scratch_shapes=[
                pltpu.VMEM((wide, ROW), jnp.bfloat16),
                pltpu.SemaphoreType.DMA((groups,)),
            ],
            compiler_params=small,
            name="mix_out",
        )(queries, convolved)
    queries = jnp.transpose(queries.astype(jnp.float32))
    return (queries * decode(convolved, 2).reshape(wide, -1)).astype(jnp.bfloat16)


def cost(flops, moved):
    return pl.CostEstimate(flops=int(flops), bytes_accessed=int(moved), transcendentals=0)


def solution(mesh):
    placed = (P(("seq", "ch"), None, None), P("ch", "seq"), P("ch"))
    return jax.shard_map(
        body, mesh=mesh, in_specs=placed, out_specs=P("ch", "seq"), check_vma=False
    )
```
